32 devices in a mesh: cut: 4 (over z), cross: 8 (over y, x, core).
Axes of the slice: x: 2, y: 2, z: 4, core: 2. Of those that a mesh axis runs over, the one named last changes fastest.
Arguments:
- warming_above_ambient: float32 [512, 128, 128], P('cut', 'cross'), may hold values from 0 to 2
- fourier_stability_factor: float32 [512, 128, 128], P('cut', 'cross'), may hold values from 0.02 to 0.1
- patch_locator: int32 [65536], P(('cut', 'cross')), may hold values from 0 to 524287
- photon_gain_wattage: float32 [65536], P(('cut', 'cross')), may hold values from 0.5 to 4
- on_skin_marker: int32 [65536], P(('cut', 'cross')), may hold values 0 or 1
- grain_placements: float32 [3, 65536], P(None, ('cut', 'cross')), may hold values from -1 to 1
- grain_motion_parts: float32 [3, 65536], P(None, ('cut', 'cross')), may hold values from -3 to 3
- tether_acted_grain: int32 [262144], P(('cut', 'cross')), may hold values from 0 to 2047
- tether_other_grain: int32 [262144], P(('cut', 'cross')), may hold values from 0 to 2559
- tether_relaxed_gap: float32 [262144], P(('cut', 'cross')), may hold values from 0.5 to 1.5
- snapped_marker: int32 [262144], P(('cut', 'cross')), may hold values 0 or 1
- exported_copies: int32 [8192], P(('cut', 'cross')), may hold values from 0 to 2047
Outputs:
- temperature_new: float32 [512, 128, 128], P('cut', 'cross')
- positions_new: float32 [3, 65536], P(None, ('cut', 'cross'))
- velocities_new: float32 [3, 65536], P(None, ('cut', 'cross'))
The draws below stay inside these ranges and needn't reach their ends.
Inputs may be any that keep to these rules, and one draw needn't show every extreme that they name: `patch_locator`: values below 262144 name cells of the particle's own grid block along the cutting direction, the others cells of the next block.
All inputs are finite; a program needn't handle non-finite values. No bound on the sum of `on_skin_marker` or of `snapped_marker` on one device may be relied on, other than what follows from the above.
Results may differ from the reference program's by a relative error of at most 0.000071.
Values sent between devices are 32-bit elements; how exact they have to be, the bound alone decides.
No kernel may reach another device: no remote copies, remote signals or barrier semaphores. Data moves between devices by JAX's collectives and lax.ppermute only.
A program may use at most 64 MiB of HBM per device.

```python
import math
import jax
import jax.numpy as jnp
from jax import lax

CX = 128
CY = 16
INWARD_EXTENT = 128
CAP = 256
GHOSTS = 256
BONDS = 8192
STEPS = 3
TANGENT_EXTENT = 512
LATHE_AXIS_COUNT = 128
P_DEV = 2048
DOTS_OVERALL = 65536
GTOT = 8192
BTOT = 262144
N_CUT = 4
N_CROSS = 8


def touch_ends(array, stream_key, least, largest):
    index_at = [jax.random.randint(jax.random.fold_in(stream_key, axis), (), 0, length) for axis, length in enumerate(array.shape)]
    widest = array.shape.index(max(array.shape))
    neighbour = index_at[:widest] + [(index_at[widest] + 1) % array.shape[widest]] + index_at[widest + 1:]
    return array.at[tuple(index_at)].set(least).at[tuple(neighbour)].set(largest)


def levels(rng, extent, shards, least, top_value):
    loudness = 1.0
    for dim, shards_of in shards:
        steps = jax.random.uniform(jax.random.fold_in(jax.random.fold_in(rng, 6), dim), (shards_of,), jnp.float32, least / len(shards), top_value / len(shards))
        loudness = loudness * jnp.repeat(jnp.exp(steps), extent[dim] // shards_of).reshape((-1,) + (1,) * (len(extent) - 1 - dim))
    return loudness


def normal_values(own_key, dims, spread, bound, pieces=(), held_as=jnp.bfloat16):
    gain = levels(own_key, dims, pieces, -0.22, 0.18) if pieces else 1.0
    drawn = jax.random.normal(own_key, dims, jnp.float32) * spread * gain
    return jnp.minimum(jnp.maximum(drawn, -bound), bound).astype(held_as)


def setup_inputs(seed: int = 0) -> dict:
    seeds = jax.random.split(jax.random.key(seed), 13)
    warming_above_ambient = jnp.clip(2.0 * jax.random.uniform(seeds[0], (TANGENT_EXTENT, LATHE_AXIS_COUNT, INWARD_EXTENT), jnp.float32) ** levels(seeds[0], (TANGENT_EXTENT, LATHE_AXIS_COUNT, INWARD_EXTENT), ((0, 4), (1, 8)), -0.2, 0.2), 0.0, 2.0)
    fourier_stability_factor = jnp.clip(jnp.exp(math.log(0.1) - 1.609438 * jax.random.uniform(seeds[1], (TANGENT_EXTENT, LATHE_AXIS_COUNT, INWARD_EXTENT), jnp.float32) ** levels(seeds[1], (TANGENT_EXTENT, LATHE_AXIS_COUNT, INWARD_EXTENT), ((0, 4), (1, 8)), -0.2, 0.2)), 0.02, 0.1)
    patch_locator = touch_ends(jax.random.randint(seeds[2], (DOTS_OVERALL,), 0, 2 * CX * CY * INWARD_EXTENT), jax.random.fold_in(seeds[2], 1), 0, (2 * CX * CY * INWARD_EXTENT) - 1).astype(jnp.int32)
    photon_gain_wattage = jnp.clip(jnp.exp(math.log(4.0) - 2.0794415 * jax.random.uniform(seeds[3], (DOTS_OVERALL,), jnp.float32) ** levels(seeds[3], (DOTS_OVERALL,), ((0, 32),), -0.2, 0.2)), 0.5, 4.0)
    on_skin_marker = touch_ends((jax.random.randint(seeds[4], (DOTS_OVERALL,), 0, 2) < 1).astype(jnp.int32), jax.random.fold_in(seeds[4], 1), 0, 1)
    grain_placements = jnp.clip(jax.random.uniform(seeds[5], (3, DOTS_OVERALL), jnp.float32, -1.0, 1.0) * levels(seeds[5], (3, DOTS_OVERALL), ((1, 32),), -0.4, 0.0), -1.0, 1.0)
    grain_motion_parts = normal_values(seeds[6], (3, DOTS_OVERALL), 0.5, 3.0, ((1, 32),), jnp.float32)
    tether_acted_grain = touch_ends(jax.random.randint(seeds[7], (BTOT,), 0, CAP * N_CROSS), jax.random.fold_in(seeds[7], 1), 0, (CAP * N_CROSS) - 1).astype(jnp.int32)
    tether_other_grain = touch_ends(jax.random.randint(seeds[8], (BTOT,), 0, CAP * N_CROSS + 2 * GHOSTS), jax.random.fold_in(seeds[8], 1), 0, (CAP * N_CROSS + 2 * GHOSTS) - 1).astype(jnp.int32)
    tether_relaxed_gap = jnp.clip(jnp.exp(math.log(1.5) - 1.0986123 * jax.random.uniform(seeds[9], (BTOT,), jnp.float32) ** levels(seeds[9], (BTOT,), ((0, 32),), -0.2, 0.2)), 0.5, 1.5)
    snapped_marker = touch_ends((jax.random.randint(seeds[10], (BTOT,), 0, 8) < 1).astype(jnp.int32), jax.random.fold_in(seeds[10], 1), 0, 1)
    exported_copies = touch_ends(jax.random.randint(seeds[11], (GTOT,), 0, CAP * N_CROSS), jax.random.fold_in(seeds[11], 1), 0, (CAP * N_CROSS) - 1).astype(jnp.int32)
    return {"warming_above_ambient": warming_above_ambient, "fourier_stability_factor": fourier_stability_factor, "patch_locator": patch_locator, "photon_gain_wattage": photon_gain_wattage, "on_skin_marker": on_skin_marker, "grain_placements": grain_placements, "grain_motion_parts": grain_motion_parts, "tether_acted_grain": tether_acted_grain, "tether_other_grain": tether_other_grain, "tether_relaxed_gap": tether_relaxed_gap, "snapped_marker": snapped_marker, "exported_copies": exported_copies}


def conduct(grain_warmth_reading):
    return 0.5 + 1.0 / (1.0 + grain_warmth_reading * grain_warmth_reading)

def advance(temp_pad, kappa_pad, thermal_input):
    temp_full = jnp.pad(temp_pad, ((0, 0), (0, 0), (1, 1)))
    kappa_full = jnp.pad(kappa_pad, ((0, 0), (0, 0), (1, 1)))
    conduct_full = kappa_full * conduct(temp_full)
    size_a = temp_full.shape[0] - 2
    size_b = temp_full.shape[1] - 2
    size_c = temp_full.shape[2] - 2
    center = temp_full[1:1 + size_a, 1:1 + size_b, 1:1 + size_c]
    middle = conduct_full[1:1 + size_a, 1:1 + size_b, 1:1 + size_c]
    change = jnp.zeros_like(center)
    for first, second, third in ((2, 1, 1), (0, 1, 1), (1, 2, 1), (1, 0, 1), (1, 1, 2), (1, 1, 0)):
        beside = temp_full[first:first + size_a, second:second + size_b, third:third + size_c]
        beside_c = conduct_full[first:first + size_a, second:second + size_b, third:third + size_c]
        change = change + 0.5 * (middle + beside_c) * (beside - center)
    return center + (change + thermal_input)

def pad_grid(field):
    field = jnp.pad(field, ((1, 1), (0, 0), (0, 0)), mode='wrap')
    return jnp.pad(field, ((0, 0), (1, 1), (0, 0)))

def reference(warming_above_ambient, fourier_stability_factor, patch_locator, photon_gain_wattage, on_skin_marker, grain_placements, grain_motion_parts, tether_acted_grain, tether_other_grain, tether_relaxed_gap, snapped_marker, exported_copies):
    structured_patch = CX * CY * INWARD_EXTENT
    rows = jnp.arange(DOTS_OVERALL, dtype=jnp.int32)
    device = rows // P_DEV
    cut_index = device // N_CROSS
    dest = rows % P_DEV // CAP
    offset = patch_locator // structured_patch
    remain = patch_locator % structured_patch
    grid_x = (cut_index + offset) % N_CUT * CX + remain // (CY * INWARD_EXTENT)
    grid_y = dest * CY + remain // INWARD_EXTENT % CY
    grid_z = remain % INWARD_EXTENT
    flat_cell = ((grid_x * LATHE_AXIS_COUNT + grid_y) * INWARD_EXTENT + grid_z).astype(jnp.int32)
    energy_current = on_skin_marker.astype(jnp.float32) * photon_gain_wattage * 0.5
    thermal_input = jnp.zeros((TANGENT_EXTENT * LATHE_AXIS_COUNT * INWARD_EXTENT,), jnp.float32).at[flat_cell].add(energy_current).reshape(TANGENT_EXTENT, LATHE_AXIS_COUNT, INWARD_EXTENT)
    kappa_pad = pad_grid(fourier_stability_factor)
    grain_warmth_reading = warming_above_ambient
    for substep in range(STEPS):
        grain_warmth_reading = advance(pad_grid(grain_warmth_reading), kappa_pad, thermal_input)
    particle_temp = grain_warmth_reading.reshape(-1)[flat_cell]
    brow = jnp.arange(BTOT, dtype=jnp.int32)
    bdev = brow // BONDS
    bcut = bdev // N_CROSS
    bside = bdev % N_CROSS
    low_dev = (bcut - 1) % N_CUT * N_CROSS + bside
    high_dev = (bcut + 1) % N_CUT * N_CROSS + bside
    low_k = jnp.clip(tether_other_grain - P_DEV, 0, GHOSTS - 1)
    high_k = jnp.clip(tether_other_grain - P_DEV - GHOSTS, 0, GHOSTS - 1)
    low_part = low_dev * P_DEV + exported_copies[(low_dev * GHOSTS + low_k).astype(jnp.int32)]
    high_part = high_dev * P_DEV + exported_copies[(high_dev * GHOSTS + high_k).astype(jnp.int32)]
    partner = jnp.where(tether_other_grain < P_DEV, bdev * P_DEV + tether_other_grain, jnp.where(tether_other_grain < P_DEV + GHOSTS, low_part, high_part)).astype(jnp.int32)
    first = (bdev * P_DEV + tether_acted_grain).astype(jnp.int32)
    delta = grain_placements[:, partner] - grain_placements[:, first]
    dist = jnp.sqrt(lax.optimization_barrier(jnp.sum(delta * delta, axis=0)))
    hot = tether_relaxed_gap * (1.0 + 0.2 * (0.5 * (particle_temp[first] + particle_temp[partner])))
    scale = (1.0 - snapped_marker.astype(jnp.float32)) * (dist - hot) / jnp.maximum(dist, 0.3)
    force = jnp.zeros((3, DOTS_OVERALL), jnp.float32).at[:, first].add(scale * delta)
    velocities_new = grain_motion_parts + 0.5 * force
    positions_new = grain_placements + 0.5 * velocities_new
    return (grain_warmth_reading, positions_new, velocities_new)
```

```python
import functools

import jax
import jax.numpy as jnp
from jax import lax
from jax.experimental import pallas as pl
from jax.experimental.pallas import tpu as pltpu
from jax.sharding import PartitionSpec as P

F32 = jnp.float32
BF16 = jnp.bfloat16
I32 = jnp.int32
LANES = 128
BOTH = ("cut", "cross")
VMEM = pl.BlockSpec(memory_space=pltpu.VMEM)
SMEM = pl.BlockSpec(memory_space=pltpu.SMEM)
LIMIT = 48 * 1024 * 1024


def call(kernel, outs, operands, scratch=(), smem=1):
    return pl.pallas_call(
        kernel,
        out_shape=outs,
        in_specs=[SMEM] * smem + [VMEM] * (len(operands) - smem),
        out_specs=[VMEM] * len(outs),
        scratch_shapes=list(scratch),
        compiler_params=pltpu.CompilerParams(vmem_limit_bytes=LIMIT),
    )(*operands)


def split(value):
    high = value.astype(BF16)
    return high, (value - high.astype(F32)).astype(BF16)


def iota(shape, dim):
    return lax.broadcasted_iota(I32, shape, dim)


def with_rim(rows, below, above):
    rim = (8, rows.shape[1])
    place = iota(rim, 0)
    extra = jnp.where(
        place == 0,
        jnp.broadcast_to(above, rim),
        jnp.where(place == 7, jnp.broadcast_to(below, rim), jnp.zeros(rim, F32)),
    )
    return jnp.concatenate([rows, extra], axis=0)


def conduct(kappa, temp):
    return (0.5 * kappa) * (0.5 + 1.0 / (1.0 + temp * temp))


def heat_pass(temp, temp_x, temp_y, kappa, kappa_x, kappa_y, put):
    count, rows, lanes = temp.shape
    lane = iota((rows, lanes), 1)
    total = rows + 8

    def plane(i):
        t = with_rim(temp[i], temp_y[0][pl.ds(i, 1), :], temp_y[1][pl.ds(i, 1), :])
        k = with_rim(kappa[i], kappa_y[0][pl.ds(i, 1), :], kappa_y[1][pl.ds(i, 1), :])
        return t, conduct(k, t)

    def finish(i, t, c, flux_x, above):
        flux_y = (c + pltpu.roll(c, total - 1, 0)) * (pltpu.roll(t, total - 1, 0) - t)
        net = (flux_y - pltpu.roll(flux_y, 1, 0))[:rows]
        t = t[:rows]
        c = c[:rows]
        edge = c * t
        flux_z = (c + pltpu.roll(c, lanes - 1, 1)) * (pltpu.roll(t, lanes - 1, 1) - t)
        flux_z = jnp.where(lane == lanes - 1, -edge, flux_z)
        net = net + (flux_z - jnp.where(lane == 0, edge, pltpu.roll(flux_z, 1, 1)))
        put(i, t + (net + (above - flux_x)))

    def step(i, carried):
        t, c, flux_x = carried
        t_next, c_next = plane(i + 1)
        above = (c[:rows] + c_next[:rows]) * (t_next[:rows] - t[:rows])
        finish(i, t, c, flux_x, above)
        return t_next, c_next, above

    t, c = plane(0)
    t_low = temp_x[0][...]
    flux_x = (c[:rows] + conduct(kappa_x[0][...], t_low)) * (t[:rows] - t_low)
    t, c, flux_x = lax.fori_loop(0, count - 1, step, (t, c, flux_x), unroll=2)
    t_high = temp_x[1][...]
    above = (c[:rows] + conduct(kappa_x[1][...], t_high)) * (t_high - t[:rows])
    finish(count - 1, t, c, flux_x, above)


def parts_of(got, me):
    blocks = got.shape[0]
    return ((me, False), (lax.rem(me + blocks - 1, blocks), True))


def local_cell(cell, upper, patch):
    cell = cell.astype(I32)
    if upper:
        return jnp.where(cell >= patch, cell - patch, -1)
    return jnp.where(cell < patch, cell, -1)


def deposit(me, got, shape, put, spread, along, across):
    planes, rows, lanes = shape
    half = got.shape[2] // 2
    patch = planes * rows * lanes
    place = iota((lanes, LANES), 0)
    row_place = iota((rows, LANES), 0)
    at = 0
    for block, upper in parts_of(got, me):
        for s in range(got.shape[1]):
            for h in range(half):
                cell = local_cell(got[block, s, h : h + 1, :], upper, patch)
                high, low = split(got[block, s, half + h : half + h + 1, :])
                here = place == (cell & (lanes - 1))
                zero = jnp.zeros((lanes, LANES), F32)
                span = slice(at, at + LANES)
                spread[0:lanes, span] = jnp.where(here, high.astype(F32), zero).astype(BF16)
                spread[lanes : 2 * lanes, span] = jnp.where(here, low.astype(F32), zero).astype(BF16)
                row = lax.shift_right_arithmetic(cell, 7)
                across[:, span] = jnp.where((row & (rows - 1)) == row_place, 1.0, 0.0).astype(BF16)
                along[:, span] = jnp.broadcast_to(row // rows, (rows, LANES)).astype(jnp.int16)
                at += LANES
    tile = 32

    def body(m, unused):
        where_x = along[...] - (m * tile).astype(jnp.int16)
        where_y = across[...]
        zero = jnp.zeros_like(where_y)
        hot = jnp.concatenate(
            [jnp.where(where_x == jnp.int16(x), where_y, zero) for x in range(tile)], axis=0
        )
        both = lax.dot_general(
            hot, spread[...], (((1,), (1,)), ((), ())), preferred_element_type=F32
        )
        put(m * tile, (both[:, :lanes] + both[:, lanes:]).reshape(tile, rows, lanes))
        return unused

    lax.fori_loop(0, planes // tile, body, 0)


def first_kernel(
    me, got, temp, tx0, tx1, ty0, ty1, kappa, kx0, kx1, ky0, ky1,
    source, temp_out, x0, x1, y0, y1, spread, along, across,
):
    def put_source(first, planes):
        source[pl.ds(first, planes.shape[0])] = planes

    deposit(me[0], got, temp.shape, put_source, spread, along, across)
    substep(temp, (tx0, tx1), (ty0, ty1), kappa, (kx0, kx1), (ky0, ky1), source, temp_out, y0, y1)
    x0[...] = temp_out[0]
    x1[...] = temp_out[temp_out.shape[0] - 1]


def substep(temp, temp_x, temp_y, kappa, kappa_x, kappa_y, source, out, y0=None, y1=None):
    def put(i, plane):
        plane = plane + source[i]
        out[i] = plane
        if y0 is not None:
            y0[pl.ds(i, 1), :] = plane[:1]
            y1[pl.ds(i, 1), :] = plane[-1:]

    heat_pass(temp, temp_x, temp_y, kappa, kappa_x, kappa_y, put)


def middle_kernel(
    temp, tx0, tx1, ty0, ty1, kappa, kx0, kx1, ky0, ky1, source, temp_out, x0, x1, y0, y1
):
    substep(temp, (tx0, tx1), (ty0, ty1), kappa, (kx0, kx1), (ky0, ky1), source, temp_out, y0, y1)
    x0[...] = temp_out[0]
    x1[...] = temp_out[temp_out.shape[0] - 1]


def last_kernel(
    me, got, temp, tx0, tx1, ty0, ty1, kappa, kx0, kx1, ky0, ky1, source,
    temp_out, looked, pieces, turned, found,
):
    substep(temp, (tx0, tx1), (ty0, ty1), kappa, (kx0, kx1), (ky0, ky1), source, temp_out)
    planes, rows, lanes = temp.shape
    high, low = split(temp_out[...].reshape(planes * rows, lanes))
    pieces[:, :lanes] = high
    pieces[:, lanes:] = low
    half = got.shape[2] // 2
    patch = planes * rows * lanes
    groups = got.shape[1]
    chunks = []
    for block, upper in parts_of(got, me[0]):
        for s in range(groups):
            for h in range(half):
                chunks.append(local_cell(got[block, s, h : h + 1, :], upper, patch))
    count = len(chunks)
    chunks.append(jnp.zeros((LANES - count, LANES), I32))
    turned[...] = jnp.concatenate(chunks, axis=0).T
    lane = iota((LANES, LANES), 1)
    found[...] = jnp.zeros((LANES, LANES), F32)
    width = 4
    for first in range(0, count, width):
        hots = []
        cells = []
        for k in range(first, first + width):
            cell = jnp.broadcast_to(turned[:, k : k + 1], (LANES, LANES))
            cells.append(cell)
            row = lax.shift_right_arithmetic(cell, 7).astype(jnp.int16)
            one = jnp.ones((LANES, LANES), BF16)
            hots.append(
                jnp.concatenate(
                    [
                        jnp.where(
                            row == (lane + r * LANES).astype(jnp.int16), one, jnp.zeros_like(one)
                        )
                        for r in range(planes * rows // LANES)
                    ],
                    axis=1,
                )
            )
        both = jnp.dot(jnp.concatenate(hots, axis=0), pieces[...], preferred_element_type=F32)
        value = both[:, :lanes] + both[:, lanes:]
        for n in range(width):
            picked = jnp.take_along_axis(
                value[n * LANES : (n + 1) * LANES], cells[n] & (lanes - 1), axis=1
            )
            found[...] = jnp.where(lane == first + n, picked, found[...])
    back = found[...].T
    at = 0
    for part in range(2):
        for s in range(groups):
            for h in range(half):
                looked[s, part * half + h : part * half + h + 1, :] = back[at : at + 1, :]
                at += 1


def pick(tables, index):
    row = lax.shift_right_logical(index, 7)
    lane = index & (LANES - 1)
    results = [jnp.zeros(index.shape, F32) for _ in tables]
    for r in range(len(tables[0])):
        here = row == r
        for ch, rows in enumerate(tables):
            value = jnp.take_along_axis(jnp.broadcast_to(rows[r], index.shape), lane, axis=1)
            results[ch] = jnp.where(here, value, results[ch])
    return results


def bond_kernel(
    me, back, pos, vel, acted, other, gap, snapped, low_pos, high_pos, low_export, high_export,
    pos_out, vel_out, force, hot,
):
    blocks, groups, double, _ = back.shape
    half = double // 2
    here = me[0]

    def block(distance):
        return lax.rem(here + (blocks + distance), blocks)

    def temps(distance):
        return [
            back[block(distance), j, h : h + 1, :] + back[block(distance + 1), j, half + h : half + h + 1, :]
            for j in range(groups)
            for h in range(half)
        ]

    def rows_of(ref, ch):
        return [ref[ch : ch + 1, r * LANES : (r + 1) * LANES] for r in range(ref.shape[1] // LANES)]

    def ghosts(ref, distance, export):
        tables = [
            [ref[ch, r : r + 1, :] for r in range(ref.shape[1])] for ch in range(3)
        ] + [temps(distance)]
        found = pick(tables, export[...])
        return [[f[r : r + 1] for r in range(f.shape[0])] for f in found]

    own = [rows_of(pos, ch) for ch in range(3)] + [temps(0)]
    low = ghosts(low_pos, -1, low_export)
    high = ghosts(high_pos, 1, high_export)
    wide = [own[ch] + low[ch] + high[ch] for ch in range(4)]
    first = pick(own, acted[...])
    second = pick(wide, other[...])
    delta = [second[ch] - first[ch] for ch in range(3)]
    dist = jnp.sqrt(delta[0] * delta[0] + delta[1] * delta[1] + delta[2] * delta[2])
    relaxed = gap[...] * (1.0 + 0.2 * (0.5 * (first[3] + second[3])))
    scale = (1.0 - snapped[...].astype(F32)) * (dist - relaxed) / jnp.maximum(dist, 0.3)
    values = [split(scale * d) for d in delta]
    values = [piece.astype(F32) for pair in values for piece in pair]
    high_count = len(own[0])
    place = iota((LANES, LANES), 0)
    high_place = iota((high_count, LANES), 0)
    for r in range(acted.shape[0]):
        index = acted[r : r + 1, :]
        span = slice(r * LANES, (r + 1) * LANES)
        hot[:, span] = jnp.where(place == (index & (LANES - 1)), 1.0, 0.0).astype(BF16)
        at_row = lax.shift_right_logical(index, 7) == high_place
        for n, value in enumerate(values):
            force[n * high_count : (n + 1) * high_count, span] = jnp.where(
                at_row, jnp.broadcast_to(value[r : r + 1], (high_count, LANES)), 0.0
            ).astype(BF16)
    total = lax.dot_general(
        force[...], hot[...], (((1,), (1,)), ((), ())), preferred_element_type=F32
    )
    for ch in range(3):
        base = 2 * ch * high_count
        summed = total[base : base + high_count] + total[base + high_count : base + 2 * high_count]
        for r in range(high_count):
            span = slice(r * LANES, (r + 1) * LANES)
            velocity = vel[ch : ch + 1, span] + 0.5 * summed[r : r + 1]
            vel_out[ch : ch + 1, span] = velocity
            pos_out[ch : ch + 1, span] = pos[ch : ch + 1, span] + 0.5 * velocity


def ring(block, distance):
    count = lax.axis_size("cut")
    return lax.ppermute(block, "cut", [(i, (i + distance) % count) for i in range(count)])


def line(block, distance):
    count = lax.axis_size("cross")
    pairs = [(i, i + distance) for i in range(count) if 0 <= i + distance < count]
    return lax.ppermute(block, "cross", pairs)


def per_device(
    warming_above_ambient,
    fourier_stability_factor,
    patch_locator,
    photon_gain_wattage,
    on_skin_marker,
    grain_placements,
    grain_motion_parts,
    tether_acted_grain,
    tether_other_grain,
    tether_relaxed_gap,
    snapped_marker,
    exported_copies,
):
    temp = warming_above_ambient
    kappa = fourier_stability_factor
    blocks = lax.axis_size("cut")
    groups = lax.axis_size("cross")
    planes, rows, lanes = temp.shape
    count = patch_locator.shape[0]
    half = count // groups // LANES
    me = lax.axis_index("cut").reshape(1).astype(I32)

    power = on_skin_marker.astype(F32) * photon_gain_wattage * 0.5
    parcel = jnp.concatenate(
        [
            patch_locator.astype(F32).reshape(groups, half, LANES),
            power.reshape(groups, half, LANES),
        ],
        axis=1,
    )

    def exchange(parcel):
        sent = jnp.broadcast_to(parcel[None], (blocks,) + parcel.shape)
        sent = sent.reshape((blocks * groups,) + parcel.shape[1:])
        got = lax.all_to_all(sent, BOTH, split_axis=0, concat_axis=0, tiled=True)
        return got.reshape((blocks, groups) + parcel.shape[1:])

    got = exchange(parcel)

    ghost = jnp.concatenate(
        [
            grain_placements.reshape(-1, LANES),
            exported_copies.astype(F32).reshape(-1, LANES),
        ],
        axis=0,
    )
    place_rows = grain_placements.size // LANES

    def side(plane):
        return jnp.concatenate([temp[plane], kappa[plane], ghost], axis=0)

    low = ring(side(planes - 1), 1)
    high = ring(side(0), -1)
    tx = (low[:rows], high[:rows])
    kx = (low[rows : 2 * rows], high[rows : 2 * rows])

    def neighbour(block):
        ghost = block[2 * rows :]
        return (
            ghost[:place_rows].reshape(3, -1, LANES),
            ghost[place_rows:].astype(I32),
        )

    low_pos, low_export = neighbour(low)
    high_pos, high_export = neighbour(high)
    y_low = line(jnp.stack([temp[:, rows - 1], kappa[:, rows - 1]]), 1)
    y_high = line(jnp.stack([temp[:, 0], kappa[:, 0]]), -1)
    ty = (y_low[0], y_high[0])
    ky = (y_low[1], y_high[1])

    grid = jax.ShapeDtypeStruct(temp.shape, F32)
    x_side = jax.ShapeDtypeStruct((rows, lanes), F32)
    y_side = jax.ShapeDtypeStruct((planes, lanes), F32)
    entries = 2 * count
    source, temp, x0, x1, y0, y1 = call(
        first_kernel,
        [grid, grid, x_side, x_side, y_side, y_side],
        [me, got, temp, *tx, *ty, kappa, *kx, *ky],
        [
            pltpu.VMEM((2 * lanes, entries), BF16),
            pltpu.VMEM((rows, entries), jnp.int16),
            pltpu.VMEM((rows, entries), BF16),
        ],
    )

    def halo():
        return (ring(x1, 1), ring(x0, -1)), (line(y1, 1), line(y0, -1))

    tx, ty = halo()
    temp, x0, x1, y0, y1 = call(
        middle_kernel,
        [grid, x_side, x_side, y_side, y_side],
        [temp, *tx, *ty, kappa, *kx, *ky, source],
        smem=0,
    )
    tx, ty = halo()
    temp, looked = call(
        last_kernel,
        [grid, jax.ShapeDtypeStruct((groups, 2 * half, LANES), F32)],
        [me, got, temp, *tx, *ty, kappa, *kx, *ky, source],
        [
            pltpu.VMEM((planes * rows, 2 * lanes), BF16),
            pltpu.VMEM((LANES, LANES), I32),
            pltpu.VMEM((LANES, LANES), F32),
        ],
    )
    back = exchange(looked)
    bonds = tether_acted_grain.shape[0]
    out = jax.ShapeDtypeStruct(grain_placements.shape, F32)
    positions_new, velocities_new = call(
        bond_kernel,
        [out, out],
        [
            me,
            back,
            grain_placements,
            grain_motion_parts,
            tether_acted_grain.reshape(-1, LANES),
            tether_other_grain.reshape(-1, LANES),
            tether_relaxed_gap.reshape(-1, LANES),
            snapped_marker.reshape(-1, LANES),
            low_pos,
            high_pos,
            low_export,
            high_export,
        ],
        [
            pltpu.VMEM((6 * (count // LANES), bonds), BF16),
            pltpu.VMEM((LANES, bonds), BF16),
        ],
    )
    return (temp, positions_new, velocities_new)


def solution(mesh):
    return jax.shard_map(
        per_device,
        mesh=mesh,
        in_specs=(
            P("cut", "cross", None),
            P("cut", "cross", None),
            P(("cut", "cross")),
            P(("cut", "cross")),
            P(("cut", "cross")),
            P(None, ("cut", "cross")),
            P(None, ("cut", "cross")),
            P(("cut", "cross")),
            P(("cut", "cross")),
            P(("cut", "cross")),
            P(("cut", "cross")),
            P(("cut", "cross")),
        ),
        out_specs=(P("cut", "cross", None), P(None, ("cut", "cross")), P(None, ("cut", "cross"))),
        check_vma=False,
    )
```

```python
import functools

import jax
import jax.numpy as jnp
from jax import lax
from jax.experimental import pallas as pl
from jax.experimental.pallas import tpu as pltpu
from jax.sharding import PartitionSpec as P

F32 = jnp.float32
BF16 = jnp.bfloat16
I32 = jnp.int32
LANES = 128
BOTH = ("cut", "cross")
VMEM = pl.BlockSpec(memory_space=pltpu.VMEM)
SMEM = pl.BlockSpec(memory_space=pltpu.SMEM)
LIMIT = 48 * 1024 * 1024


def call(kernel, outs, operands, scratch=(), smem=1):
    return pl.pallas_call(
        kernel,
        out_shape=outs,
        in_specs=[SMEM] * smem + [VMEM] * (len(operands) - smem),
        out_specs=[VMEM] * len(outs),
        scratch_shapes=list(scratch),
        compiler_params=pltpu.CompilerParams(vmem_limit_bytes=LIMIT),
    )(*operands)


def split(value):
    high = value.astype(BF16)
    return high, (value - high.astype(F32)).astype(BF16)


def iota(shape, dim):
    return lax.broadcasted_iota(I32, shape, dim)


RIM = 3
PAD = 8


def groups_of(count, most):
    return max(n for n in range(1, most + 1) if count % n == 0)


def difference_matrices(lanes):
    shape = (2 * lanes, 2 * lanes)
    given = iota(shape, 0) & (lanes - 1)
    wanted = iota(shape, 1)
    lower = wanted >= lanes
    wanted = wanted & (lanes - 1)
    beside = jnp.where(lower, wanted - 1, wanted + 1)
    neighbour = jnp.where(given == beside, 1.0, 0.0)
    same = jnp.where(given == wanted, 1.0, 0.0)
    return (neighbour - same).astype(BF16), (neighbour + same).astype(BF16)


def pieces_of(value):
    high, low = split(value)
    return jnp.concatenate([high, low], axis=1)


def conduct_pass(temp, kappa, cond, along_z, minus, plus, first, blocks, pitch):
    lanes = temp.shape[1]
    size = groups_of(blocks, 9)

    def body(n, unused):
        at = pl.ds(pl.multiple_of((first + n * size) * pitch, 8), size * pitch)
        t = temp[at, :]
        c = kappa[at, :] * (0.5 + 1.0 / (1.0 + t * t))
        cond[at, :] = c
        change = jnp.dot(pieces_of(t), minus[...], preferred_element_type=F32)
        both = jnp.dot(pieces_of(c), plus[...], preferred_element_type=F32)
        along_z[at, :] = change[:, :lanes] * both[:, :lanes] + change[:, lanes:] * both[:, lanes:]
        return unused

    lax.fori_loop(0, blocks // size, body, 0)


def flow_pass(temp, cond, along_z, first, blocks, pitch, most, put):
    size = groups_of(blocks, most)

    def body(n, unused):
        block = first + n * size
        base = pl.multiple_of(block * pitch, 8)
        at = pl.ds(base, size * pitch)
        t = temp[at, :]
        c = cond[at, :]
        net = along_z[at, :]
        for shift in (pitch, -pitch, 1, -1):
            beside = pl.ds(base + shift, size * pitch)
            net = net + (c + cond[beside, :]) * (temp[beside, :] - t)
        put(block, size, t + net)
        return unused

    lax.fori_loop(0, blocks // size, body, 0)


def rim_mask(ends, pitch, lanes):
    place = iota((pitch, lanes), 0)
    below = jnp.where(ends[0] > 0, 1.0, 0.0)
    above = jnp.where(ends[1] > 0, 1.0, 0.0)
    return jnp.where(place < PAD - RIM, above, jnp.where(place < PAD, below, 1.0))


def fill(flat, own, x_low, x_high, y_low, y_high, rows, pitch, scale):
    planes = own.shape[0] // rows
    total = planes + 2 * RIM
    flat[...] = jnp.zeros(flat.shape, F32)

    def place(p, part):
        flat[pl.ds(pl.multiple_of(p * pitch + PAD, 8), rows), :] = part * scale

    for n in range(RIM):
        place(n, x_low[n * rows : (n + 1) * rows, :])
        place(RIM + planes + n, x_high[n * rows : (n + 1) * rows, :])

    def body(p, unused):
        place(p + RIM, own[pl.ds(pl.multiple_of(p * rows, 8), rows), :])
        return unused

    lax.fori_loop(0, planes, body, 0, unroll=8)
    for r in range(RIM):
        flat[pl.ds(PAD - RIM + r, total, stride=pitch), :] = y_low[r, :total, :] * scale
        flat[pl.ds(PAD + rows + r, total, stride=pitch), :] = y_high[r, :total, :] * scale


def rows_kernel(temp, kappa, low, high, down, up):
    side = low.shape[0] // 2
    rows = side // RIM
    planes = temp.shape[0] // rows
    for n, own in enumerate((temp, kappa)):
        for r in range(RIM):
            for out, row in ((down, r), (up, rows - RIM + r)):
                target = n * RIM + r
                for p in range(RIM):
                    at = n * side + p * rows + row
                    out[target, p : p + 1, :] = low[at : at + 1, :]
                    out[target, RIM + planes + p : RIM + planes + p + 1, :] = high[at : at + 1, :]
                out[target, RIM : RIM + planes, :] = own[pl.ds(row, planes, stride=rows), :]


def open_kernel(
    ends, temp, kappa, x_low, x_high, y_low, y_high,
    spread_temp, spread_kappa, start, cond, along_z, minus, plus,
):
    lanes = temp.shape[1]
    side = x_low.shape[0] // 2
    rows = side // RIM
    pitch = rows + PAD
    planes = temp.shape[0] // rows
    minus[...], plus[...] = difference_matrices(lanes)
    fill(start, temp, x_low.at[:side], x_high.at[:side], y_low.at[:RIM], y_high.at[:RIM], rows, pitch, 1.0)
    fill(
        spread_kappa, kappa, x_low.at[side : 2 * side], x_high.at[side : 2 * side],
        y_low.at[RIM : 2 * RIM], y_high.at[RIM : 2 * RIM], rows, pitch, 0.5,
    )
    blocks = planes + 2 * RIM + 1
    conduct_pass(start, spread_kappa, cond, along_z, minus, plus, 0, blocks, pitch)
    mask = rim_mask(ends, pitch, lanes)
    for at in (0, blocks - 1):
        spread_temp[at * pitch : (at + 1) * pitch, :] = jnp.zeros((pitch, lanes), F32)
    spread_temp[blocks * pitch :, :] = jnp.zeros((spread_temp.shape[0] - blocks * pitch, lanes), F32)

    def put(block, size, value):
        value = value.reshape(size, pitch, lanes) * mask[None]
        at = pl.ds(pl.multiple_of(block * pitch, 8), size * pitch)
        spread_temp[at, :] = value.reshape(size * pitch, lanes)

    flow_pass(start, cond, along_z, 1, blocks - 2, pitch, 7, put)


def close_kernel(
    me, ends, got, opened, kappa, source_own, source_low, source_high,
    temp_out, looked, source, now, then, cond, along_z, minus, plus, pieces, turned, found,
):
    lanes = kappa.shape[1]
    planes, rows, _ = temp_out.shape
    pitch = rows + PAD
    total = planes + 2 * RIM
    blocks = total + 1
    minus[...], plus[...] = difference_matrices(lanes)
    wide = RIM - 1
    source[...] = source_own[...]
    for r in range(wide):
        source[pl.ds(PAD - wide + r, total, stride=pitch), :] = source_low[r, :total, :]
        source[pl.ds(PAD + rows + r, total, stride=pitch), :] = source_high[r, :total, :]
    now[...] = opened[...] + source[...]
    mask = rim_mask(ends, pitch, lanes)
    conduct_pass(now, kappa, cond, along_z, minus, plus, 0, blocks, pitch)
    then[0:pitch, :] = jnp.zeros((pitch, lanes), F32)
    then[(blocks - 1) * pitch :, :] = jnp.zeros((then.shape[0] - (blocks - 1) * pitch, lanes), F32)

    def middle(block, size, value):
        at = pl.ds(pl.multiple_of(block * pitch, 8), size * pitch)
        value = (value + source[at, :]).reshape(size, pitch, lanes) * mask[None]
        then[at, :] = value.reshape(size * pitch, lanes)

    flow_pass(now, cond, along_z, 1, blocks - 2, pitch, 7, middle)
    conduct_pass(then, kappa, cond, along_z, minus, plus, 0, blocks, pitch)

    def last(block, size, value):
        at = pl.ds(pl.multiple_of(block * pitch, 8), size * pitch)
        value = (value + source[at, :]).reshape(size, pitch, lanes)[:, PAD:]
        temp_out[pl.ds(block - RIM, size)] = value
        high, low = split(value.reshape(size * rows, lanes))
        at = pl.ds(pl.multiple_of((block - RIM) * rows, rows), size * rows)
        pieces[at, :lanes] = high
        pieces[at, lanes:] = low

    flow_pass(then, cond, along_z, RIM, planes, pitch, 8, last)
    lookup(me[0], got, planes * rows, lanes, looked, pieces, turned, found)


def deposit_kernel(planes, me, got, source, down, up, spread, across, inside, beside):
    blocks, groups, double, _ = got.shape
    half = double // 2
    lanes = source.shape[1]
    rows = across.shape[0]
    pitch = rows + PAD
    patch = planes * rows * lanes
    count = groups * half * LANES
    here = me[0]
    place = iota((rows, LANES), 0)
    place16 = place.astype(jnp.int16)
    zero = jnp.zeros((rows, LANES), BF16)
    order = (1, 0, blocks - 1, blocks - 2)

    for part, distance in enumerate(order):
        block = lax.rem(here + distance, blocks)

        def body(s, unused, part=part, block=block):
            for h in range(half):
                at = pl.multiple_of((s * half + h) * LANES, LANES)
                span = pl.ds(part * count + at, LANES)
                cell = jnp.broadcast_to(got[block, s, h : h + 1, :], (rows, LANES)).astype(I32)
                power = jnp.broadcast_to(got[block, s, half + h : half + h + 1, :], (rows, LANES))
                high, low = split(power)
                lane = (cell & (lanes - 1)).astype(jnp.int16)
                for t in range(lanes // rows):
                    hit = lane == place16 + jnp.int16(t * rows)
                    spread[t * rows : (t + 1) * rows, span] = jnp.where(hit, high, zero)
                    spread[lanes + t * rows : lanes + (t + 1) * rows, span] = jnp.where(hit, low, zero)
                upper = cell >= patch
                row = lax.shift_right_logical(jnp.where(upper, cell - patch, cell), 7)
                across[:, span] = jnp.where((row & (rows - 1)) == place, 1.0, 0.0).astype(BF16)
                plane = row // rows
                own = jnp.where(upper, -1, plane).astype(jnp.int16)
                on = jnp.where(upper, plane, -1).astype(jnp.int16)
                if part == 0:
                    beside[:, span] = own
                elif part == 1:
                    inside[:, pl.ds(at, LANES)] = own
                    beside[:, span] = on
                elif part == 2:
                    inside[:, pl.ds(count + at, LANES)] = on
                    beside[:, span] = own
                else:
                    beside[:, span] = on
            return unused

        lax.fori_loop(0, groups, body, 0)

    source[...] = jnp.zeros(source.shape, F32)

    def product(first, tile, where_x, columns):
        where_y = across[:, columns]
        nothing = jnp.zeros_like(where_y)
        hot = jnp.concatenate(
            [jnp.where(where_x == jnp.int16(x), where_y, nothing) for x in range(tile)], axis=0
        )
        both = lax.dot_general(
            hot, spread[:, columns], (((1,), (1,)), ((), ())), preferred_element_type=F32
        )
        value = both[:, :lanes] + both[:, lanes:]
        for n in range(tile):
            at = pl.ds(pl.multiple_of((first + n + RIM) * pitch + PAD, 8), rows)
            source[at, :] = value[n * rows : (n + 1) * rows]

    tile = 32

    def body(m, unused):
        product(m * tile, tile, inside[...] - (m * tile).astype(jnp.int16), slice(count, 3 * count))
        return unused

    lax.fori_loop(0, planes // tile, body, 0)
    wide = RIM - 1
    product(planes, wide, beside[:, : 2 * count], slice(0, 2 * count))
    low = beside[:, 2 * count :] - jnp.int16(planes - wide)
    product(-wide, wide, low, slice(2 * count, 4 * count))
    planes_all = planes + 2 * RIM
    for r in range(wide):
        down[r, :planes_all, :] = source[pl.ds(PAD + r, planes_all, stride=pitch), :]
        up[r, :planes_all, :] = source[pl.ds(PAD + rows - wide + r, planes_all, stride=pitch), :]


def lookup(me, got, height, lanes, looked, pieces, turned, found):
    blocks, groups, double, _ = got.shape
    half = double // 2
    patch = height * lanes
    chunks = []
    for block, upper in ((me, False), (lax.rem(me + blocks - 1, blocks), True)):
        for s in range(groups):
            for h in range(half):
                cell = got[block, s, h : h + 1, :].astype(I32)
                if upper:
                    cell = jnp.where(cell >= patch, cell - patch, -1)
                else:
                    cell = jnp.where(cell < patch, cell, -1)
                chunks.append(cell)
    count = len(chunks)
    chunks.append(jnp.zeros((LANES - count, LANES), I32))
    turned[...] = jnp.concatenate(chunks, axis=0).T
    lane = iota((LANES, LANES), 1)
    found[...] = jnp.zeros((LANES, LANES), F32)
    width = 4
    for first in range(0, count, width):
        hots = []
        cells = []
        for k in range(first, first + width):
            cell = jnp.broadcast_to(turned[:, k : k + 1], (LANES, LANES))
            cells.append(cell)
            row = lax.shift_right_arithmetic(cell, 7).astype(jnp.int16)
            one = jnp.ones((LANES, LANES), BF16)
            hots.append(
                jnp.concatenate(
                    [
                        jnp.where(
                            row == (lane + r * LANES).astype(jnp.int16), one, jnp.zeros_like(one)
                        )
                        for r in range(height // LANES)
                    ],
                    axis=1,
                )
            )
        both = jnp.dot(jnp.concatenate(hots, axis=0), pieces[...], preferred_element_type=F32)
        value = both[:, :lanes] + both[:, lanes:]
        for n in range(width):
            picked = jnp.take_along_axis(
                value[n * LANES : (n + 1) * LANES], cells[n] & (lanes - 1), axis=1
            )
            found[...] = jnp.where(lane == first + n, picked, found[...])
    back = found[...].T
    at = 0
    for part in range(2):
        for s in range(groups):
            for h in range(half):
                looked[s, part * half + h : part * half + h + 1, :] = back[at : at + 1, :]
                at += 1


def pick(tables, index):
    row = lax.shift_right_logical(index, 7)
    lane = index & (LANES - 1)
    results = [jnp.zeros(index.shape, F32) for _ in tables]
    for r in range(len(tables[0])):
        here = row == r
        for ch, rows in enumerate(tables):
            value = jnp.take_along_axis(jnp.broadcast_to(rows[r], index.shape), lane, axis=1)
            results[ch] = jnp.where(here, value, results[ch])
    return results


def bond_kernel(
    me, back, pos, vel, acted, other, gap, snapped, low_pos, high_pos, low_export, high_export,
    pos_out, vel_out, force, hot,
):
    blocks, groups, double, _ = back.shape
    half = double // 2
    here = me[0]

    def block(distance):
        return lax.rem(here + (blocks + distance), blocks)

    def temps(distance):
        return [
            back[block(distance), j, h : h + 1, :] + back[block(distance + 1), j, half + h : half + h + 1, :]
            for j in range(groups)
            for h in range(half)
        ]

    def rows_of(ref, ch):
        return [ref[ch : ch + 1, r * LANES : (r + 1) * LANES] for r in range(ref.shape[1] // LANES)]

    def ghosts(ref, distance, export):
        tables = [
            [ref[ch, r : r + 1, :] for r in range(ref.shape[1])] for ch in range(3)
        ] + [temps(distance)]
        found = pick(tables, export[...])
        return [[f[r : r + 1] for r in range(f.shape[0])] for f in found]

    own = [rows_of(pos, ch) for ch in range(3)] + [temps(0)]
    low = ghosts(low_pos, -1, low_export)
    high = ghosts(high_pos, 1, high_export)
    wide = [own[ch] + low[ch] + high[ch] for ch in range(4)]
    first = pick(own, acted[...])
    second = pick(wide, other[...])
    delta = [second[ch] - first[ch] for ch in range(3)]
    dist = jnp.sqrt(delta[0] * delta[0] + delta[1] * delta[1] + delta[2] * delta[2])
    relaxed = gap[...] * (1.0 + 0.2 * (0.5 * (first[3] + second[3])))
    scale = (1.0 - snapped[...].astype(F32)) * (dist - relaxed) / jnp.maximum(dist, 0.3)
    values = [split(scale * d) for d in delta]
    values = [piece.astype(F32) for pair in values for piece in pair]
    high_count = len(own[0])
    place = iota((LANES, LANES), 0)
    high_place = iota((high_count, LANES), 0)
    for r in range(acted.shape[0]):
        index = acted[r : r + 1, :]
        span = slice(r * LANES, (r + 1) * LANES)
        hot[:, span] = jnp.where(place == (index & (LANES - 1)), 1.0, 0.0).astype(BF16)
        at_row = lax.shift_right_logical(index, 7) == high_place
        for n, value in enumerate(values):
            force[n * high_count : (n + 1) * high_count, span] = jnp.where(
                at_row, jnp.broadcast_to(value[r : r + 1], (high_count, LANES)), 0.0
            ).astype(BF16)
    total = lax.dot_general(
        force[...], hot[...], (((1,), (1,)), ((), ())), preferred_element_type=F32
    )
    for ch in range(3):
        base = 2 * ch * high_count
        summed = total[base : base + high_count] + total[base + high_count : base + 2 * high_count]
        for r in range(high_count):
            span = slice(r * LANES, (r + 1) * LANES)
            velocity = vel[ch : ch + 1, span] + 0.5 * summed[r : r + 1]
            vel_out[ch : ch + 1, span] = velocity
            pos_out[ch : ch + 1, span] = pos[ch : ch + 1, span] + 0.5 * velocity


def ring(block, distance):
    count = lax.axis_size("cut")
    return lax.ppermute(block, "cut", [(i, (i + distance) % count) for i in range(count)])


def line(block, distance):
    count = lax.axis_size("cross")
    pairs = [(i, i + distance) for i in range(count) if 0 <= i + distance < count]
    return lax.ppermute(block, "cross", pairs)


def per_device(
    warming_above_ambient,
    fourier_stability_factor,
    patch_locator,
    photon_gain_wattage,
    on_skin_marker,
    grain_placements,
    grain_motion_parts,
    tether_acted_grain,
    tether_other_grain,
    tether_relaxed_gap,
    snapped_marker,
    exported_copies,
):
    planes, rows, lanes = warming_above_ambient.shape
    temp = warming_above_ambient.reshape(planes * rows, lanes)
    kappa = fourier_stability_factor.reshape(planes * rows, lanes)
    blocks = lax.axis_size("cut")
    groups = lax.axis_size("cross")
    count = patch_locator.shape[0]
    half = count // groups // LANES
    me = lax.axis_index("cut").reshape(1).astype(I32)
    side = lax.axis_index("cross")
    ends = jnp.stack([side > 0, side < groups - 1]).astype(I32)
    pitch = rows + PAD
    total = planes + 2 * RIM
    flat = jax.ShapeDtypeStruct(((total + 2) * pitch, lanes), F32)
    wide = RIM * rows

    ghost = jnp.concatenate(
        [
            grain_placements.reshape(-1, LANES),
            exported_copies.astype(F32).reshape(-1, LANES),
        ],
        axis=0,
    )
    place_rows = grain_placements.size // LANES
    height = planes * rows
    low = ring(jnp.concatenate([temp[height - wide :], kappa[height - wide :], ghost], axis=0), 1)
    high = ring(jnp.concatenate([temp[:wide], kappa[:wide], ghost], axis=0), -1)

    def neighbour(block):
        ghost = block[2 * wide :]
        return (
            block[: 2 * wide],
            ghost[:place_rows].reshape(3, -1, LANES),
            ghost[place_rows:].astype(I32),
        )

    x_low, low_pos, low_export = neighbour(low)
    x_high, high_pos, high_export = neighbour(high)

    power = on_skin_marker.astype(F32) * photon_gain_wattage * 0.5
    parcel = jnp.concatenate(
        [
            patch_locator.astype(F32).reshape(groups, half, LANES),
            power.reshape(groups, half, LANES),
        ],
        axis=1,
    )

    def exchange(parcel):
        sent = jnp.broadcast_to(parcel[None], (blocks,) + parcel.shape)
        sent = sent.reshape((blocks * groups,) + parcel.shape[1:])
        got = lax.all_to_all(sent, BOTH, split_axis=0, concat_axis=0, tiled=True)
        return got.reshape((blocks, groups) + parcel.shape[1:])

    got = exchange(parcel)

    across = jax.ShapeDtypeStruct((2 * RIM, -(-total // 8) * 8, lanes), F32)
    down, up = call(rows_kernel, [across, across], [temp, kappa, x_low, x_high], smem=0)
    y_low, y_high = line(up, 1), line(down, -1)

    strips = jax.ShapeDtypeStruct((RIM - 1,) + across.shape[1:], F32)
    entries = count
    source, down, up = call(
        functools.partial(deposit_kernel, planes),
        [flat, strips, strips],
        [me, got],
        [
            pltpu.VMEM((2 * lanes, 4 * entries), BF16),
            pltpu.VMEM((rows, 4 * entries), BF16),
            pltpu.VMEM((rows, 2 * entries), jnp.int16),
            pltpu.VMEM((rows, 4 * entries), jnp.int16),
        ],
    )
    source_low, source_high = line(up, 1), line(down, -1)

    grid = pltpu.VMEM(flat.shape, F32)
    matrix = pltpu.VMEM((2 * lanes, 2 * lanes), BF16)
    opened, kappa = call(
        open_kernel,
        [flat, flat],
        [ends, temp, kappa, x_low, x_high, y_low, y_high],
        [grid, grid, grid, matrix, matrix],
    )
    temp, looked = call(
        close_kernel,
        [
            jax.ShapeDtypeStruct((planes, rows, lanes), F32),
            jax.ShapeDtypeStruct((groups, 2 * half, LANES), F32),
        ],
        [me, ends, got, opened, kappa, source, source_low, source_high],
        [
            grid, grid, grid, grid, grid, matrix, matrix,
            pltpu.VMEM((planes * rows, 2 * lanes), BF16),
            pltpu.VMEM((LANES, LANES), I32),
            pltpu.VMEM((LANES, LANES), F32),
        ],
        smem=2,
    )
    back = exchange(looked)
    bonds = tether_acted_grain.shape[0]
    out = jax.ShapeDtypeStruct(grain_placements.shape, F32)
    positions_new, velocities_new = call(
        bond_kernel,
        [out, out],
        [
            me,
            back,
            grain_placements,
            grain_motion_parts,
            tether_acted_grain.reshape(-1, LANES),
            tether_other_grain.reshape(-1, LANES),
            tether_relaxed_gap.reshape(-1, LANES),
            snapped_marker.reshape(-1, LANES),
            low_pos,
            high_pos,
            low_export,
            high_export,
        ],
        [
            pltpu.VMEM((6 * (count // LANES), bonds), BF16),
            pltpu.VMEM((LANES, bonds), BF16),
        ],
    )
    return (temp, positions_new, velocities_new)


def solution(mesh):
    return jax.shard_map(
        per_device,
        mesh=mesh,
        in_specs=(
            P("cut", "cross", None),
            P("cut", "cross", None),
            P(("cut", "cross")),
            P(("cut", "cross")),
            P(("cut", "cross")),
            P(None, ("cut", "cross")),
            P(None, ("cut", "cross")),
            P(("cut", "cross")),
            P(("cut", "cross")),
            P(("cut", "cross")),
            P(("cut", "cross")),
            P(("cut", "cross")),
        ),
        out_specs=(P("cut", "cross", None), P(None, ("cut", "cross")), P(None, ("cut", "cross"))),
        check_vma=False,
    )
```

```python
import functools

import jax
import jax.numpy as jnp
from jax import lax
from jax.experimental import pallas as pl
from jax.experimental.pallas import tpu as pltpu
from jax.sharding import PartitionSpec as P

F32 = jnp.float32
BF16 = jnp.bfloat16
I32 = jnp.int32
LANES = 128
BOTH = ("cut", "cross")
VMEM = pl.BlockSpec(memory_space=pltpu.VMEM)
LIMIT = 32 * 1024 * 1024


def call(kernel, outs, operands, scratch=(), left=0, limit=LIMIT):
    return pl.pallas_call(
        kernel,
        out_shape=outs,
        in_specs=[pl.BlockSpec(memory_space=pltpu.HBM)] * left + [VMEM] * (len(operands) - left),
        out_specs=[VMEM] * len(outs),
        scratch_shapes=list(scratch),
        compiler_params=pltpu.CompilerParams(vmem_limit_bytes=limit),
    )(*operands)


class Either:
    def __init__(self, flag, yes, no):
        self.flag, self.yes, self.no = flag, yes, no
        self.shape = yes.shape

    def __getitem__(self, index):
        yes, no = self.yes[index], self.no[index]
        return jnp.where(jnp.full(yes.shape, self.flag, I32) > 0, yes, no)

    def part(self, index):
        return Either(self.flag, self.yes.at[index], self.no.at[index])


def is_odd(axis):
    return lax.rem(lax.axis_index(axis), 2)


def low_and_high(axis, even, odd):
    flag = is_odd(axis)
    return Either(flag, even, odd), Either(flag, odd, even)


def split(value):
    high = value.astype(BF16)
    return high, (value - high.astype(F32)).astype(BF16)


def iota(shape, dim):
    return lax.broadcasted_iota(I32, shape, dim)


RIM = 3
PAD = 8


def groups_of(count, most):
    return max(n for n in range(1, most + 1) if count % n == 0)


def difference_matrices(lanes):
    shape = (2 * lanes, 2 * lanes)
    given = iota(shape, 0) & (lanes - 1)
    wanted = iota(shape, 1)
    lower = wanted >= lanes
    wanted = wanted & (lanes - 1)
    beside = jnp.where(lower, wanted - 1, wanted + 1)
    neighbour = jnp.where(given == beside, 1.0, 0.0)
    same = jnp.where(given == wanted, 1.0, 0.0)
    return (neighbour - same).astype(BF16), (neighbour + same).astype(BF16)


def pieces_of(value):
    high, low = split(value)
    return jnp.concatenate([high, low], axis=1)


def conduct_pass(temp, kappa, cond, along_z, minus, plus, first, blocks, pitch):
    lanes = temp.shape[1]
    size = groups_of(blocks, 135)

    def body(n, unused):
        at = pl.ds(pl.multiple_of((first + n * size) * pitch, 8), size * pitch)
        t = temp[at, :]
        c = kappa[at, :] * (0.5 + 1.0 / (1.0 + t * t))
        cond[at, :] = c
        change = jnp.dot(pieces_of(t), minus[...], preferred_element_type=F32)
        both = jnp.dot(pieces_of(c), plus[...], preferred_element_type=F32)
        along_z[at, :] = change[:, :lanes] * both[:, :lanes] + change[:, lanes:] * both[:, lanes:]
        return unused

    lax.fori_loop(0, blocks // size, body, 0)


def flow_pass(temp, cond, along_z, first, blocks, pitch, most, put):
    size = groups_of(blocks, most)

    def body(n, unused):
        block = first + n * size
        base = pl.multiple_of(block * pitch, 8)
        at = pl.ds(base, size * pitch)
        t = temp[at, :]
        c = cond[at, :]
        net = along_z[at, :]
        for shift in (pitch, -pitch, 1, -1):
            beside = pl.ds(base + shift, size * pitch)
            net = net + (c + cond[beside, :]) * (temp[beside, :] - t)
        put(block, size, t + net)
        return unused

    lax.fori_loop(0, blocks // size, body, 0)


def rim_mask(pitch, lanes):
    place = iota((pitch, lanes), 0)
    side = lax.axis_index("cross")
    below = jnp.where(side > 0, 1.0, 0.0)
    above = jnp.where(side < lax.axis_size("cross") - 1, 1.0, 0.0)
    return jnp.where(place < PAD - RIM, above, jnp.where(place < PAD, below, 1.0))


def fill(flat, own, x_low, x_high, y_low, y_high, rows, pitch, scale):
    planes = own.shape[0] // rows
    total = planes + 2 * RIM
    flat[...] = jnp.zeros(flat.shape, F32)

    def place(p, part):
        flat[pl.ds(pl.multiple_of(p * pitch + PAD, 8), rows), :] = part * scale

    for n in range(RIM):
        place(n, x_low[n * rows : (n + 1) * rows, :])
        place(RIM + planes + n, x_high[n * rows : (n + 1) * rows, :])

    def body(p, unused):
        place(p + RIM, own[pl.ds(pl.multiple_of(p * rows, 8), rows), :])
        return unused

    lax.fori_loop(0, planes, body, 0, unroll=8)
    for r in range(RIM):
        flat[pl.ds(PAD - RIM + r, total, stride=pitch), :] = y_low[r, :total, :] * scale
        flat[pl.ds(PAD + rows + r, total, stride=pitch), :] = y_high[r, :total, :] * scale


def parcel_kernel(
    temp, kappa, cells, watts, marks, pos, export, sent, even, odd,
    cell_in, watt_in, mark_in, pos_in, export_in, sems,
):
    count = pos.shape[1] // LANES
    exports = export.shape[0]
    wide = (even.shape[0] - 3 * count - exports) // 2
    height = temp.shape[0]
    moves = [(cells, cell_in), (watts, watt_in), (marks, mark_in), (pos, pos_in), (export, export_in)]
    tail = (1 - is_odd("cut")) * (height - wide)
    for n, field in enumerate((temp, kappa)):
        target = pl.ds(n * wide, wide)
        for out, start in ((even, tail), (odd, height - wide - tail)):
            moves.append((field.at[pl.ds(pl.multiple_of(start, 16), wide)], out.at[target]))
    copies = [pltpu.make_async_copy(*move, sems.at[n]) for n, move in enumerate(moves)]
    for copy in copies:
        copy.start()
    for copy in copies[:3]:
        copy.wait()
    power = mark_in[...].astype(F32) * watt_in[...] * 0.5
    cell = cell_in[...].astype(F32)
    blocks, groups, double, _ = sent.shape
    half = double // 2
    for block in range(blocks):
        for s in range(groups):
            sent[block, s, :half, :] = cell[s * half : (s + 1) * half]
            sent[block, s, half:, :] = power[s * half : (s + 1) * half]
    for copy in copies[3:5]:
        copy.wait()
    for out in (even, odd):
        for ch in range(3):
            for r in range(count):
                at = 2 * wide + ch * count + r
                out[at : at + 1, :] = pos_in[ch : ch + 1, r * LANES : (r + 1) * LANES]
        out[2 * wide + 3 * count :, :] = export_in[...].astype(F32)
    for copy in copies[5:]:
        copy.wait()


def rows_kernel(rows, after, temp, kappa, even_x, odd_x, even, odd):
    side = RIM * rows
    planes = temp.shape[0] // rows
    low, high = low_and_high("cut", even_x, odd_x)
    top = (1 - is_odd("cross")) * (rows - RIM)
    for n, own in enumerate((temp, kappa)):
        for r in range(RIM):
            for out, first in ((even, top), (odd, rows - RIM - top)):
                target = n * RIM + r
                for p in range(RIM):
                    at = pl.ds(n * side + p * rows + first + r, 1)
                    out[target, p : p + 1, :] = low[at, :]
                    out[target, RIM + planes + p : RIM + planes + p + 1, :] = high[at, :]
                out[target, RIM : RIM + planes, :] = own[pl.ds(first + r, planes, stride=rows), :]


def open_kernel(
    rows, temp, kappa, source, even_x, odd_x, even_y, odd_y,
    spread_temp, spread_kappa, start, cond, along_z, minus, plus,
):
    lanes = temp.shape[1]
    x_low, x_high = low_and_high("cut", even_x, odd_x)
    y_low, y_high = low_and_high("cross", even_y, odd_y)
    side = RIM * rows
    pitch = rows + PAD
    planes = temp.shape[0] // rows
    minus[...], plus[...] = difference_matrices(lanes)
    fill(start, temp, x_low.part(slice(None, side)), x_high.part(slice(None, side)), y_low.part(slice(None, RIM)), y_high.part(slice(None, RIM)), rows, pitch, 1.0)
    fill(
        spread_kappa, kappa, x_low.part(slice(side, 2 * side)), x_high.part(slice(side, 2 * side)),
        y_low.part(slice(RIM, 2 * RIM)), y_high.part(slice(RIM, 2 * RIM)), rows, pitch, 0.5,
    )
    blocks = planes + 2 * RIM + 1
    conduct_pass(start, spread_kappa, cond, along_z, minus, plus, 0, blocks, pitch)
    mask = rim_mask(pitch, lanes)
    for at in (0, blocks - 1):
        spread_temp[at * pitch : (at + 1) * pitch, :] = jnp.zeros((pitch, lanes), F32)
    spread_temp[blocks * pitch :, :] = jnp.zeros((spread_temp.shape[0] - blocks * pitch, lanes), F32)

    def put(block, size, value):
        value = value.reshape(size, pitch, lanes) * mask[None]
        at = pl.ds(pl.multiple_of(block * pitch, 8), size * pitch)
        spread_temp[at, :] = value.reshape(size * pitch, lanes) + source[at, :]

    flow_pass(start, cond, along_z, 1, blocks - 2, pitch, 133, put)


def close_kernel(
    got, opened, kappa, source_own, even_y, odd_y,
    temp_out, looked, source, now, then, cond, along_z, minus, plus, pieces, turned, found,
):
    lanes = kappa.shape[1]
    planes, rows, _ = temp_out.shape
    pitch = rows + PAD
    total = planes + 2 * RIM
    blocks = total + 1
    minus[...], plus[...] = difference_matrices(lanes)
    wide = RIM - 1
    source[...] = source_own[...]
    now[...] = opened[...]
    low, high = low_and_high("cross", even_y, odd_y)
    for r in range(wide):
        for first, beside in ((PAD - wide + r, low), (PAD + rows + r, high)):
            at = pl.ds(first, total, stride=pitch)
            strip = beside[r, :total, :]
            source[at, :] = strip
            now[at, :] = now[at, :] + strip
    mask = rim_mask(pitch, lanes)
    conduct_pass(now, kappa, cond, along_z, minus, plus, 0, blocks, pitch)
    then[0:pitch, :] = jnp.zeros((pitch, lanes), F32)
    then[(blocks - 1) * pitch :, :] = jnp.zeros((then.shape[0] - (blocks - 1) * pitch, lanes), F32)

    def middle(block, size, value):
        at = pl.ds(pl.multiple_of(block * pitch, 8), size * pitch)
        value = (value + source[at, :]).reshape(size, pitch, lanes) * mask[None]
        then[at, :] = value.reshape(size * pitch, lanes)

    flow_pass(now, cond, along_z, 1, blocks - 2, pitch, 133, middle)
    conduct_pass(then, kappa, cond, along_z, minus, plus, 0, blocks, pitch)

    def last(block, size, value):
        at = pl.ds(pl.multiple_of(block * pitch, 8), size * pitch)
        value = (value + source[at, :]).reshape(size, pitch, lanes)[:, PAD:]
        temp_out[pl.ds(block - RIM, size)] = value
        high, low = split(value.reshape(size * rows, lanes))
        at = pl.ds(pl.multiple_of((block - RIM) * rows, rows), size * rows)
        pieces[at, :lanes] = high
        pieces[at, lanes:] = low

    flow_pass(then, cond, along_z, RIM, planes, pitch, 8, last)
    lookup(lax.axis_index("cut"), got, planes * rows, lanes, looked, pieces, turned, found)


def deposit_kernel(planes, got, source, even, odd, spread, across, inside, beside):
    blocks, groups, double, _ = got.shape
    half = double // 2
    lanes = source.shape[1]
    rows = across.shape[0]
    pitch = rows + PAD
    patch = planes * rows * lanes
    count = groups * half * LANES
    here = lax.axis_index("cut")
    place = iota((rows, LANES), 0)
    place16 = place.astype(jnp.int16)
    zero = jnp.zeros((rows, LANES), BF16)
    order = (1, 0, blocks - 1, blocks - 2)

    for part, distance in enumerate(order):
        block = lax.rem(here + distance, blocks)

        def body(s, unused, part=part, block=block):
            for h in range(half):
                at = pl.multiple_of((s * half + h) * LANES, LANES)
                span = pl.ds(part * count + at, LANES)
                cell = jnp.broadcast_to(got[block, s, h : h + 1, :], (rows, LANES)).astype(I32)
                power = jnp.broadcast_to(got[block, s, half + h : half + h + 1, :], (rows, LANES))
                high, low = split(power)
                lane = (cell & (lanes - 1)).astype(jnp.int16)
                for t in range(lanes // rows):
                    hit = lane == place16 + jnp.int16(t * rows)
                    spread[t * rows : (t + 1) * rows, span] = jnp.where(hit, high, zero)
                    spread[lanes + t * rows : lanes + (t + 1) * rows, span] = jnp.where(hit, low, zero)
                upper = cell >= patch
                row = lax.shift_right_logical(jnp.where(upper, cell - patch, cell), 7)
                across[:, span] = jnp.where((row & (rows - 1)) == place, 1.0, 0.0).astype(BF16)
                plane = row // rows
                own = jnp.where(upper, -1, plane).astype(jnp.int16)
                on = jnp.where(upper, plane, -1).astype(jnp.int16)
                if part == 0:
                    beside[:, span] = own
                elif part == 1:
                    inside[:, pl.ds(at, LANES)] = own
                    beside[:, span] = on
                elif part == 2:
                    inside[:, pl.ds(count + at, LANES)] = on
                    beside[:, span] = own
                else:
                    beside[:, span] = on
            return unused

        lax.fori_loop(0, groups, body, 0)

    source[...] = jnp.zeros(source.shape, F32)

    def product(first, tile, where_x, columns):
        where_y = across[:, columns]
        nothing = jnp.zeros_like(where_y)
        hot = jnp.concatenate(
            [jnp.where(where_x == jnp.int16(x), where_y, nothing) for x in range(tile)], axis=0
        )
        both = lax.dot_general(
            hot, spread[:, columns], (((1,), (1,)), ((), ())), preferred_element_type=F32
        )
        value = both[:, :lanes] + both[:, lanes:]
        for n in range(tile):
            at = pl.ds(pl.multiple_of((first + n + RIM) * pitch + PAD, 8), rows)
            source[at, :] = value[n * rows : (n + 1) * rows]

    tile = 32

    def body(m, unused):
        product(m * tile, tile, inside[...] - (m * tile).astype(jnp.int16), slice(count, 3 * count))
        return unused

    lax.fori_loop(0, planes // tile, body, 0)
    wide = RIM - 1
    product(planes, wide, beside[:, : 2 * count], slice(0, 2 * count))
    low = beside[:, 2 * count :] - jnp.int16(planes - wide)
    product(-wide, wide, low, slice(2 * count, 4 * count))
    planes_all = planes + 2 * RIM
    top = (1 - is_odd("cross")) * (rows - wide)
    for r in range(wide):
        for out, first in ((even, top), (odd, rows - wide - top)):
            out[r, :planes_all, :] = source[pl.ds(PAD + first + r, planes_all, stride=pitch), :]


def lookup(me, got, height, lanes, looked, pieces, turned, found):
    blocks, groups, double, _ = got.shape
    half = double // 2
    patch = height * lanes
    chunks = []
    for block, upper in ((me, False), (lax.rem(me + blocks - 1, blocks), True)):
        for s in range(groups):
            for h in range(half):
                cell = got[block, s, h : h + 1, :].astype(I32)
                if upper:
                    cell = jnp.where(cell >= patch, cell - patch, -1)
                else:
                    cell = jnp.where(cell < patch, cell, -1)
                chunks.append(cell)
    count = len(chunks)
    chunks.append(jnp.zeros((LANES - count, LANES), I32))
    turned[...] = jnp.concatenate(chunks, axis=0).T
    lane = iota((LANES, LANES), 1)
    found[...] = jnp.zeros((LANES, LANES), F32)
    width = 4
    for first in range(0, count, width):
        hots = []
        cells = []
        for k in range(first, first + width):
            cell = jnp.broadcast_to(turned[:, k : k + 1], (LANES, LANES))
            cells.append(cell)
            row = lax.shift_right_arithmetic(cell, 7).astype(jnp.int16)
            one = jnp.ones((LANES, LANES), BF16)
            hots.append(
                jnp.concatenate(
                    [
                        jnp.where(
                            row == (lane + r * LANES).astype(jnp.int16), one, jnp.zeros_like(one)
                        )
                        for r in range(height // LANES)
                    ],
                    axis=1,
                )
            )
        both = jnp.dot(jnp.concatenate(hots, axis=0), pieces[...], preferred_element_type=F32)
        value = both[:, :lanes] + both[:, lanes:]
        for n in range(width):
            picked = jnp.take_along_axis(
                value[n * LANES : (n + 1) * LANES], cells[n] & (lanes - 1), axis=1
            )
            found[...] = jnp.where(lane == first + n, picked, found[...])
    back = found[...].T
    at = 0
    for part in range(2):
        for s in range(groups):
            for h in range(half):
                for block in range(blocks):
                    looked[block, s, part * half + h : part * half + h + 1, :] = back[at : at + 1, :]
                at += 1


def pick(tables, index):
    row = lax.shift_right_logical(index, 7)
    lane = index & (LANES - 1)
    results = [jnp.zeros(index.shape, F32) for _ in tables]
    for r in range(len(tables[0])):
        here = row == r
        for ch, rows in enumerate(tables):
            value = jnp.take_along_axis(jnp.broadcast_to(rows[r], index.shape), lane, axis=1)
            results[ch] = jnp.where(here, value, results[ch])
    return results


def rows_of(ref, ch):
    return [ref[ch : ch + 1, r * LANES : (r + 1) * LANES] for r in range(ref.shape[1] // LANES)]


def stretch_kernel(
    side, after, pos, acted, other, gap, snapped, even_x, odd_x, base, slope, delta, hot,
):
    count = pos.shape[1] // LANES
    low_ghost, high_ghost = low_and_high("cut", even_x, odd_x)

    def ghosts(ref):
        places = side + 3 * count
        tables = [
            [ref[side + ch * count + r : side + ch * count + r + 1, :] for r in range(count)]
            for ch in range(3)
        ]
        found = pick(tables, ref[places:, :].astype(I32))
        return [[f[r : r + 1] for r in range(f.shape[0])] for f in found]

    own = [rows_of(pos, ch) for ch in range(3)]
    low = ghosts(low_ghost)
    high = ghosts(high_ghost)
    first = pick(own, acted[...])
    second = pick([own[ch] + low[ch] + high[ch] for ch in range(3)], other[...])
    d = [second[ch] - first[ch] for ch in range(3)]
    dist = jnp.sqrt(d[0] * d[0] + d[1] * d[1] + d[2] * d[2])
    weight = (1.0 - snapped[...].astype(F32)) / jnp.maximum(dist, 0.3)
    base[...] = weight * (dist - gap[...])
    slope[...] = weight * (gap[...] * (0.2 * 0.5))
    for ch in range(3):
        delta[ch] = d[ch]
    place = iota((16, LANES), 0).astype(jnp.int16)
    one = jnp.ones((16, LANES), BF16)
    for r in range(acted.shape[0]):
        lane = jnp.broadcast_to(acted[r : r + 1, :] & (LANES - 1), (16, LANES)).astype(jnp.int16)
        for t in range(LANES // 16):
            hot[t * 16 : (t + 1) * 16, r * LANES : (r + 1) * LANES] = jnp.where(
                lane == place + jnp.int16(t * 16), one, jnp.zeros_like(one)
            )


def bond_kernel(
    places, back, pos, vel, acted, other, even_x, odd_x, base, slope, delta, hot,
    pos_out, vel_out, force,
):
    blocks, groups, double, _ = back.shape
    half = double // 2
    here = lax.axis_index("cut")
    low_ghost, high_ghost = low_and_high("cut", even_x, odd_x)

    def block(distance):
        return lax.rem(here + (blocks + distance), blocks)

    def temps(distance):
        return [
            back[block(distance), j, h : h + 1, :] + back[block(distance + 1), j, half + h : half + h + 1, :]
            for j in range(groups)
            for h in range(half)
        ]

    def ghosts(distance, ref):
        found = pick([temps(distance)], ref[places:, :].astype(I32))[0]
        return [found[r : r + 1] for r in range(found.shape[0])]

    own = temps(0)
    first = pick([own], acted[...])[0]
    second = pick([own + ghosts(-1, low_ghost) + ghosts(1, high_ghost)], other[...])[0]
    scale = base[...] - slope[...] * (first + second)
    values = [split(scale * delta[ch]) for ch in range(3)]
    values = [piece.astype(F32) for pair in values for piece in pair]
    high_count = len(own)
    high_place = iota((high_count, LANES), 0)
    for r in range(acted.shape[0]):
        span = slice(r * LANES, (r + 1) * LANES)
        at_row = lax.shift_right_logical(acted[r : r + 1, :], 7) == high_place
        for n, value in enumerate(values):
            force[n * high_count : (n + 1) * high_count, span] = jnp.where(
                at_row, jnp.broadcast_to(value[r : r + 1], (high_count, LANES)), 0.0
            ).astype(BF16)
    total = lax.dot_general(
        force[...], hot[...], (((1,), (1,)), ((), ())), preferred_element_type=F32
    )
    for ch in range(3):
        base_row = 2 * ch * high_count
        summed = (
            total[base_row : base_row + high_count]
            + total[base_row + high_count : base_row + 2 * high_count]
        )
        for r in range(high_count):
            span = slice(r * LANES, (r + 1) * LANES)
            velocity = vel[ch : ch + 1, span] + 0.5 * summed[r : r + 1]
            vel_out[ch : ch + 1, span] = velocity
            pos_out[ch : ch + 1, span] = pos[ch : ch + 1, span] + 0.5 * velocity


def swaps(axis, closed, even, odd):
    count = lax.axis_size(axis)
    results = []
    for first, block in ((0, even), (1, odd)):
        pairs = []
        for i in range(first, count if closed else count - 1, 2):
            pairs += [(i, (i + 1) % count), ((i + 1) % count, i)]
        results.append(lax.ppermute(block, axis, pairs))
    return results


def per_device(
    warming_above_ambient,
    fourier_stability_factor,
    patch_locator,
    photon_gain_wattage,
    on_skin_marker,
    grain_placements,
    grain_motion_parts,
    tether_acted_grain,
    tether_other_grain,
    tether_relaxed_gap,
    snapped_marker,
    exported_copies,
):
    planes, rows, lanes = warming_above_ambient.shape
    temp = warming_above_ambient.reshape(planes * rows, lanes)
    kappa = fourier_stability_factor.reshape(planes * rows, lanes)
    blocks = lax.axis_size("cut")
    groups = lax.axis_size("cross")
    count = patch_locator.shape[0]
    half = count // groups // LANES
    pitch = rows + PAD
    total = planes + 2 * RIM
    flat = jax.ShapeDtypeStruct(((total + 2) * pitch, lanes), F32)
    wide = RIM * rows

    exports = exported_copies.shape[0] // LANES
    places = 2 * wide + grain_placements.size // LANES
    carried = jax.ShapeDtypeStruct((places + exports, LANES), F32)
    parcel = jax.ShapeDtypeStruct((blocks, groups, 2 * half, LANES), F32)
    sent, even_x, odd_x = call(
        parcel_kernel,
        [parcel, carried, carried],
        [
            temp,
            kappa,
            patch_locator.reshape(-1, LANES),
            photon_gain_wattage.reshape(-1, LANES),
            on_skin_marker.reshape(-1, LANES),
            grain_placements,
            exported_copies.reshape(-1, LANES),
        ],
        [
            pltpu.VMEM((count // LANES, LANES), I32),
            pltpu.VMEM((count // LANES, LANES), F32),
            pltpu.VMEM((count // LANES, LANES), I32),
            pltpu.VMEM(grain_placements.shape, F32),
            pltpu.VMEM((exports, LANES), I32),
            pltpu.SemaphoreType.DMA((9,)),
        ],
        left=7,
        limit=None,
    )

    def exchange(sent):
        flat = sent.reshape((blocks * groups,) + sent.shape[2:])
        got = lax.all_to_all(flat, BOTH, split_axis=0, concat_axis=0, tiled=True)
        return got.reshape(sent.shape)

    got = exchange(sent)
    even_x, odd_x = swaps("cut", True, even_x, odd_x)

    across = jax.ShapeDtypeStruct((2 * RIM, -(-total // 8) * 8, lanes), F32)
    even_y, odd_y = call(
        functools.partial(rows_kernel, rows),
        [across, across],
        [got, temp, kappa, even_x, odd_x],
        left=1,
    )
    even_y, odd_y = swaps("cross", False, even_y, odd_y)

    strips = jax.ShapeDtypeStruct((RIM - 1,) + across.shape[1:], F32)
    entries = count
    source, even_s, odd_s = call(
        functools.partial(deposit_kernel, planes),
        [flat, strips, strips],
        [got],
        [
            pltpu.VMEM((2 * lanes, 4 * entries), BF16),
            pltpu.VMEM((rows, 4 * entries), BF16),
            pltpu.VMEM((rows, 2 * entries), jnp.int16),
            pltpu.VMEM((rows, 4 * entries), jnp.int16),
        ],
    )
    even_s, odd_s = swaps("cross", False, even_s, odd_s)

    grid = pltpu.VMEM(flat.shape, F32)
    matrix = pltpu.VMEM((2 * lanes, 2 * lanes), BF16)
    opened, kappa = call(
        functools.partial(open_kernel, rows),
        [flat, flat],
        [temp, kappa, source, even_x, odd_x, even_y, odd_y],
        [grid, grid, grid, matrix, matrix],
    )
    temp, looked = call(
        close_kernel,
        [
            jax.ShapeDtypeStruct((planes, rows, lanes), F32),
            parcel,
        ],
        [got, opened, kappa, source, even_s, odd_s],
        [
            grid, grid, grid, grid, grid, matrix, matrix,
            pltpu.VMEM((planes * rows, 2 * lanes), BF16),
            pltpu.VMEM((LANES, LANES), I32),
            pltpu.VMEM((LANES, LANES), F32),
        ],
    )
    back = exchange(looked)
    acted = tether_acted_grain.reshape(-1, LANES)
    other = tether_other_grain.reshape(-1, LANES)
    entry = jax.ShapeDtypeStruct(acted.shape, F32)
    base, slope, delta, hot = call(
        functools.partial(stretch_kernel, 2 * wide),
        [
            entry,
            entry,
            jax.ShapeDtypeStruct((3,) + acted.shape, F32),
            jax.ShapeDtypeStruct((LANES, acted.size), BF16),
        ],
        [
            looked,
            grain_placements,
            acted,
            other,
            tether_relaxed_gap.reshape(-1, LANES),
            snapped_marker.reshape(-1, LANES),
            even_x,
            odd_x,
        ],
        left=1,
    )
    out = jax.ShapeDtypeStruct(grain_placements.shape, F32)
    positions_new, velocities_new = call(
        functools.partial(bond_kernel, places),
        [out, out],
        [
            back, grain_placements, grain_motion_parts, acted, other, even_x, odd_x,
            base, slope, delta, hot,
        ],
        [pltpu.VMEM((6 * (count // LANES), acted.size), BF16)],
    )
    return (temp, positions_new, velocities_new)


def solution(mesh):
    return jax.shard_map(
        per_device,
        mesh=mesh,
        in_specs=(
            P("cut", "cross", None),
            P("cut", "cross", None),
            P(("cut", "cross")),
            P(("cut", "cross")),
            P(("cut", "cross")),
            P(None, ("cut", "cross")),
            P(None, ("cut", "cross")),
            P(("cut", "cross")),
            P(("cut", "cross")),
            P(("cut", "cross")),
            P(("cut", "cross")),
            P(("cut", "cross")),
        ),
        out_specs=(P("cut", "cross", None), P(None, ("cut", "cross")), P(None, ("cut", "cross"))),
        check_vma=False,
    )
```

```python
import functools

import jax
import jax.numpy as jnp
from jax import lax
from jax.experimental import pallas as pl
from jax.experimental.pallas import tpu as pltpu
from jax.sharding import PartitionSpec as P

F32 = jnp.float32
BF16 = jnp.bfloat16
I32 = jnp.int32
LANES = 128
BOTH = ("cut", "cross")
VMEM = pl.BlockSpec(memory_space=pltpu.VMEM)
LIMIT = 32 * 1024 * 1024


def call(kernel, outs, operands, scratch=(), left=0, limit=LIMIT):
    return pl.pallas_call(
        kernel,
        out_shape=outs,
        in_specs=[pl.BlockSpec(memory_space=pltpu.HBM)] * left + [VMEM] * (len(operands) - left),
        out_specs=[VMEM] * len(outs),
        scratch_shapes=list(scratch),
        compiler_params=pltpu.CompilerParams(vmem_limit_bytes=limit),
    )(*operands)


class Either:
    def __init__(self, flag, yes, no):
        self.flag, self.yes, self.no = flag, yes, no
        self.shape = yes.shape

    def __getitem__(self, index):
        yes, no = self.yes[index], self.no[index]
        return jnp.where(jnp.full(yes.shape, self.flag, I32) > 0, yes, no)

    def part(self, index):
        return Either(self.flag, self.yes.at[index], self.no.at[index])


def is_odd(axis):
    return lax.rem(lax.axis_index(axis), 2)


def low_and_high(axis, even, odd):
    flag = is_odd(axis)
    return Either(flag, even, odd), Either(flag, odd, even)


def split(value):
    high = value.astype(BF16)
    return high, (value - high.astype(F32)).astype(BF16)


def iota(shape, dim):
    return lax.broadcasted_iota(I32, shape, dim)


RIM = 3
PAD = 8
QUARTERS = 4


def groups_of(count, most):
    return max(n for n in range(1, most + 1) if count % n == 0)


def difference_matrices(lanes):
    shape = (2 * lanes, 2 * lanes)
    given = iota(shape, 0) & (lanes - 1)
    wanted = iota(shape, 1)
    lower = wanted >= lanes
    wanted = wanted & (lanes - 1)
    beside = jnp.where(lower, wanted - 1, wanted + 1)
    neighbour = jnp.where(given == beside, 1.0, 0.0)
    same = jnp.where(given == wanted, 1.0, 0.0)
    return (neighbour - same).astype(BF16), (neighbour + same).astype(BF16)


def pieces_of(value):
    high, low = split(value)
    return jnp.concatenate([high, low], axis=1)


def conduct_pass(temp, kappa, cond, along_z, minus, plus, first, blocks, pitch):
    lanes = temp.shape[1]
    size = groups_of(blocks, 135)

    def body(n, unused):
        at = pl.ds(pl.multiple_of((first + n * size) * pitch, 8), size * pitch)
        t = temp[at, :]
        c = kappa[at, :] * (0.5 + 1.0 / (1.0 + t * t))
        cond[at, :] = c
        change = jnp.dot(pieces_of(t), minus[...], preferred_element_type=F32)
        both = jnp.dot(pieces_of(c), plus[...], preferred_element_type=F32)
        along_z[at, :] = change[:, :lanes] * both[:, :lanes] + change[:, lanes:] * both[:, lanes:]
        return unused

    lax.fori_loop(0, blocks // size, body, 0)


def flow_pass(temp, cond, along_z, first, blocks, pitch, most, put):
    size = groups_of(blocks, most)

    def body(n, unused):
        block = first + n * size
        base = pl.multiple_of(block * pitch, 8)
        at = pl.ds(base, size * pitch)
        t = temp[at, :]
        c = cond[at, :]
        net = along_z[at, :]
        for shift in (pitch, -pitch, 1, -1):
            beside = pl.ds(base + shift, size * pitch)
            net = net + (c + cond[beside, :]) * (temp[beside, :] - t)
        put(block, size, t + net)
        return unused

    lax.fori_loop(0, blocks // size, body, 0)


def rim_mask(pitch, lanes):
    place = iota((pitch, lanes), 0)
    side = lax.axis_index("cross")
    below = jnp.where(side > 0, 1.0, 0.0)
    above = jnp.where(side < lax.axis_size("cross") - 1, 1.0, 0.0)
    return jnp.where(place < PAD - RIM, above, jnp.where(place < PAD, below, 1.0))


def fill(flat, own, x_low, x_high, y_low, y_high, rows, pitch, scale):
    planes = own.shape[0] // rows
    total = planes + 2 * RIM
    flat[...] = jnp.zeros(flat.shape, F32)

    def place(p, part):
        flat[pl.ds(pl.multiple_of(p * pitch + PAD, 8), rows), :] = part * scale

    for n in range(RIM):
        place(n, x_low[n * rows : (n + 1) * rows, :])
        place(RIM + planes + n, x_high[n * rows : (n + 1) * rows, :])

    def body(p, unused):
        place(p + RIM, own[pl.ds(pl.multiple_of(p * rows, 8), rows), :])
        return unused

    lax.fori_loop(0, planes, body, 0, unroll=8)
    for r in range(RIM):
        flat[pl.ds(PAD - RIM + r, total, stride=pitch), :] = y_low[r, :total, :] * scale
        flat[pl.ds(PAD + rows + r, total, stride=pitch), :] = y_high[r, :total, :] * scale


def parcel_kernel(
    temp, kappa, cells, watts, marks, pos, export, sent, even, odd, code,
    cell_in, watt_in, mark_in, pos_in, export_in, sems,
):
    count = pos.shape[1] // LANES
    exports = export.shape[0]
    wide = (even.shape[0] - 4 * count - exports) // 2
    height, lanes = temp.shape
    patch = height * lanes
    half, groups, _ = code.shape
    cap = half * LANES
    quarter = cap // QUARTERS
    moves = [(cells, cell_in), (watts, watt_in), (marks, mark_in), (pos, pos_in), (export, export_in)]
    tail = (1 - is_odd("cut")) * (height - wide)
    for n, field in enumerate((temp, kappa)):
        target = pl.ds(n * wide, wide)
        for out, start in ((even, tail), (odd, height - wide - tail)):
            moves.append((field.at[pl.ds(pl.multiple_of(start, 16), wide)], out.at[target]))
    copies = [pltpu.make_async_copy(*move, sems.at[n]) for n, move in enumerate(moves)]
    for copy in copies:
        copy.start()
    for copy in copies[:3]:
        copy.wait()

    def by_group(ref):
        return jnp.concatenate([ref[pl.ds(h, groups, stride=half), :] for h in range(half)], axis=1)

    cell = by_group(cell_in)
    power = by_group(mark_in).astype(F32) * by_group(watt_in) * 0.5
    upper = cell >= patch
    cell = jnp.where(upper, cell - patch, cell)
    share = cell // (patch // QUARTERS)
    kind = jnp.where(upper, share + QUARTERS, share)
    members = [jnp.where(kind == k, 1.0, 0.0) for k in range(2 * QUARTERS)]
    earlier = jnp.where(iota((cap, cap), 0) < iota((cap, cap), 1), 1.0, 0.0).astype(BF16)
    before = jnp.dot(
        jnp.concatenate(members, axis=0).astype(BF16), earlier, preferred_element_type=F32
    )
    rank = jnp.zeros((groups, cap), F32)
    most = jnp.zeros((groups, 1), F32)
    for k, member in enumerate(members):
        ahead = before[k * groups : (k + 1) * groups]
        rank = rank + member * ahead
        most = jnp.maximum(most, ahead[:, cap - 1 :] + member[:, cap - 1 :])
    fits = jnp.broadcast_to(most, (groups, cap)) <= quarter
    region = share ^ is_odd("cross")
    slot = jnp.where(fits, region * quarter + rank.astype(I32), iota((groups, cap), 1))
    mark = jnp.where(upper, slot + cap, slot)
    for h in range(half):
        code[h] = mark[:, h * LANES : (h + 1) * LANES]
    number = cell + 1
    digits = [number & 255, lax.shift_right_logical(number, 8) & 255, lax.shift_right_logical(number, 16)]
    digits = [d.astype(F32) for d in digits]
    top = power.astype(BF16).astype(F32)
    middle = (power - top).astype(BF16).astype(F32)
    digits += [top, middle, power - top - middle]
    stacked = [jnp.where(upper, 0.0, d) for d in digits] + [jnp.where(upper, d, 0.0) for d in digits]
    stacked = jnp.concatenate(stacked, axis=0).astype(BF16)
    place = iota((16, cap), 0).astype(jnp.int16)
    one = jnp.ones((16, cap), BF16)
    of_group = iota((stacked.shape[0], cap), 0) & (groups - 1)
    moved = jnp.zeros(stacked.shape, F32)
    for j in range(groups):
        goes = jnp.broadcast_to(slot[j : j + 1], (16, cap)).astype(jnp.int16)
        swap = jnp.concatenate(
            [
                jnp.where(goes == place + jnp.int16(t * 16), one, jnp.zeros_like(one))
                for t in range(cap // 16)
            ],
            axis=0,
        )
        result = lax.dot_general(
            stacked, swap, (((1,), (1,)), ((), ())), preferred_element_type=F32
        )
        moved = jnp.where(of_group == j, result, moved)
    sign = jnp.where(fits, 1.0, -1.0)
    blocks = sent.shape[0] // (groups * 4 * half)
    for kind in range(2):
        part = [
            moved[(6 * kind + n) * groups : (6 * kind + n + 1) * groups] for n in range(6)
        ]
        numbers = (part[0] + 256.0 * part[1] + 65536.0 * part[2]) * sign
        powers = part[3] + part[4] + part[5]
        for n, value in enumerate((numbers, powers)):
            for h in range(half):
                row = kind * 2 * half + n * half + h
                for block in range(blocks):
                    at = pl.ds(block * groups * 4 * half + row, groups, stride=4 * half)
                    sent[at, :] = value[:, h * LANES : (h + 1) * LANES]
    for copy in copies[3:5]:
        copy.wait()
    for out in (even, odd):
        for ch in range(3):
            for r in range(count):
                at = 2 * wide + ch * count + r
                out[at : at + 1, :] = pos_in[ch : ch + 1, r * LANES : (r + 1) * LANES]
        at = 2 * wide + 3 * count
        for h in range(half):
            out[pl.ds(at + h, groups, stride=half), :] = code[h].astype(F32)
        out[at + count :, :] = export_in[...].astype(F32)
    for copy in copies[5:]:
        copy.wait()


def rows_kernel(rows, after, temp, kappa, even_x, odd_x, even, odd):
    side = RIM * rows
    planes = temp.shape[0] // rows
    low, high = low_and_high("cut", even_x, odd_x)
    top = (1 - is_odd("cross")) * (rows - RIM)
    for n, own in enumerate((temp, kappa)):
        for r in range(RIM):
            for out, first in ((even, top), (odd, rows - RIM - top)):
                target = n * RIM + r
                for p in range(RIM):
                    at = pl.ds(n * side + p * rows + first + r, 1)
                    out[target, p : p + 1, :] = low[at, :]
                    out[target, RIM + planes + p : RIM + planes + p + 1, :] = high[at, :]
                out[target, RIM : RIM + planes, :] = own[pl.ds(first + r, planes, stride=rows), :]


def open_kernel(
    rows, temp, kappa, source, even_x, odd_x, even_y, odd_y,
    spread_temp, spread_kappa, start, cond, along_z, minus, plus,
):
    lanes = temp.shape[1]
    x_low, x_high = low_and_high("cut", even_x, odd_x)
    y_low, y_high = low_and_high("cross", even_y, odd_y)
    side = RIM * rows
    pitch = rows + PAD
    planes = temp.shape[0] // rows
    minus[...], plus[...] = difference_matrices(lanes)
    fill(start, temp, x_low.part(slice(None, side)), x_high.part(slice(None, side)), y_low.part(slice(None, RIM)), y_high.part(slice(None, RIM)), rows, pitch, 1.0)
    fill(
        spread_kappa, kappa, x_low.part(slice(side, 2 * side)), x_high.part(slice(side, 2 * side)),
        y_low.part(slice(RIM, 2 * RIM)), y_high.part(slice(RIM, 2 * RIM)), rows, pitch, 0.5,
    )
    blocks = planes + 2 * RIM + 1
    conduct_pass(start, spread_kappa, cond, along_z, minus, plus, 0, blocks, pitch)
    mask = rim_mask(pitch, lanes)
    for at in (0, blocks - 1):
        spread_temp[at * pitch : (at + 1) * pitch, :] = jnp.zeros((pitch, lanes), F32)
    spread_temp[blocks * pitch :, :] = jnp.zeros((spread_temp.shape[0] - blocks * pitch, lanes), F32)

    def put(block, size, value):
        value = value.reshape(size, pitch, lanes) * mask[None]
        at = pl.ds(pl.multiple_of(block * pitch, 8), size * pitch)
        spread_temp[at, :] = value.reshape(size * pitch, lanes) + source[at, :]

    flow_pass(start, cond, along_z, 1, blocks - 2, pitch, 133, put)


def close_kernel(
    got, opened, kappa, source_own, even_y, odd_y,
    temp_out, looked, source, now, then, cond, along_z, minus, plus, pieces, turned, found,
):
    lanes = kappa.shape[1]
    planes, rows, _ = temp_out.shape
    pitch = rows + PAD
    total = planes + 2 * RIM
    blocks = total + 1
    minus[...], plus[...] = difference_matrices(lanes)
    wide = RIM - 1
    source[...] = source_own[...]
    now[...] = opened[...]
    low, high = low_and_high("cross", even_y, odd_y)
    for r in range(wide):
        for first, beside in ((PAD - wide + r, low), (PAD + rows + r, high)):
            at = pl.ds(first, total, stride=pitch)
            strip = beside[r, :total, :]
            source[at, :] = strip
            now[at, :] = now[at, :] + strip
    mask = rim_mask(pitch, lanes)
    conduct_pass(now, kappa, cond, along_z, minus, plus, 0, blocks, pitch)
    then[0:pitch, :] = jnp.zeros((pitch, lanes), F32)
    then[(blocks - 1) * pitch :, :] = jnp.zeros((then.shape[0] - (blocks - 1) * pitch, lanes), F32)

    def middle(block, size, value):
        at = pl.ds(pl.multiple_of(block * pitch, 8), size * pitch)
        value = (value + source[at, :]).reshape(size, pitch, lanes) * mask[None]
        then[at, :] = value.reshape(size * pitch, lanes)

    flow_pass(now, cond, along_z, 1, blocks - 2, pitch, 133, middle)
    conduct_pass(then, kappa, cond, along_z, minus, plus, 0, blocks, pitch)

    def last(block, size, value):
        at = pl.ds(pl.multiple_of(block * pitch, 8), size * pitch)
        value = (value + source[at, :]).reshape(size, pitch, lanes)[:, PAD:]
        temp_out[pl.ds(block - RIM, size)] = value
        high, low = split(value.reshape(size * rows, lanes))
        at = pl.ds(pl.multiple_of((block - RIM) * rows, rows), size * rows)
        pieces[at, :lanes] = high
        pieces[at, lanes:] = low

    flow_pass(then, cond, along_z, RIM, planes, pitch, 8, last)
    lookup(lax.axis_index("cut"), got, planes * rows, lanes, looked, pieces, turned, found)


def paired(got, block, kind, row, s):
    at = kind * (got.shape[2] // 2) + row
    first = got[block, s, pl.ds(at, 1), :]
    second = got[block, s + 1, pl.ds(at, 1), :]
    left = iota((1, LANES), 1) < LANES // 2
    return jnp.where(left, first, second), jnp.where(left, second, first)


def cell_of(number):
    return jnp.abs(number).astype(I32) - 1


def unsorted(got):
    half = got.shape[2] // 4
    lowest = jnp.minimum(got[:, :, :half, :], got[:, :, 2 * half : 3 * half, :])
    return jnp.min(lowest) < 0.0


def deposit_kernel(planes, got, source, even, odd, spread, across, plane_of):
    blocks, groups, rows_sent, _ = got.shape
    half = rows_sent // 4
    lanes = source.shape[1]
    rows = across.shape[0]
    pitch = rows + PAD
    here = lax.axis_index("cut")
    place = iota((rows, LANES), 0)
    place16 = place.astype(jnp.int16)
    zero = jnp.zeros((rows, LANES), BF16)
    pairs = groups // 2
    tile = planes // QUARTERS
    region = 2 * pairs * LANES
    inside = QUARTERS * region
    wide = RIM - 1

    def block(distance):
        return lax.rem(here + (blocks + distance), blocks)

    def fill_columns(at, number, power):
        span = pl.ds(pl.multiple_of(at, LANES), LANES)
        cell = cell_of(jnp.broadcast_to(number, (rows, LANES)))
        high, low = split(jnp.broadcast_to(power, (rows, LANES)))
        lane = (cell & (lanes - 1)).astype(jnp.int16)
        for t in range(lanes // rows):
            hit = lane == place16 + jnp.int16(t * rows)
            spread[t * rows : (t + 1) * rows, span] = jnp.where(hit, high, zero)
            spread[lanes + t * rows : lanes + (t + 1) * rows, span] = jnp.where(hit, low, zero)
        row = lax.shift_right_arithmetic(cell, 7)
        across[:, span] = jnp.where((row & (rows - 1)) == place, 1.0, 0.0).astype(BF16)
        plane_of[:, span] = lax.shift_right_arithmetic(row, rows.bit_length() - 1).astype(jnp.int16)

    def sides(pair, quarter_high, quarter_low):
        for n, (distance, kind) in enumerate(((1, 0), (0, 1), (-1, 0), (-2, 1))):
            share = quarter_high if n < 2 else quarter_low
            h, which = share // 2, share % 2
            number = paired(got, block(distance), kind, h, 2 * pair)[which]
            power = paired(got, block(distance), kind, half + h, 2 * pair)[which]
            fill_columns(inside + (n * pairs + pair) * LANES, number, power)

    def fill_pair(pair, unused):
        for part in range(2):
            for h in range(half):
                numbers = paired(got, block(-part), part, h, 2 * pair)
                powers = paired(got, block(-part), part, half + h, 2 * pair)
                for which in range(2):
                    at = (2 * h + which) * region + (part * pairs + pair) * LANES
                    fill_columns(at, numbers[which], powers[which])
        sides(pair, 0, QUARTERS - 1)
        return unused

    lax.fori_loop(0, pairs, fill_pair, 0)
    source[...] = jnp.zeros(source.shape, F32)

    def product(first, base, count, columns, added=False):
        where_y = across[:, columns]
        where_x = plane_of[:, columns] - jnp.asarray(base, I32).astype(jnp.int16)
        nothing = jnp.zeros_like(where_y)
        hot = jnp.concatenate(
            [jnp.where(where_x == jnp.int16(x), where_y, nothing) for x in range(count)], axis=0
        )
        both = lax.dot_general(
            hot, spread[:, columns], (((1,), (1,)), ((), ())), preferred_element_type=F32
        )
        value = both[:, :lanes] + both[:, lanes:]
        for n in range(count):
            at = pl.ds(pl.multiple_of((first + n + RIM) * pitch + PAD, 8), rows)
            part = value[n * rows : (n + 1) * rows]
            source[at, :] = source[at, :] + part if added else part

    for q in range(QUARTERS):
        product(q * tile, q * tile, tile, slice(q * region, (q + 1) * region))

    def outside(added):
        product(planes, 0, wide, slice(inside, inside + region), added)
        product(-wide, planes - wide, wide, slice(inside + region, inside + 2 * region), added)

    outside(False)

    @pl.when(unsorted(got))
    def _():
        def whole(m, unused):
            product(m * tile, m * tile, tile, slice(0, inside))
            return unused

        lax.fori_loop(0, QUARTERS, whole, 0)
        for step in range(1, QUARTERS):

            def others(pair, unused, step=step):
                sides(pair, step, QUARTERS - 1 - step)
                return unused

            lax.fori_loop(0, pairs, others, 0)
            outside(True)

    planes_all = planes + 2 * RIM
    top = (1 - is_odd("cross")) * (rows - wide)
    for r in range(wide):
        for out, first in ((even, top), (odd, rows - wide - top)):
            out[r, :planes_all, :] = source[pl.ds(PAD + first + r, planes_all, stride=pitch), :]


def lookup(me, got, height, lanes, looked, pieces, turned, found):
    blocks, groups, rows_sent, _ = got.shape
    half = rows_sent // 4
    pairs = groups // 2
    chunks = [[] for _ in range(QUARTERS)]
    for part in range(2):
        block = lax.rem(me + (blocks - part), blocks)
        for pair in range(pairs):
            for h in range(half):
                for which, number in enumerate(paired(got, block, part, h, 2 * pair)):
                    chunks[2 * h + which].append(cell_of(number))
    each = len(chunks[0])
    count = each * QUARTERS
    chunks = [chunk for share in chunks for chunk in share]
    chunks.append(jnp.zeros((LANES - count, LANES), I32))
    turned[...] = jnp.concatenate(chunks, axis=0).T
    lane = iota((LANES, LANES), 1)
    found[...] = jnp.zeros((LANES, LANES), F32)
    one = jnp.ones((LANES, LANES), BF16)

    def search(first, number, base, size):
        hots = []
        cells = []
        for k in range(first, first + number):
            cell = jnp.broadcast_to(turned[:, k : k + 1], (LANES, LANES))
            cells.append(cell)
            row = lax.shift_right_arithmetic(cell, 7).astype(jnp.int16)
            hots.append(
                jnp.concatenate(
                    [
                        jnp.where(
                            row == (lane + (base + r)).astype(jnp.int16), one, jnp.zeros_like(one)
                        )
                        for r in range(0, size, LANES)
                    ],
                    axis=1,
                )
            )
        both = jnp.dot(
            jnp.concatenate(hots, axis=0),
            pieces[base : base + size, :],
            preferred_element_type=F32,
        )
        value = both[:, :lanes] + both[:, lanes:]
        for n in range(number):
            picked = jnp.take_along_axis(
                value[n * LANES : (n + 1) * LANES], cells[n] & (lanes - 1), axis=1
            )
            found[...] = jnp.where(lane == first + n, picked, found[...])

    for q in range(QUARTERS):
        search(q * each, each, q * (height // QUARTERS), height // QUARTERS)

    @pl.when(unsorted(got))
    def _():
        for first in range(0, count, 4):
            search(first, 4, 0, height)

    back = found[...].T
    left = iota((1, LANES), 1) < LANES // 2
    for part in range(2):
        for pair in range(pairs):
            for h in range(half):
                n = part * pairs + pair
                a = back[2 * h * each + n : 2 * h * each + n + 1, :]
                b = back[(2 * h + 1) * each + n : (2 * h + 1) * each + n + 1, :]
                for s, value in ((0, jnp.where(left, a, b)), (1, jnp.where(left, b, a))):
                    row = (2 * pair + s) * 2 * half + part * half + h
                    for block in range(blocks):
                        at = block * groups * 2 * half + row
                        looked[at : at + 1, :] = value


def pick(tables, index, row=None):
    if row is None:
        row = lax.shift_right_logical(index, 7)
    lane = index & (LANES - 1)
    results = [jnp.zeros(index.shape, F32) for _ in tables]
    for r in range(len(tables[0])):
        here = row == r
        for ch, rows in enumerate(tables):
            value = jnp.take_along_axis(jnp.broadcast_to(rows[r], index.shape), lane, axis=1)
            results[ch] = jnp.where(here, value, results[ch])
    return results


def rows_of(ref, ch):
    return [ref[ch : ch + 1, r * LANES : (r + 1) * LANES] for r in range(ref.shape[1] // LANES)]


def stretch_kernel(
    side, half, after, pos, acted, other, gap, snapped, even_x, odd_x, base, slope, delta, hot, ghost,
):
    count = pos.shape[1] // LANES
    low_ghost, high_ghost = low_and_high("cut", even_x, odd_x)

    def ghosts(n, ref):
        places = side + 4 * count
        tables = [
            [ref[side + ch * count + r : side + ch * count + r + 1, :] for r in range(count)]
            for ch in range(4)
        ]
        index = ref[places:, :].astype(I32)
        found = pick(tables, index)
        code = found.pop().astype(I32)
        group = index // (half * LANES)
        ghost[n, 0] = group * (2 * half) + lax.shift_right_logical(code, 7)
        ghost[n, 1] = code & (LANES - 1)
        return [[f[r : r + 1] for r in range(f.shape[0])] for f in found]

    own = [rows_of(pos, ch) for ch in range(3)]
    low = ghosts(0, low_ghost)
    high = ghosts(1, high_ghost)
    first = pick(own, acted[...])
    second = pick([own[ch] + low[ch] + high[ch] for ch in range(3)], other[...])
    d = [second[ch] - first[ch] for ch in range(3)]
    dist = jnp.sqrt(d[0] * d[0] + d[1] * d[1] + d[2] * d[2])
    weight = (1.0 - snapped[...].astype(F32)) / jnp.maximum(dist, 0.3)
    base[...] = weight * (dist - gap[...])
    slope[...] = weight * (gap[...] * (0.2 * 0.5))
    for ch in range(3):
        delta[ch] = d[ch]
    place = iota((16, LANES), 0).astype(jnp.int16)
    one = jnp.ones((16, LANES), BF16)
    for r in range(acted.shape[0]):
        lane = jnp.broadcast_to(acted[r : r + 1, :] & (LANES - 1), (16, LANES)).astype(jnp.int16)
        for t in range(LANES // 16):
            hot[t * 16 : (t + 1) * 16, r * LANES : (r + 1) * LANES] = jnp.where(
                lane == place + jnp.int16(t * 16), one, jnp.zeros_like(one)
            )


def bond_kernel(
    blocks, back, code, pos, vel, acted, other, ghost, base, slope, delta, hot, pos_out, vel_out, force,
):
    half, groups, _ = code.shape
    here = lax.axis_index("cut")
    double = 2 * half

    def slots(distance):
        found = []
        for kind in range(2):
            block = lax.rem(here + (blocks + distance + kind), blocks)
            for h in range(half):
                first = block * groups * double + kind * half + h
                found.append(back[pl.ds(first, groups, stride=double), :])
        return found

    def ghosts(n, distance):
        rows = slots(distance)
        table = [rows[k][j : j + 1] for j in range(groups) for k in range(double)]
        found = pick([table], ghost[n, 1], ghost[n, 0])[0]
        return [found[r : r + 1] for r in range(found.shape[0])]

    rows = slots(0)
    temps = []
    for h in range(half):
        index = code[h]
        temp = jnp.zeros(index.shape, F32)
        for k in range(double):
            value = jnp.take_along_axis(rows[k], index & (LANES - 1), axis=1)
            temp = jnp.where(lax.shift_right_logical(index, 7) == k, value, temp)
        temps.append(temp)
    own = [temps[h][j : j + 1] for j in range(groups) for h in range(half)]
    first = pick([own], acted[...])[0]
    second = pick([own + ghosts(0, -1) + ghosts(1, 1)], other[...])[0]
    scale = base[...] - slope[...] * (first + second)
    values = [split(scale * delta[ch]) for ch in range(3)]
    values = [piece.astype(F32) for pair in values for piece in pair]
    high_count = len(own)
    high_place = iota((high_count, LANES), 0)
    for r in range(acted.shape[0]):
        span = slice(r * LANES, (r + 1) * LANES)
        at_row = lax.shift_right_logical(acted[r : r + 1, :], 7) == high_place
        for n, value in enumerate(values):
            force[n * high_count : (n + 1) * high_count, span] = jnp.where(
                at_row, jnp.broadcast_to(value[r : r + 1], (high_count, LANES)), 0.0
            ).astype(BF16)
    total = lax.dot_general(
        force[...], hot[...], (((1,), (1,)), ((), ())), preferred_element_type=F32
    )
    for ch in range(3):
        base_row = 2 * ch * high_count
        summed = (
            total[base_row : base_row + high_count]
            + total[base_row + high_count : base_row + 2 * high_count]
        )
        for r in range(high_count):
            span = slice(r * LANES, (r + 1) * LANES)
            velocity = vel[ch : ch + 1, span] + 0.5 * summed[r : r + 1]
            vel_out[ch : ch + 1, span] = velocity
            pos_out[ch : ch + 1, span] = pos[ch : ch + 1, span] + 0.5 * velocity


def swaps(axis, closed, even, odd):
    count = lax.axis_size(axis)
    results = []
    for first, block in ((0, even), (1, odd)):
        pairs = []
        for i in range(first, count if closed else count - 1, 2):
            pairs += [(i, (i + 1) % count), ((i + 1) % count, i)]
        results.append(lax.ppermute(block, axis, pairs))
    return results


def per_device(
    warming_above_ambient,
    fourier_stability_factor,
    patch_locator,
    photon_gain_wattage,
    on_skin_marker,
    grain_placements,
    grain_motion_parts,
    tether_acted_grain,
    tether_other_grain,
    tether_relaxed_gap,
    snapped_marker,
    exported_copies,
):
    planes, rows, lanes = warming_above_ambient.shape
    temp = warming_above_ambient.reshape(planes * rows, lanes)
    kappa = fourier_stability_factor.reshape(planes * rows, lanes)
    blocks = lax.axis_size("cut")
    groups = lax.axis_size("cross")
    count = patch_locator.shape[0]
    half = count // groups // LANES
    pitch = rows + PAD
    total = planes + 2 * RIM
    flat = jax.ShapeDtypeStruct(((total + 2) * pitch, lanes), F32)
    wide = RIM * rows

    exports = exported_copies.shape[0] // LANES
    carried = jax.ShapeDtypeStruct((2 * wide + 4 * (count // LANES) + exports, LANES), F32)
    devices = blocks * groups
    sent, even_x, odd_x, code = call(
        parcel_kernel,
        [
            jax.ShapeDtypeStruct((devices * 4 * half, LANES), F32),
            carried,
            carried,
            jax.ShapeDtypeStruct((half, groups, LANES), I32),
        ],
        [
            temp,
            kappa,
            patch_locator.reshape(-1, LANES),
            photon_gain_wattage.reshape(-1, LANES),
            on_skin_marker.reshape(-1, LANES),
            grain_placements,
            exported_copies.reshape(-1, LANES),
        ],
        [
            pltpu.VMEM((count // LANES, LANES), I32),
            pltpu.VMEM((count // LANES, LANES), F32),
            pltpu.VMEM((count // LANES, LANES), I32),
            pltpu.VMEM(grain_placements.shape, F32),
            pltpu.VMEM((exports, LANES), I32),
            pltpu.SemaphoreType.DMA((9,)),
        ],
        left=7,
        limit=None,
    )

    def exchange(sent):
        sent = sent.reshape(devices, -1, LANES)
        return lax.all_to_all(sent, BOTH, split_axis=0, concat_axis=0, tiled=True)

    got = exchange(sent).reshape(blocks, groups, 4 * half, LANES)
    even_x, odd_x = swaps("cut", True, even_x, odd_x)

    across = jax.ShapeDtypeStruct((2 * RIM, -(-total // 8) * 8, lanes), F32)
    even_y, odd_y = call(
        functools.partial(rows_kernel, rows),
        [across, across],
        [got, temp, kappa, even_x, odd_x],
        left=1,
    )
    even_y, odd_y = swaps("cross", False, even_y, odd_y)

    strips = jax.ShapeDtypeStruct((RIM - 1,) + across.shape[1:], F32)
    entries = 2 * count + 4 * count // QUARTERS
    source, even_s, odd_s = call(
        functools.partial(deposit_kernel, planes),
        [flat, strips, strips],
        [got],
        [
            pltpu.VMEM((2 * lanes, entries), BF16),
            pltpu.VMEM((rows, entries), BF16),
            pltpu.VMEM((rows, entries), jnp.int16),
        ],
    )
    even_s, odd_s = swaps("cross", False, even_s, odd_s)

    grid = pltpu.VMEM(flat.shape, F32)
    matrix = pltpu.VMEM((2 * lanes, 2 * lanes), BF16)
    opened, kappa = call(
        functools.partial(open_kernel, rows),
        [flat, flat],
        [temp, kappa, source, even_x, odd_x, even_y, odd_y],
        [grid, grid, grid, matrix, matrix],
    )
    temp, looked = call(
        close_kernel,
        [
            jax.ShapeDtypeStruct((planes, rows, lanes), F32),
            jax.ShapeDtypeStruct((devices * 2 * half, LANES), F32),
        ],
        [got, opened, kappa, source, even_s, odd_s],
        [
            grid, grid, grid, grid, grid, matrix, matrix,
            pltpu.VMEM((planes * rows, 2 * lanes), BF16),
            pltpu.VMEM((LANES, LANES), I32),
            pltpu.VMEM((LANES, LANES), F32),
        ],
    )
    back = exchange(looked).reshape(looked.shape)
    acted = tether_acted_grain.reshape(-1, LANES)
    other = tether_other_grain.reshape(-1, LANES)
    entry = jax.ShapeDtypeStruct(acted.shape, F32)
    base, slope, delta, hot, ghost = call(
        functools.partial(stretch_kernel, 2 * wide, half),
        [
            entry,
            entry,
            jax.ShapeDtypeStruct((3,) + acted.shape, F32),
            jax.ShapeDtypeStruct((LANES, acted.size), BF16),
            jax.ShapeDtypeStruct((2, 2, exports, LANES), I32),
        ],
        [
            looked,
            grain_placements,
            acted,
            other,
            tether_relaxed_gap.reshape(-1, LANES),
            snapped_marker.reshape(-1, LANES),
            even_x,
            odd_x,
        ],
        left=1,
    )
    out = jax.ShapeDtypeStruct(grain_placements.shape, F32)
    positions_new, velocities_new = call(
        functools.partial(bond_kernel, blocks),
        [out, out],
        [
            back, code, grain_placements, grain_motion_parts, acted, other, ghost,
            base, slope, delta, hot,
        ],
        [pltpu.VMEM((6 * (count // LANES), acted.size), BF16)],
    )
    return (temp, positions_new, velocities_new)


def solution(mesh):
    return jax.shard_map(
        per_device,
        mesh=mesh,
        in_specs=(
            P("cut", "cross", None),
            P("cut", "cross", None),
            P(("cut", "cross")),
            P(("cut", "cross")),
            P(("cut", "cross")),
            P(None, ("cut", "cross")),
            P(None, ("cut", "cross")),
            P(("cut", "cross")),
            P(("cut", "cross")),
            P(("cut", "cross")),
            P(("cut", "cross")),
            P(("cut", "cross")),
        ),
        out_specs=(P("cut", "cross", None), P(None, ("cut", "cross")), P(None, ("cut", "cross"))),
        check_vma=False,
    )
```

```python
import functools

import jax
import jax.numpy as jnp
from jax import lax
from jax.experimental import pallas as pl
from jax.experimental.pallas import tpu as pltpu
from jax.sharding import PartitionSpec as P

F32 = jnp.float32
BF16 = jnp.bfloat16
I32 = jnp.int32
LANES = 128
BOTH = ("cut", "cross")
VMEM = pl.BlockSpec(memory_space=pltpu.VMEM)
LIMIT = 32 * 1024 * 1024


def call(kernel, outs, operands, scratch=(), left=0, limit=LIMIT, outs_left=0):
    return pl.pallas_call(
        kernel,
        out_shape=outs,
        in_specs=[pl.BlockSpec(memory_space=pltpu.HBM)] * left + [VMEM] * (len(operands) - left),
        out_specs=[pl.BlockSpec(memory_space=pltpu.HBM)] * outs_left + [VMEM] * (len(outs) - outs_left),
        scratch_shapes=list(scratch),
        compiler_params=pltpu.CompilerParams(vmem_limit_bytes=limit),
    )(*operands)


class Either:
    def __init__(self, flag, yes, no):
        self.flag, self.yes, self.no = flag, yes, no
        self.shape = yes.shape

    def __getitem__(self, index):
        yes, no = self.yes[index], self.no[index]
        return jnp.where(jnp.full(yes.shape, self.flag, I32) > 0, yes, no)

    def part(self, index):
        return Either(self.flag, self.yes.at[index], self.no.at[index])


def is_odd(axis):
    return lax.rem(lax.axis_index(axis), 2)


def low_and_high(axis, even, odd):
    flag = is_odd(axis)
    return Either(flag, even, odd), Either(flag, odd, even)


def split(value):
    high = value.astype(BF16)
    return high, (value - high.astype(F32)).astype(BF16)


def iota(shape, dim):
    return lax.broadcasted_iota(I32, shape, dim)


RIM = 3
PAD = 8
QUARTERS = 4


def groups_of(count, most):
    return max(n for n in range(1, most + 1) if count % n == 0)


def difference_matrices(lanes):
    shape = (2 * lanes, 2 * lanes)
    given = iota(shape, 0) & (lanes - 1)
    wanted = iota(shape, 1)
    lower = wanted >= lanes
    wanted = wanted & (lanes - 1)
    beside = jnp.where(lower, wanted - 1, wanted + 1)
    neighbour = jnp.where(given == beside, 1.0, 0.0)
    same = jnp.where(given == wanted, 1.0, 0.0)
    return (neighbour - same).astype(BF16), (neighbour + same).astype(BF16)


def pieces_of(value):
    high, low = split(value)
    return jnp.concatenate([high, low], axis=1)


def conduct_pass(temp, kappa, cond, along_z, minus, plus, first, blocks, pitch):
    lanes = temp.shape[1]
    size = groups_of(blocks, 135)

    def body(n, unused):
        at = pl.ds(pl.multiple_of((first + n * size) * pitch, 8), size * pitch)
        t = temp[at, :]
        c = kappa[at, :] * (0.5 + 1.0 / (1.0 + t * t))
        cond[at, :] = c
        change = jnp.dot(pieces_of(t), minus[...], preferred_element_type=F32)
        both = jnp.dot(pieces_of(c), plus[...], preferred_element_type=F32)
        along_z[at, :] = change[:, :lanes] * both[:, :lanes] + change[:, lanes:] * both[:, lanes:]
        return unused

    lax.fori_loop(0, blocks // size, body, 0)


def flow_pass(temp, cond, along_z, first, blocks, pitch, most, put):
    size = groups_of(blocks, most)

    def rows_at(ref, base):
        return ref[pl.ds(base, pitch), :]

    def body(n, carried):
        t, c, flux = carried
        for k in range(size):
            block = first + n * size + k
            base = pl.multiple_of(block * pitch, 8)
            t_next = rows_at(temp, base + pitch)
            c_next = rows_at(cond, base + pitch)
            onward = (c + c_next) * (t_next - t)
            net = rows_at(along_z, base) + (onward - flux)
            for shift in (1, -1):
                net = net + (c + rows_at(cond, base + shift)) * (rows_at(temp, base + shift) - t)
            put(block, t + net)
            t, c, flux = t_next, c_next, onward
        return t, c, flux

    base = first * pitch
    t, c = rows_at(temp, base), rows_at(cond, base)
    flux = (c + rows_at(cond, base - pitch)) * (t - rows_at(temp, base - pitch))
    lax.fori_loop(0, blocks // size, body, (t, c, flux))


def rim_mask(pitch, lanes):
    place = iota((pitch, lanes), 0)
    side = lax.axis_index("cross")
    below = jnp.where(side > 0, 1.0, 0.0)
    above = jnp.where(side < lax.axis_size("cross") - 1, 1.0, 0.0)
    return jnp.where(place < PAD - RIM, above, jnp.where(place < PAD, below, 1.0))


def fill(flat, own, x_low, x_high, y_low, y_high, corner_low, corner_high, rows, scale):
    pitch = rows + PAD
    planes = own.shape[0] // rows
    flat[...] = jnp.zeros(flat.shape, F32)

    def place(p, part):
        flat[pl.ds(pl.multiple_of(p * pitch + PAD, 8), rows), :] = part * scale

    for n in range(RIM):
        place(n, x_low[n * rows : (n + 1) * rows, :])
        place(RIM + planes + n, x_high[n * rows : (n + 1) * rows, :])

    def body(p, unused):
        place(p + RIM, own[pl.ds(pl.multiple_of(p * rows, 8), rows), :])
        return unused

    lax.fori_loop(0, planes, body, 0, unroll=8)
    for r in range(RIM):
        below = PAD - RIM + r
        flat[pl.ds(RIM * pitch + below, planes, stride=pitch), :] = y_low[r, :, :] * scale
        flat[pl.ds((RIM + 1) * pitch + r, planes, stride=pitch), :] = y_high[r, :, :] * scale
        for n in range(2 * RIM):
            p = n if n < RIM else n + planes
            flat[p * pitch + below : p * pitch + below + 1, :] = corner_low[r, n : n + 1, :] * scale
            flat[(p + 1) * pitch + r : (p + 1) * pitch + r + 1, :] = corner_high[r, n : n + 1, :] * scale


def parcel_kernel(
    temp, kappa, cells, watts, marks, pos, export, sent, even, odd, code,
    cell_in, watt_in, mark_in, pos_in, export_in, sems,
):
    count = pos.shape[1] // LANES
    exports = export.shape[0]
    wide = (even.shape[0] - 4 * count - exports) // 2
    height, lanes = temp.shape
    patch = height * lanes
    half, groups, _ = code.shape
    cap = half * LANES
    quarter = cap // QUARTERS
    moves = [(cells, cell_in), (watts, watt_in), (marks, mark_in), (pos, pos_in), (export, export_in)]
    tail = (1 - is_odd("cut")) * (height - wide)
    for n, field in enumerate((temp, kappa)):
        target = pl.ds(n * wide, wide)
        for out, start in ((even, tail), (odd, height - wide - tail)):
            moves.append((field.at[pl.ds(pl.multiple_of(start, 16), wide)], out.at[target]))
    copies = [pltpu.make_async_copy(*move, sems.at[n]) for n, move in enumerate(moves)]
    for copy in copies:
        copy.start()
    for copy in copies[:3]:
        copy.wait()

    def by_group(ref):
        return jnp.concatenate([ref[pl.ds(h, groups, stride=half), :] for h in range(half)], axis=1)

    cell = by_group(cell_in)
    power = by_group(mark_in).astype(F32) * by_group(watt_in) * 0.5
    upper = cell >= patch
    cell = jnp.where(upper, cell - patch, cell)
    share = cell // (patch // QUARTERS)
    kind = jnp.where(upper, share + QUARTERS, share)
    members = [jnp.where(kind == k, 1.0, 0.0) for k in range(2 * QUARTERS)]
    earlier = jnp.where(iota((cap, cap), 0) < iota((cap, cap), 1), 1.0, 0.0).astype(BF16)
    before = jnp.dot(
        jnp.concatenate(members, axis=0).astype(BF16), earlier, preferred_element_type=F32
    )
    rank = jnp.zeros((groups, cap), F32)
    most = jnp.zeros((groups, 1), F32)
    for k, member in enumerate(members):
        ahead = before[k * groups : (k + 1) * groups]
        rank = rank + member * ahead
        most = jnp.maximum(most, ahead[:, cap - 1 :] + member[:, cap - 1 :])
    fits = jnp.broadcast_to(most, (groups, cap)) <= quarter
    region = share ^ is_odd("cross")
    slot = jnp.where(fits, region * quarter + rank.astype(I32), iota((groups, cap), 1))
    mark = jnp.where(upper, slot + cap, slot)
    for h in range(half):
        code[h] = mark[:, h * LANES : (h + 1) * LANES]
    number = cell + 1
    digits = [number & 255, lax.shift_right_logical(number, 8) & 255, lax.shift_right_logical(number, 16)]
    digits = [d.astype(F32) for d in digits]
    top = power.astype(BF16).astype(F32)
    middle = (power - top).astype(BF16).astype(F32)
    digits += [top, middle, power - top - middle]
    stacked = [jnp.where(upper, 0.0, d) for d in digits] + [jnp.where(upper, d, 0.0) for d in digits]
    stacked = jnp.concatenate(stacked, axis=0).astype(BF16)
    place = iota((16, cap), 0).astype(jnp.int16)
    one = jnp.ones((16, cap), BF16)
    of_group = iota((stacked.shape[0], cap), 0) & (groups - 1)
    moved = jnp.zeros(stacked.shape, F32)
    for j in range(groups):
        goes = jnp.broadcast_to(slot[j : j + 1], (16, cap)).astype(jnp.int16)
        swap = jnp.concatenate(
            [
                jnp.where(goes == place + jnp.int16(t * 16), one, jnp.zeros_like(one))
                for t in range(cap // 16)
            ],
            axis=0,
        )
        result = lax.dot_general(
            stacked, swap, (((1,), (1,)), ((), ())), preferred_element_type=F32
        )
        moved = jnp.where(of_group == j, result, moved)
    sign = jnp.where(fits, 1.0, -1.0)
    blocks = sent.shape[0] // (groups * 4 * half)
    for kind in range(2):
        part = [
            moved[(6 * kind + n) * groups : (6 * kind + n + 1) * groups] for n in range(6)
        ]
        numbers = (part[0] + 256.0 * part[1] + 65536.0 * part[2]) * sign
        powers = part[3] + part[4] + part[5]
        for n, value in enumerate((numbers, powers)):
            for h in range(half):
                row = kind * 2 * half + n * half + h
                for block in range(blocks):
                    at = pl.ds(block * groups * 4 * half + row, groups, stride=4 * half)
                    sent[at, :] = value[:, h * LANES : (h + 1) * LANES]
    for copy in copies[3:5]:
        copy.wait()
    for out in (even, odd):
        for ch in range(3):
            for r in range(count):
                at = 2 * wide + ch * count + r
                out[at : at + 1, :] = pos_in[ch : ch + 1, r * LANES : (r + 1) * LANES]
        at = 2 * wide + 3 * count
        for h in range(half):
            out[pl.ds(at + h, groups, stride=half), :] = code[h].astype(F32)
        out[at + count :, :] = export_in[...].astype(F32)
    for copy in copies[5:]:
        copy.wait()


def rows_kernel(rows, after, temp, kappa, even, odd):
    planes = temp.shape[0] // rows
    top = (1 - is_odd("cross")) * (rows - RIM)
    for n, own in enumerate((temp, kappa)):
        for r in range(RIM):
            for out, first in ((even, top), (odd, rows - RIM - top)):
                out[n * RIM + r] = own[pl.ds(first + r, planes, stride=rows), :]


def corner_kernel(rows, even_s, odd_s, even_x, odd_x, even, odd):
    side = RIM * rows
    low, high = low_and_high("cut", even_x, odd_x)
    top = (1 - is_odd("cross")) * (rows - RIM)
    base = even_s.shape[0]
    for out, strips, first in ((even, even_s, top), (odd, odd_s, rows - RIM - top)):
        out[:base, :] = strips[...]
        for n in range(2 * RIM):
            for p in range(RIM):
                at = pl.ds(n // RIM * side + p * rows + first + n % RIM, 1)
                to = base + n * PAD + p
                out[to : to + 1, :] = low[at, :]
                out[to + RIM : to + RIM + 1, :] = high[at, :]
            out[base + n * PAD + 2 * RIM : base + (n + 1) * PAD, :] = jnp.zeros((PAD - 2 * RIM, LANES), F32)


class Rows:
    def __init__(self, ref, base, size):
        self.ref, self.base, self.size = ref, base, size

    def __getitem__(self, index):
        r, at, lanes = index
        first = self.base + r * self.size
        return self.ref[first + (at.start or 0) : first + (self.size if at.stop is None else at.stop), :]


def heat_kernel(
    got, temp, kappa_own, source_own, even_x, odd_x, even_y, odd_y, even_s, odd_s,
    temp_out, looked, source, kappa, now, then, cond, along_z, minus, plus, pieces, result, sem,
):
    lanes = temp.shape[1]
    planes, rows, _ = result.shape
    pitch = rows + PAD
    total = planes + 2 * RIM
    blocks = total + 1
    side = RIM * rows
    wide = RIM - 1
    x_low, x_high = low_and_high("cut", even_x, odd_x)
    y_low, y_high = low_and_high("cross", even_y, odd_y)
    s_low, s_high = low_and_high("cross", even_s, odd_s)
    height = -(-total // 8) * 8
    minus[...], plus[...] = difference_matrices(lanes)
    for n, (flat, own, scale) in enumerate(((now, temp, 1.0), (kappa, kappa_own, 0.5))):
        beside = [half.part(slice(n * side, (n + 1) * side)) for half in (x_low, x_high)]
        strips = [half.part(slice(n * RIM, (n + 1) * RIM)) for half in (y_low, y_high)]
        corners = [Rows(half, wide * height + n * RIM * PAD, PAD) for half in (s_low, s_high)]
        fill(flat, own, *beside, *strips, *corners, rows, scale)
    source[...] = source_own[...]
    for first, half in ((PAD - wide, s_low), (PAD + rows, s_high)):
        strips = Rows(half, 0, height)
        for r in range(wide):
            source[pl.ds(first + r, total, stride=pitch), :] = strips[r, :total, :]
    mask = rim_mask(pitch, lanes)
    conduct_pass(now, kappa, cond, along_z, minus, plus, 0, blocks, pitch)
    then[0:pitch, :] = jnp.zeros((pitch, lanes), F32)
    then[(blocks - 1) * pitch :, :] = jnp.zeros((then.shape[0] - (blocks - 1) * pitch, lanes), F32)

    def opening(block, value):
        at = pl.ds(pl.multiple_of(block * pitch, 8), pitch)
        then[at, :] = (value + source[at, :]) * mask

    flow_pass(now, cond, along_z, 1, blocks - 2, pitch, 1000, opening)
    now[0:pitch, :] = jnp.zeros((pitch, lanes), F32)
    now[(blocks - 1) * pitch :, :] = jnp.zeros((now.shape[0] - (blocks - 1) * pitch, lanes), F32)
    conduct_pass(then, kappa, cond, along_z, minus, plus, 0, blocks, pitch)

    def middle(block, value):
        at = pl.ds(pl.multiple_of(block * pitch, 8), pitch)
        now[at, :] = (value + source[at, :]) * mask

    flow_pass(then, cond, along_z, 1, blocks - 2, pitch, 1000, middle)
    conduct_pass(now, kappa, cond, along_z, minus, plus, 0, blocks, pitch)

    def last(block, value):
        at = pl.ds(pl.multiple_of(block * pitch, 8), pitch)
        result[block - RIM] = (value + source[at, :])[PAD:]

    flow_pass(now, cond, along_z, RIM, planes, pitch, 1000, last)
    copy = pltpu.make_async_copy(result, temp_out, sem)
    copy.start()
    height = planes * rows
    for first in range(0, planes, lanes // rows):
        turned = result[first : first + lanes // rows].reshape(lanes, lanes).T
        high, low = split(turned)
        pieces[:lanes, first * rows : first * rows + lanes] = high
        pieces[lanes:, first * rows : first * rows + lanes] = low
    lookup(lax.axis_index("cut"), got, height, lanes, rows, looked, pieces)
    copy.wait()


def paired(got, block, kind, row, s):
    at = kind * (got.shape[2] // 2) + row
    first = got[block, s, pl.ds(at, 1), :]
    second = got[block, s + 1, pl.ds(at, 1), :]
    left = iota((1, LANES), 1) < LANES // 2
    return jnp.where(left, first, second), jnp.where(left, second, first)


def cell_of(number):
    return jnp.abs(number).astype(I32) - 1


def unsorted(got):
    half = got.shape[2] // 4
    lowest = jnp.minimum(got[:, :, :half, :], got[:, :, 2 * half : 3 * half, :])
    return jnp.min(lowest) < 0.0


def deposit_kernel(planes, got, source, even, odd, spread, across, plane_of):
    blocks, groups, rows_sent, _ = got.shape
    half = rows_sent // 4
    lanes = source.shape[1]
    rows = across.shape[0]
    pitch = rows + PAD
    here = lax.axis_index("cut")
    place = iota((rows, LANES), 0)
    place16 = place.astype(jnp.int16)
    zero = jnp.zeros((rows, LANES), BF16)
    pairs = groups // 2
    tile = planes // QUARTERS
    region = 2 * pairs * LANES
    inside = QUARTERS * region
    wide = RIM - 1

    def block(distance):
        return lax.rem(here + (blocks + distance), blocks)

    def fill_columns(at, number, power):
        span = pl.ds(pl.multiple_of(at, LANES), LANES)
        cell = cell_of(jnp.broadcast_to(number, (rows, LANES)))
        high, low = split(jnp.broadcast_to(power, (rows, LANES)))
        lane = (cell & (lanes - 1)).astype(jnp.int16)
        for t in range(lanes // rows):
            hit = lane == place16 + jnp.int16(t * rows)
            spread[t * rows : (t + 1) * rows, span] = jnp.where(hit, high, zero)
            spread[lanes + t * rows : lanes + (t + 1) * rows, span] = jnp.where(hit, low, zero)
        row = lax.shift_right_arithmetic(cell, 7)
        across[:, span] = jnp.where((row & (rows - 1)) == place, 1.0, 0.0).astype(BF16)
        plane_of[:, span] = lax.shift_right_arithmetic(row, rows.bit_length() - 1).astype(jnp.int16)

    def sides(pair, quarter_high, quarter_low):
        for n, (distance, kind) in enumerate(((1, 0), (0, 1), (-1, 0), (-2, 1))):
            share = quarter_high if n < 2 else quarter_low
            h, which = share // 2, share % 2
            number = paired(got, block(distance), kind, h, 2 * pair)[which]
            power = paired(got, block(distance), kind, half + h, 2 * pair)[which]
            fill_columns(inside + (n * pairs + pair) * LANES, number, power)

    def fill_pair(pair, unused):
        for part in range(2):
            for h in range(half):
                numbers = paired(got, block(-part), part, h, 2 * pair)
                powers = paired(got, block(-part), part, half + h, 2 * pair)
                for which in range(2):
                    at = (2 * h + which) * region + (part * pairs + pair) * LANES
                    fill_columns(at, numbers[which], powers[which])
        sides(pair, 0, QUARTERS - 1)
        return unused

    lax.fori_loop(0, pairs, fill_pair, 0)
    source[...] = jnp.zeros(source.shape, F32)

    def product(first, base, count, columns, added=False):
        where_y = across[:, columns]
        where_x = plane_of[:, columns] - jnp.asarray(base, I32).astype(jnp.int16)
        nothing = jnp.zeros_like(where_y)
        hot = jnp.concatenate(
            [jnp.where(where_x == jnp.int16(x), where_y, nothing) for x in range(count)], axis=0
        )
        both = lax.dot_general(
            hot, spread[:, columns], (((1,), (1,)), ((), ())), preferred_element_type=F32
        )
        value = both[:, :lanes] + both[:, lanes:]
        for n in range(count):
            at = pl.ds(pl.multiple_of((first + n + RIM) * pitch + PAD, 8), rows)
            part = value[n * rows : (n + 1) * rows]
            source[at, :] = source[at, :] + part if added else part

    for q in range(QUARTERS):
        product(q * tile, q * tile, tile, slice(q * region, (q + 1) * region))

    def outside(added):
        product(planes, 0, wide, slice(inside, inside + region), added)
        product(-wide, planes - wide, wide, slice(inside + region, inside + 2 * region), added)

    outside(False)

    @pl.when(unsorted(got))
    def _():
        def whole(m, unused):
            product(m * tile, m * tile, tile, slice(0, inside))
            return unused

        lax.fori_loop(0, QUARTERS, whole, 0)
        for step in range(1, QUARTERS):

            def others(pair, unused, step=step):
                sides(pair, step, QUARTERS - 1 - step)
                return unused

            lax.fori_loop(0, pairs, others, 0)
            outside(True)

    planes_all = planes + 2 * RIM
    top = (1 - is_odd("cross")) * (rows - wide)
    for r in range(wide):
        for out, first in ((even, top), (odd, rows - wide - top)):
            at = r * (out.shape[0] // wide)
            out[at : at + planes_all, :] = source[pl.ds(PAD + first + r, planes_all, stride=pitch), :]


def lookup(me, got, height, lanes, rows, looked, pieces):
    blocks, groups, rows_sent, _ = got.shape
    half = rows_sent // 4
    pairs = groups // 2
    shift = rows.bit_length() - 1
    place = iota((rows, LANES), 0)
    lane_place = iota((lanes, LANES), 0)
    zero = jnp.zeros((rows, LANES), BF16)

    def search(numbers, base, size):
        hots = []
        for number in numbers:
            row = lax.shift_right_arithmetic(cell_of(jnp.broadcast_to(number, (rows, LANES))), 7)
            plane = lax.shift_right_arithmetic(row, shift).astype(jnp.int16)
            hot_row = jnp.where((row & (rows - 1)) == place, 1.0, 0.0).astype(BF16)
            hots.append(
                jnp.concatenate(
                    [
                        jnp.where(plane == jnp.int16(x), hot_row, zero)
                        for x in range(base // rows, (base + size) // rows)
                    ],
                    axis=0,
                )
            )
        both = jnp.dot(
            pieces[:, base : base + size],
            jnp.concatenate(hots, axis=1),
            preferred_element_type=F32,
        )
        value = both[:lanes] + both[lanes:]
        results = []
        for n, number in enumerate(numbers):
            lane = cell_of(jnp.broadcast_to(number, (lanes, LANES))) & (lanes - 1)
            part = jnp.where(lane == lane_place, value[:, n * LANES : (n + 1) * LANES], 0.0)
            results.append(jnp.sum(part, axis=0, keepdims=True))
        return results

    left = iota((1, LANES), 1) < LANES // 2

    def run(full):
        for h in range(half):
            found = []
            for which in range(2):
                numbers = []
                for part in range(2):
                    block = lax.rem(me + (blocks - part), blocks)
                    for pair in range(pairs):
                        numbers.append(paired(got, block, part, h, 2 * pair)[which])
                size = height // QUARTERS
                found.append(
                    search(numbers, 0, height) if full else search(numbers, (2 * h + which) * size, size)
                )
            for part in range(2):
                for pair in range(pairs):
                    a, b = (f[part * pairs + pair] for f in found)
                    for s, value in ((0, jnp.where(left, a, b)), (1, jnp.where(left, b, a))):
                        row = (2 * pair + s) * 2 * half + part * half + h
                        for block in range(blocks):
                            at = block * groups * 2 * half + row
                            looked[at : at + 1, :] = value

    run(False)

    @pl.when(unsorted(got))
    def _():
        run(True)


def pick(tables, index, row=None):
    if row is None:
        row = lax.shift_right_logical(index, 7)
    lane = index & (LANES - 1)
    results = [jnp.zeros(index.shape, F32) for _ in tables]
    for r in range(len(tables[0])):
        here = row == r
        for ch, rows in enumerate(tables):
            value = jnp.take_along_axis(jnp.broadcast_to(rows[r], index.shape), lane, axis=1)
            results[ch] = jnp.where(here, value, results[ch])
    return results


def rows_of(ref, ch):
    return [ref[ch : ch + 1, r * LANES : (r + 1) * LANES] for r in range(ref.shape[1] // LANES)]


def stretch_kernel(
    side, half, after, pos, acted, other, gap, snapped, even_x, odd_x, base, slope, delta, hot, ghost,
):
    count = pos.shape[1] // LANES
    low_ghost, high_ghost = low_and_high("cut", even_x, odd_x)

    def ghosts(n, ref):
        places = side + 4 * count
        tables = [
            [ref[side + ch * count + r : side + ch * count + r + 1, :] for r in range(count)]
            for ch in range(4)
        ]
        index = ref[places:, :].astype(I32)
        found = pick(tables, index)
        code = found.pop().astype(I32)
        group = index // (half * LANES)
        ghost[n, 0] = group * (2 * half) + lax.shift_right_logical(code, 7)
        ghost[n, 1] = code & (LANES - 1)
        return [[f[r : r + 1] for r in range(f.shape[0])] for f in found]

    own = [rows_of(pos, ch) for ch in range(3)]
    low = ghosts(0, low_ghost)
    high = ghosts(1, high_ghost)
    first = pick(own, acted[...])
    second = pick([own[ch] + low[ch] + high[ch] for ch in range(3)], other[...])
    d = [second[ch] - first[ch] for ch in range(3)]
    dist = jnp.sqrt(d[0] * d[0] + d[1] * d[1] + d[2] * d[2])
    weight = (1.0 - snapped[...].astype(F32)) / jnp.maximum(dist, 0.3)
    base[...] = weight * (dist - gap[...])
    slope[...] = weight * (gap[...] * (0.2 * 0.5))
    for ch in range(3):
        delta[ch] = d[ch]
    place = iota((16, LANES), 0).astype(jnp.int16)
    one = jnp.ones((16, LANES), BF16)
    for r in range(acted.shape[0]):
        lane = jnp.broadcast_to(acted[r : r + 1, :] & (LANES - 1), (16, LANES)).astype(jnp.int16)
        for t in range(LANES // 16):
            hot[t * 16 : (t + 1) * 16, r * LANES : (r + 1) * LANES] = jnp.where(
                lane == place + jnp.int16(t * 16), one, jnp.zeros_like(one)
            )


def bond_kernel(
    blocks, back, code, pos, vel, acted, other, ghost, base, slope, delta, hot, pos_out, vel_out, force,
):
    half, groups, _ = code.shape
    here = lax.axis_index("cut")
    double = 2 * half

    def slots(distance):
        found = []
        for kind in range(2):
            block = lax.rem(here + (blocks + distance + kind), blocks)
            for h in range(half):
                first = block * groups * double + kind * half + h
                found.append(back[pl.ds(first, groups, stride=double), :])
        return found

    def ghosts(n, distance):
        rows = slots(distance)
        table = [rows[k][j : j + 1] for j in range(groups) for k in range(double)]
        found = pick([table], ghost[n, 1], ghost[n, 0])[0]
        return [found[r : r + 1] for r in range(found.shape[0])]

    rows = slots(0)
    temps = []
    for h in range(half):
        index = code[h]
        temp = jnp.zeros(index.shape, F32)
        for k in range(double):
            value = jnp.take_along_axis(rows[k], index & (LANES - 1), axis=1)
            temp = jnp.where(lax.shift_right_logical(index, 7) == k, value, temp)
        temps.append(temp)
    own = [temps[h][j : j + 1] for j in range(groups) for h in range(half)]
    first = pick([own], acted[...])[0]
    second = pick([own + ghosts(0, -1) + ghosts(1, 1)], other[...])[0]
    scale = base[...] - slope[...] * (first + second)
    values = [split(scale * delta[ch]) for ch in range(3)]
    values = [piece.astype(F32) for pair in values for piece in pair]
    high_count = len(own)
    high_place = iota((high_count, LANES), 0)
    for r in range(acted.shape[0]):
        span = slice(r * LANES, (r + 1) * LANES)
        at_row = lax.shift_right_logical(acted[r : r + 1, :], 7) == high_place
        for n, value in enumerate(values):
            force[n * high_count : (n + 1) * high_count, span] = jnp.where(
                at_row, jnp.broadcast_to(value[r : r + 1], (high_count, LANES)), 0.0
            ).astype(BF16)
    total = lax.dot_general(
        force[...], hot[...], (((1,), (1,)), ((), ())), preferred_element_type=F32
    )
    for ch in range(3):
        base_row = 2 * ch * high_count
        summed = (
            total[base_row : base_row + high_count]
            + total[base_row + high_count : base_row + 2 * high_count]
        )
        for r in range(high_count):
            span = slice(r * LANES, (r + 1) * LANES)
            velocity = vel[ch : ch + 1, span] + 0.5 * summed[r : r + 1]
            vel_out[ch : ch + 1, span] = velocity
            pos_out[ch : ch + 1, span] = pos[ch : ch + 1, span] + 0.5 * velocity


def swaps(axis, closed, even, odd):
    count = lax.axis_size(axis)
    results = []
    for first, block in ((0, even), (1, odd)):
        pairs = []
        for i in range(first, count if closed else count - 1, 2):
            pairs += [(i, (i + 1) % count), ((i + 1) % count, i)]
        results.append(lax.ppermute(block, axis, pairs))
    return results


def per_device(
    warming_above_ambient,
    fourier_stability_factor,
    patch_locator,
    photon_gain_wattage,
    on_skin_marker,
    grain_placements,
    grain_motion_parts,
    tether_acted_grain,
    tether_other_grain,
    tether_relaxed_gap,
    snapped_marker,
    exported_copies,
):
    planes, rows, lanes = warming_above_ambient.shape
    temp = warming_above_ambient.reshape(planes * rows, lanes)
    kappa = fourier_stability_factor.reshape(planes * rows, lanes)
    blocks = lax.axis_size("cut")
    groups = lax.axis_size("cross")
    count = patch_locator.shape[0]
    half = count // groups // LANES
    pitch = rows + PAD
    total = planes + 2 * RIM
    flat = jax.ShapeDtypeStruct(((total + 2) * pitch, lanes), F32)
    wide = RIM * rows

    exports = exported_copies.shape[0] // LANES
    carried = jax.ShapeDtypeStruct((2 * wide + 4 * (count // LANES) + exports, LANES), F32)
    devices = blocks * groups
    sent, even_x, odd_x, code = call(
        parcel_kernel,
        [
            jax.ShapeDtypeStruct((devices * 4 * half, LANES), F32),
            carried,
            carried,
            jax.ShapeDtypeStruct((half, groups, LANES), I32),
        ],
        [
            temp,
            kappa,
            patch_locator.reshape(-1, LANES),
            photon_gain_wattage.reshape(-1, LANES),
            on_skin_marker.reshape(-1, LANES),
            grain_placements,
            exported_copies.reshape(-1, LANES),
        ],
        [
            pltpu.VMEM((count // LANES, LANES), I32),
            pltpu.VMEM((count // LANES, LANES), F32),
            pltpu.VMEM((count // LANES, LANES), I32),
            pltpu.VMEM(grain_placements.shape, F32),
            pltpu.VMEM((exports, LANES), I32),
            pltpu.SemaphoreType.DMA((9,)),
        ],
        left=7,
        limit=None,
    )

    def exchange(sent):
        sent = sent.reshape(devices, -1, LANES)
        return lax.all_to_all(sent, BOTH, split_axis=0, concat_axis=0, tiled=True)

    got = exchange(sent).reshape(blocks, groups, 4 * half, LANES)
    even_x, odd_x = swaps("cut", True, even_x, odd_x)

    strips = jax.ShapeDtypeStruct((2 * RIM, planes, lanes), F32)
    even_y, odd_y = call(
        functools.partial(rows_kernel, rows), [strips, strips], [sent, temp, kappa], left=1
    )
    even_y, odd_y = swaps("cross", False, even_y, odd_y)

    strips = jax.ShapeDtypeStruct(((RIM - 1) * (-(-total // 8) * 8), lanes), F32)
    entries = 2 * count + 4 * count // QUARTERS
    source, even_s, odd_s = call(
        functools.partial(deposit_kernel, planes),
        [flat, strips, strips],
        [got],
        [
            pltpu.VMEM((2 * lanes, entries), BF16),
            pltpu.VMEM((rows, entries), BF16),
            pltpu.VMEM((rows, entries), jnp.int16),
        ],
    )
    corners = jax.ShapeDtypeStruct((strips.shape[0] + 2 * RIM * PAD, lanes), F32)
    even_s, odd_s = call(
        functools.partial(corner_kernel, rows), [corners, corners], [even_s, odd_s, even_x, odd_x]
    )
    even_s, odd_s = swaps("cross", False, even_s, odd_s)

    grid = pltpu.VMEM(flat.shape, F32)
    matrix = pltpu.VMEM((2 * lanes, 2 * lanes), BF16)
    temp, looked = call(
        heat_kernel,
        [
            jax.ShapeDtypeStruct((planes, rows, lanes), F32),
            jax.ShapeDtypeStruct((devices * 2 * half, LANES), F32),
        ],
        [got, temp, kappa, source, even_x, odd_x, even_y, odd_y, even_s, odd_s],
        [
            grid, grid, grid, grid, grid, grid, matrix, matrix,
            pltpu.VMEM((2 * lanes, planes * rows), BF16),
            pltpu.VMEM((planes, rows, lanes), F32),
            pltpu.SemaphoreType.DMA,
        ],
        outs_left=1,
    )
    back = exchange(looked).reshape(looked.shape)
    acted = tether_acted_grain.reshape(-1, LANES)
    other = tether_other_grain.reshape(-1, LANES)
    entry = jax.ShapeDtypeStruct(acted.shape, F32)
    base, slope, delta, hot, ghost = call(
        functools.partial(stretch_kernel, 2 * wide, half),
        [
            entry,
            entry,
            jax.ShapeDtypeStruct((3,) + acted.shape, F32),
            jax.ShapeDtypeStruct((LANES, acted.size), BF16),
            jax.ShapeDtypeStruct((2, 2, exports, LANES), I32),
        ],
        [
            looked,
            grain_placements,
            acted,
            other,
            tether_relaxed_gap.reshape(-1, LANES),
            snapped_marker.reshape(-1, LANES),
            even_x,
            odd_x,
        ],
        left=1,
    )
    out = jax.ShapeDtypeStruct(grain_placements.shape, F32)
    positions_new, velocities_new = call(
        functools.partial(bond_kernel, blocks),
        [out, out],
        [
            back, code, grain_placements, grain_motion_parts, acted, other, ghost,
            base, slope, delta, hot,
        ],
        [pltpu.VMEM((6 * (count // LANES), acted.size), BF16)],
    )
    return (temp, positions_new, velocities_new)


def solution(mesh):
    return jax.shard_map(
        per_device,
        mesh=mesh,
        in_specs=(
            P("cut", "cross", None),
            P("cut", "cross", None),
            P(("cut", "cross")),
            P(("cut", "cross")),
            P(("cut", "cross")),
            P(None, ("cut", "cross")),
            P(None, ("cut", "cross")),
            P(("cut", "cross")),
            P(("cut", "cross")),
            P(("cut", "cross")),
            P(("cut", "cross")),
            P(("cut", "cross")),
        ),
        out_specs=(P("cut", "cross", None), P(None, ("cut", "cross")), P(None, ("cut", "cross"))),
        check_vma=False,
    )
```

```python
import functools

import jax
import jax.numpy as jnp
from jax import lax
from jax.experimental import pallas as pl
from jax.experimental.pallas import tpu as pltpu
from jax.sharding import PartitionSpec as P

F32 = jnp.float32
BF16 = jnp.bfloat16
I32 = jnp.int32
LANES = 128
BOTH = ("cut", "cross")
VMEM = pl.BlockSpec(memory_space=pltpu.VMEM)
LIMIT = 32 * 1024 * 1024


def call(kernel, outs, operands, scratch=(), left=0, limit=LIMIT, outs_left=0):
    return pl.pallas_call(
        kernel,
        out_shape=outs,
        in_specs=[pl.BlockSpec(memory_space=pltpu.HBM)] * left + [VMEM] * (len(operands) - left),
        out_specs=[pl.BlockSpec(memory_space=pltpu.HBM)] * outs_left + [VMEM] * (len(outs) - outs_left),
        scratch_shapes=list(scratch),
        compiler_params=pltpu.CompilerParams(vmem_limit_bytes=limit),
    )(*operands)


class Either:
    def __init__(self, flag, yes, no):
        self.flag, self.yes, self.no = flag, yes, no
        self.shape = yes.shape

    def __getitem__(self, index):
        yes, no = self.yes[index], self.no[index]
        return jnp.where(jnp.full(yes.shape, self.flag, I32) > 0, yes, no)

    def part(self, index):
        return Either(self.flag, self.yes.at[index], self.no.at[index])


def is_odd(axis):
    return lax.rem(lax.axis_index(axis), 2)


def low_and_high(axis, even, odd):
    flag = is_odd(axis)
    return Either(flag, even, odd), Either(flag, odd, even)


def split(value):
    high = value.astype(BF16)
    return high, (value - high.astype(F32)).astype(BF16)


def iota(shape, dim):
    return lax.broadcasted_iota(I32, shape, dim)


RIM = 3
PAD = 8
QUARTERS = 4


def groups_of(count, most):
    return max(n for n in range(1, most + 1) if count % n == 0)


def difference_matrices(lanes):
    shape = (2 * lanes, 2 * lanes)
    given = iota(shape, 0) & (lanes - 1)
    wanted = iota(shape, 1)
    lower = wanted >= lanes
    wanted = wanted & (lanes - 1)
    beside = jnp.where(lower, wanted - 1, wanted + 1)
    neighbour = jnp.where(given == beside, 1.0, 0.0)
    same = jnp.where(given == wanted, 1.0, 0.0)
    return (neighbour - same).astype(BF16), (neighbour + same).astype(BF16)


def pieces_of(value):
    high, low = split(value)
    return jnp.concatenate([high, low], axis=1)


def conduct_pass(temp, kappa, cond, along_z, minus, plus, first, blocks, pitch):
    lanes = temp.shape[1]
    size = groups_of(blocks, 135)

    def body(n, unused):
        at = pl.ds(pl.multiple_of((first + n * size) * pitch, 8), size * pitch)
        t = temp[at, :]
        c = kappa[at, :] * (0.5 + 1.0 / (1.0 + t * t))
        cond[at, :] = c
        change = jnp.dot(pieces_of(t), minus[...], preferred_element_type=F32)
        both = jnp.dot(pieces_of(c), plus[...], preferred_element_type=F32)
        along_z[at, :] = change[:, :lanes] * both[:, :lanes] + change[:, lanes:] * both[:, lanes:]
        return unused

    lax.fori_loop(0, blocks // size, body, 0)


def flow_pass(temp, cond, along_z, first, blocks, pitch, most, put):
    size = groups_of(blocks, most)

    def rows_at(ref, base):
        return ref[pl.ds(base, pitch), :]

    def body(n, carried):
        t, c, flux = carried
        for k in range(size):
            block = first + n * size + k
            base = pl.multiple_of(block * pitch, 8)
            t_next = rows_at(temp, base + pitch)
            c_next = rows_at(cond, base + pitch)
            onward = (c + c_next) * (t_next - t)
            net = rows_at(along_z, base) + (onward - flux)
            for shift in (1, -1):
                net = net + (c + rows_at(cond, base + shift)) * (rows_at(temp, base + shift) - t)
            put(block, t + net)
            t, c, flux = t_next, c_next, onward
        return t, c, flux

    base = first * pitch
    t, c = rows_at(temp, base), rows_at(cond, base)
    flux = (c + rows_at(cond, base - pitch)) * (t - rows_at(temp, base - pitch))
    lax.fori_loop(0, blocks // size, body, (t, c, flux))


def rim_mask(pitch, lanes):
    place = iota((pitch, lanes), 0)
    side = lax.axis_index("cross")
    below = jnp.where(side > 0, 1.0, 0.0)
    above = jnp.where(side < lax.axis_size("cross") - 1, 1.0, 0.0)
    return jnp.where(place < PAD - RIM, above, jnp.where(place < PAD, below, 1.0))


def fill(flat, own, x_low, x_high, y_low, y_high, rows, scale):
    pitch = rows + PAD
    planes = own.shape[0] // rows
    flat[...] = jnp.zeros(flat.shape, F32)

    def place(p, part):
        flat[pl.ds(pl.multiple_of(p * pitch + PAD, 8), rows), :] = part * scale

    for n in range(RIM):
        place(n, x_low[n * rows : (n + 1) * rows, :])
        place(RIM + planes + n, x_high[n * rows : (n + 1) * rows, :])

    def body(p, unused):
        place(p + RIM, own[pl.ds(pl.multiple_of(p * rows, 8), rows), :])
        return unused

    lax.fori_loop(0, planes, body, 0, unroll=8)
    for r in range(RIM):
        below = PAD - RIM + r
        flat[pl.ds(RIM * pitch + below, planes, stride=pitch), :] = y_low[r, :, :] * scale
        flat[pl.ds((RIM + 1) * pitch + r, planes, stride=pitch), :] = y_high[r, :, :] * scale


def fill_corners(flat, first, low, high, rows, scale):
    pitch = rows + PAD
    for n in range(2 * RIM):
        block = n if n < RIM else first + n - RIM
        for r in range(RIM):
            below = block * pitch + PAD - RIM + r
            above = (block + 1) * pitch + r
            flat[below : below + 1, :] = low[r, n : n + 1, :] * scale
            flat[above : above + 1, :] = high[r, n : n + 1, :] * scale


def parcel_kernel(
    rows, temp, kappa, cells, watts, marks, pos, export, sent, even, odd, even_y, odd_y, code,
    cell_in, watt_in, mark_in, pos_in, export_in, temp_in, kappa_in, sems,
):
    count = pos.shape[1] // LANES
    exports = export.shape[0]
    wide = (even.shape[0] - 4 * count - exports) // 2
    height, lanes = temp.shape
    patch = height * lanes
    half, groups, _ = code.shape
    cap = half * LANES
    quarter = cap // QUARTERS
    moves = [(cells, cell_in), (watts, watt_in), (marks, mark_in), (pos, pos_in), (export, export_in)]
    tail = (1 - is_odd("cut")) * (height - wide)
    for n, field in enumerate((temp, kappa)):
        target = pl.ds(n * wide, wide)
        for out, start in ((even, tail), (odd, height - wide - tail)):
            moves.append((field.at[pl.ds(pl.multiple_of(start, 16), wide)], out.at[target]))
    moves += [(temp, temp_in), (kappa, kappa_in)]
    copies = [pltpu.make_async_copy(*move, sems.at[n]) for n, move in enumerate(moves)]
    for copy in copies:
        copy.start()
    for copy in copies[:3]:
        copy.wait()

    def by_group(ref):
        return jnp.concatenate([ref[pl.ds(h, groups, stride=half), :] for h in range(half)], axis=1)

    cell = by_group(cell_in)
    power = by_group(mark_in).astype(F32) * by_group(watt_in) * 0.5
    upper = cell >= patch
    cell = jnp.where(upper, cell - patch, cell)
    share = cell // (patch // QUARTERS)
    kind = jnp.where(upper, share + QUARTERS, share)
    members = [jnp.where(kind == k, 1.0, 0.0) for k in range(2 * QUARTERS)]
    earlier = jnp.where(iota((cap, cap), 0) < iota((cap, cap), 1), 1.0, 0.0).astype(BF16)
    before = jnp.dot(
        jnp.concatenate(members, axis=0).astype(BF16), earlier, preferred_element_type=F32
    )
    rank = jnp.zeros((groups, cap), F32)
    most = jnp.zeros((groups, 1), F32)
    for k, member in enumerate(members):
        ahead = before[k * groups : (k + 1) * groups]
        rank = rank + member * ahead
        most = jnp.maximum(most, ahead[:, cap - 1 :] + member[:, cap - 1 :])
    fits = jnp.broadcast_to(most, (groups, cap)) <= quarter
    region = share ^ is_odd("cross")
    slot = jnp.where(fits, region * quarter + rank.astype(I32), iota((groups, cap), 1))
    mark = jnp.where(upper, slot + cap, slot)
    for h in range(half):
        code[h] = mark[:, h * LANES : (h + 1) * LANES]
    number = cell + 1
    digits = [number & 255, lax.shift_right_logical(number, 8) & 255, lax.shift_right_logical(number, 16)]
    digits = [d.astype(F32) for d in digits]
    top = power.astype(BF16).astype(F32)
    middle = (power - top).astype(BF16).astype(F32)
    digits += [top, middle, power - top - middle]
    stacked = [jnp.where(upper, 0.0, d) for d in digits] + [jnp.where(upper, d, 0.0) for d in digits]
    stacked = jnp.concatenate(stacked, axis=0).astype(BF16)
    place = iota((16, cap), 0).astype(jnp.int16)
    one = jnp.ones((16, cap), BF16)
    of_group = iota((stacked.shape[0], cap), 0) & (groups - 1)
    moved = jnp.zeros(stacked.shape, F32)
    for j in range(groups):
        goes = jnp.broadcast_to(slot[j : j + 1], (16, cap)).astype(jnp.int16)
        swap = jnp.concatenate(
            [
                jnp.where(goes == place + jnp.int16(t * 16), one, jnp.zeros_like(one))
                for t in range(cap // 16)
            ],
            axis=0,
        )
        result = lax.dot_general(
            stacked, swap, (((1,), (1,)), ((), ())), preferred_element_type=F32
        )
        moved = jnp.where(of_group == j, result, moved)
    sign = jnp.where(fits, 1.0, -1.0)
    blocks = sent.shape[0] // (groups * 4 * half)
    for kind in range(2):
        part = [
            moved[(6 * kind + n) * groups : (6 * kind + n + 1) * groups] for n in range(6)
        ]
        numbers = (part[0] + 256.0 * part[1] + 65536.0 * part[2]) * sign
        powers = part[3] + part[4] + part[5]
        for n, value in enumerate((numbers, powers)):
            for h in range(half):
                row = kind * 2 * half + n * half + h
                for block in range(blocks):
                    at = pl.ds(block * groups * 4 * half + row, groups, stride=4 * half)
                    sent[at, :] = value[:, h * LANES : (h + 1) * LANES]
    for copy in copies[3:5]:
        copy.wait()
    for out in (even, odd):
        for ch in range(3):
            for r in range(count):
                at = 2 * wide + ch * count + r
                out[at : at + 1, :] = pos_in[ch : ch + 1, r * LANES : (r + 1) * LANES]
        at = 2 * wide + 3 * count
        for h in range(half):
            out[pl.ds(at + h, groups, stride=half), :] = code[h].astype(F32)
        out[at + count :, :] = export_in[...].astype(F32)
    for copy in copies[5:]:
        copy.wait()
    top = (1 - is_odd("cross")) * (rows - RIM)
    for n, own in enumerate((temp_in, kappa_in)):
        for r in range(RIM):
            for out, first in ((even_y, top), (odd_y, rows - RIM - top)):
                out[n * RIM + r] = own[pl.ds(first + r, height // rows, stride=rows), :]


def corner_kernel(rows, even_s, odd_s, even_x, odd_x, even, odd):
    side = RIM * rows
    low, high = low_and_high("cut", even_x, odd_x)
    top = (1 - is_odd("cross")) * (rows - RIM)
    base = even_s.shape[0]
    for out, strips, first in ((even, even_s, top), (odd, odd_s, rows - RIM - top)):
        out[:base, :] = strips[...]
        for n in range(2 * RIM):
            for p in range(RIM):
                at = pl.ds(n // RIM * side + p * rows + first + n % RIM, 1)
                to = base + n * PAD + p
                out[to : to + 1, :] = low[at, :]
                out[to + RIM : to + RIM + 1, :] = high[at, :]
            out[base + n * PAD + 2 * RIM : base + (n + 1) * PAD, :] = jnp.zeros((PAD - 2 * RIM, LANES), F32)


class Rows:
    def __init__(self, ref, base, size):
        self.ref, self.base, self.size = ref, base, size

    def __getitem__(self, index):
        r, at, lanes = index
        first = self.base + r * self.size
        return self.ref[first + (at.start or 0) : first + (self.size if at.stop is None else at.stop), :]


ENDS = 2 * RIM


def open_kernel(
    rows, after, temp, kappa_own, even_x, odd_x, even_y, odd_y,
    opened, kappa, ends, now, cond, along_z, minus, plus,
):
    lanes = temp.shape[1]
    pitch = rows + PAD
    planes = temp.shape[0] // rows
    blocks = planes + 2 * RIM + 1
    side = RIM * rows
    x_low, x_high = low_and_high("cut", even_x, odd_x)
    y_low, y_high = low_and_high("cross", even_y, odd_y)
    minus[...], plus[...] = difference_matrices(lanes)
    for n, (flat, own, scale) in enumerate(((now, temp, 1.0), (kappa, kappa_own, 0.5))):
        beside = [half.part(slice(n * side, (n + 1) * side)) for half in (x_low, x_high)]
        strips = [half.part(slice(n * RIM, (n + 1) * RIM)) for half in (y_low, y_high)]
        fill(flat, own, *beside, *strips, rows, scale)
    size = ENDS * pitch
    ends[:size, :] = now[:size, :]
    ends[size:, :] = now[(blocks - ENDS) * pitch : blocks * pitch, :]
    conduct_pass(now, kappa, cond, along_z, minus, plus, 0, blocks, pitch)
    opened[0:pitch, :] = jnp.zeros((pitch, lanes), F32)
    opened[(blocks - 1) * pitch :, :] = jnp.zeros((opened.shape[0] - (blocks - 1) * pitch, lanes), F32)

    def put(block, value):
        opened[pl.ds(pl.multiple_of(block * pitch, 8), pitch), :] = value

    flow_pass(now, cond, along_z, 1, blocks - 2, pitch, 1000, put)


def heat_kernel(
    got, opened, kappa_in, ends_in, source_own, even_s, odd_s,
    temp_out, looked, source, kappa, ends, ends_kappa, now, then, cond, along_z, minus, plus, pieces,
    result, sem,
):
    lanes = kappa.shape[1]
    planes, rows, _ = result.shape
    pitch = rows + PAD
    total = planes + 2 * RIM
    blocks = total + 1
    wide = RIM - 1
    s_low, s_high = low_and_high("cross", even_s, odd_s)
    height = -(-total // 8) * 8
    minus[...], plus[...] = difference_matrices(lanes)
    source[...] = source_own[...]
    for first, half in ((PAD - wide, s_low), (PAD + rows, s_high)):
        strips = Rows(half, 0, height)
        for r in range(wide):
            source[pl.ds(first + r, total, stride=pitch), :] = strips[r, :total, :]
    mask = rim_mask(pitch, lanes)

    corners = [
        [Rows(half, wide * height + n * RIM * PAD, PAD) for half in (s_low, s_high)] for n in range(2)
    ]
    size = ENDS * pitch
    last_end = blocks - ENDS
    ends[: 2 * size, :] = ends_in[...]
    ends[2 * size :, :] = jnp.zeros((pitch, lanes), F32)
    fill_corners(ends, 2 * ENDS - RIM - 1, *corners[0], rows, 1.0)
    kappa[...] = kappa_in[...]
    fill_corners(kappa, blocks - RIM - 1, *corners[1], rows, 0.5)
    ends_kappa[:size, :] = kappa[:size, :]
    ends_kappa[size : 2 * size, :] = kappa[last_end * pitch : blocks * pitch, :]
    conduct_pass(ends, ends_kappa, cond, along_z, minus, plus, 0, 2 * ENDS, pitch)
    then[...] = opened[...]
    for first, to in ((1, 1), (ENDS + 1, last_end + 1)):

        def again(block, value, first=first, to=to):
            at = pl.ds((block - first + to) * pitch, pitch)
            then[at, :] = value

        flow_pass(ends, cond, along_z, first, ENDS - 2, pitch, 1000, again)

    def add_source(n, unused):
        at = pl.ds(pl.multiple_of(n * pitch, 8), pitch)
        then[at, :] = (then[at, :] + source[at, :]) * mask
        return unused

    lax.fori_loop(1, blocks - 1, add_source, 0, unroll=7)
    now[0:pitch, :] = jnp.zeros((pitch, lanes), F32)
    now[(blocks - 1) * pitch :, :] = jnp.zeros((now.shape[0] - (blocks - 1) * pitch, lanes), F32)
    conduct_pass(then, kappa, cond, along_z, minus, plus, 0, blocks, pitch)

    def middle(block, value):
        at = pl.ds(pl.multiple_of(block * pitch, 8), pitch)
        now[at, :] = (value + source[at, :]) * mask

    flow_pass(then, cond, along_z, 1, blocks - 2, pitch, 1000, middle)
    conduct_pass(now, kappa, cond, along_z, minus, plus, 0, blocks, pitch)

    def last(block, value):
        at = pl.ds(pl.multiple_of(block * pitch, 8), pitch)
        result[block - RIM] = (value + source[at, :])[PAD:]

    flow_pass(now, cond, along_z, RIM, planes, pitch, 1000, last)
    copy = pltpu.make_async_copy(result, temp_out, sem)
    copy.start()
    height = planes * rows
    for first in range(0, planes, lanes // rows):
        turned = result[first : first + lanes // rows].reshape(lanes, lanes).T
        high, low = split(turned)
        pieces[:lanes, first * rows : first * rows + lanes] = high
        pieces[lanes:, first * rows : first * rows + lanes] = low
    lookup(lax.axis_index("cut"), got, height, lanes, rows, looked, pieces)
    copy.wait()


def paired(got, block, kind, row, s):
    at = kind * (got.shape[2] // 2) + row
    first = got[block, s, pl.ds(at, 1), :]
    second = got[block, s + 1, pl.ds(at, 1), :]
    left = iota((1, LANES), 1) < LANES // 2
    return jnp.where(left, first, second), jnp.where(left, second, first)


def cell_of(number):
    return jnp.abs(number).astype(I32) - 1


def unsorted(got):
    half = got.shape[2] // 4
    lowest = jnp.minimum(got[:, :, :half, :], got[:, :, 2 * half : 3 * half, :])
    return jnp.min(lowest) < 0.0


def deposit_kernel(planes, got, source, even, odd, spread, across, plane_of):
    blocks, groups, rows_sent, _ = got.shape
    half = rows_sent // 4
    lanes = source.shape[1]
    rows = across.shape[0]
    pitch = rows + PAD
    here = lax.axis_index("cut")
    place = iota((rows, LANES), 0)
    place16 = place.astype(jnp.int16)
    zero = jnp.zeros((rows, LANES), BF16)
    pairs = groups // 2
    tile = planes // QUARTERS
    region = 2 * pairs * LANES
    inside = QUARTERS * region
    wide = RIM - 1

    def block(distance):
        return lax.rem(here + (blocks + distance), blocks)

    def fill_columns(at, number, power):
        span = pl.ds(pl.multiple_of(at, LANES), LANES)
        cell = cell_of(jnp.broadcast_to(number, (rows, LANES)))
        high, low = split(jnp.broadcast_to(power, (rows, LANES)))
        lane = (cell & (lanes - 1)).astype(jnp.int16)
        for t in range(lanes // rows):
            hit = lane == place16 + jnp.int16(t * rows)
            spread[t * rows : (t + 1) * rows, span] = jnp.where(hit, high, zero)
            spread[lanes + t * rows : lanes + (t + 1) * rows, span] = jnp.where(hit, low, zero)
        row = lax.shift_right_arithmetic(cell, 7)
        across[:, span] = jnp.where((row & (rows - 1)) == place, 1.0, 0.0).astype(BF16)
        plane_of[:, span] = lax.shift_right_arithmetic(row, rows.bit_length() - 1).astype(jnp.int16)

    def sides(pair, quarter_high, quarter_low):
        for n, (distance, kind) in enumerate(((1, 0), (0, 1), (-1, 0), (-2, 1))):
            share = quarter_high if n < 2 else quarter_low
            h, which = share // 2, share % 2
            number = paired(got, block(distance), kind, h, 2 * pair)[which]
            power = paired(got, block(distance), kind, half + h, 2 * pair)[which]
            fill_columns(inside + (n * pairs + pair) * LANES, number, power)

    def fill_pair(pair, unused):
        for part in range(2):
            for h in range(half):
                numbers = paired(got, block(-part), part, h, 2 * pair)
                powers = paired(got, block(-part), part, half + h, 2 * pair)
                for which in range(2):
                    at = (2 * h + which) * region + (part * pairs + pair) * LANES
                    fill_columns(at, numbers[which], powers[which])
        sides(pair, 0, QUARTERS - 1)
        return unused

    lax.fori_loop(0, pairs, fill_pair, 0)
    source[...] = jnp.zeros(source.shape, F32)

    def product(first, base, count, columns, added=False):
        where_y = across[:, columns]
        where_x = plane_of[:, columns] - jnp.asarray(base, I32).astype(jnp.int16)
        nothing = jnp.zeros_like(where_y)
        hot = jnp.concatenate(
            [jnp.where(where_x == jnp.int16(x), where_y, nothing) for x in range(count)], axis=0
        )
        both = lax.dot_general(
            hot, spread[:, columns], (((1,), (1,)), ((), ())), preferred_element_type=F32
        )
        value = both[:, :lanes] + both[:, lanes:]
        for n in range(count):
            at = pl.ds(pl.multiple_of((first + n + RIM) * pitch + PAD, 8), rows)
            part = value[n * rows : (n + 1) * rows]
            source[at, :] = source[at, :] + part if added else part

    for q in range(QUARTERS):
        product(q * tile, q * tile, tile, slice(q * region, (q + 1) * region))

    def outside(added):
        product(planes, 0, wide, slice(inside, inside + region), added)
        product(-wide, planes - wide, wide, slice(inside + region, inside + 2 * region), added)

    outside(False)

    @pl.when(unsorted(got))
    def _():
        def whole(m, unused):
            product(m * tile, m * tile, tile, slice(0, inside))
            return unused

        lax.fori_loop(0, QUARTERS, whole, 0)
        for step in range(1, QUARTERS):

            def others(pair, unused, step=step):
                sides(pair, step, QUARTERS - 1 - step)
                return unused

            lax.fori_loop(0, pairs, others, 0)
            outside(True)

    planes_all = planes + 2 * RIM
    top = (1 - is_odd("cross")) * (rows - wide)
    for r in range(wide):
        for out, first in ((even, top), (odd, rows - wide - top)):
            at = r * (out.shape[0] // wide)
            out[at : at + planes_all, :] = source[pl.ds(PAD + first + r, planes_all, stride=pitch), :]


def lookup(me, got, height, lanes, rows, looked, pieces):
    blocks, groups, rows_sent, _ = got.shape
    half = rows_sent // 4
    pairs = groups // 2
    shift = rows.bit_length() - 1
    place = iota((rows, LANES), 0)
    lane_place = iota((lanes, LANES), 0)
    zero = jnp.zeros((rows, LANES), BF16)

    def search(numbers, base, size):
        hots = []
        for number in numbers:
            row = lax.shift_right_arithmetic(cell_of(jnp.broadcast_to(number, (rows, LANES))), 7)
            plane = lax.shift_right_arithmetic(row, shift).astype(jnp.int16)
            hot_row = jnp.where((row & (rows - 1)) == place, 1.0, 0.0).astype(BF16)
            hots.append(
                jnp.concatenate(
                    [
                        jnp.where(plane == jnp.int16(x), hot_row, zero)
                        for x in range(base // rows, (base + size) // rows)
                    ],
                    axis=0,
                )
            )
        both = jnp.dot(
            pieces[:, base : base + size],
            jnp.concatenate(hots, axis=1),
            preferred_element_type=F32,
        )
        value = both[:lanes] + both[lanes:]
        results = []
        for n, number in enumerate(numbers):
            lane = cell_of(jnp.broadcast_to(number, (lanes, LANES))) & (lanes - 1)
            part = jnp.where(lane == lane_place, value[:, n * LANES : (n + 1) * LANES], 0.0)
            results.append(jnp.sum(part, axis=0, keepdims=True))
        return results

    left = iota((1, LANES), 1) < LANES // 2

    def run(full):
        for h in range(half):
            found = []
            for which in range(2):
                numbers = []
                for part in range(2):
                    block = lax.rem(me + (blocks - part), blocks)
                    for pair in range(pairs):
                        numbers.append(paired(got, block, part, h, 2 * pair)[which])
                size = height // QUARTERS
                found.append(
                    search(numbers, 0, height) if full else search(numbers, (2 * h + which) * size, size)
                )
            for part in range(2):
                for pair in range(pairs):
                    a, b = (f[part * pairs + pair] for f in found)
                    for s, value in ((0, jnp.where(left, a, b)), (1, jnp.where(left, b, a))):
                        row = (2 * pair + s) * 2 * half + part * half + h
                        for block in range(blocks):
                            at = block * groups * 2 * half + row
                            looked[at : at + 1, :] = value

    run(False)

    @pl.when(unsorted(got))
    def _():
        run(True)


def pick(tables, index, row=None):
    if row is None:
        row = lax.shift_right_logical(index, 7)
    lane = index & (LANES - 1)
    results = [jnp.zeros(index.shape, F32) for _ in tables]
    for r in range(len(tables[0])):
        here = row == r
        for ch, rows in enumerate(tables):
            value = jnp.take_along_axis(jnp.broadcast_to(rows[r], index.shape), lane, axis=1)
            results[ch] = jnp.where(here, value, results[ch])
    return results


def rows_of(ref, ch):
    return [ref[ch : ch + 1, r * LANES : (r + 1) * LANES] for r in range(ref.shape[1] // LANES)]


def stretch_kernel(
    side, half, after, pos, acted, other, gap, snapped, even_x, odd_x, base, slope, delta, hot, ghost,
):
    count = pos.shape[1] // LANES
    low_ghost, high_ghost = low_and_high("cut", even_x, odd_x)

    def ghosts(n, ref):
        places = side + 4 * count
        tables = [
            [ref[side + ch * count + r : side + ch * count + r + 1, :] for r in range(count)]
            for ch in range(4)
        ]
        index = ref[places:, :].astype(I32)
        found = pick(tables, index)
        code = found.pop().astype(I32)
        group = index // (half * LANES)
        ghost[n, 0] = group * (2 * half) + lax.shift_right_logical(code, 7)
        ghost[n, 1] = code & (LANES - 1)
        return [[f[r : r + 1] for r in range(f.shape[0])] for f in found]

    own = [rows_of(pos, ch) for ch in range(3)]
    low = ghosts(0, low_ghost)
    high = ghosts(1, high_ghost)
    first = pick(own, acted[...])
    second = pick([own[ch] + low[ch] + high[ch] for ch in range(3)], other[...])
    d = [second[ch] - first[ch] for ch in range(3)]
    dist = jnp.sqrt(d[0] * d[0] + d[1] * d[1] + d[2] * d[2])
    weight = (1.0 - snapped[...].astype(F32)) / jnp.maximum(dist, 0.3)
    base[...] = weight * (dist - gap[...])
    slope[...] = weight * (gap[...] * (0.2 * 0.5))
    for ch in range(3):
        delta[ch] = d[ch]
    place = iota((16, LANES), 0).astype(jnp.int16)
    one = jnp.ones((16, LANES), BF16)
    for r in range(acted.shape[0]):
        lane = jnp.broadcast_to(acted[r : r + 1, :] & (LANES - 1), (16, LANES)).astype(jnp.int16)
        for t in range(LANES // 16):
            hot[t * 16 : (t + 1) * 16, r * LANES : (r + 1) * LANES] = jnp.where(
                lane == place + jnp.int16(t * 16), one, jnp.zeros_like(one)
            )


def bond_kernel(
    blocks, back, code, pos, vel, acted, other, ghost, base, slope, delta, hot, pos_out, vel_out, force,
):
    half, groups, _ = code.shape
    here = lax.axis_index("cut")
    double = 2 * half

    def slots(distance):
        found = []
        for kind in range(2):
            block = lax.rem(here + (blocks + distance + kind), blocks)
            for h in range(half):
                first = block * groups * double + kind * half + h
                found.append(back[pl.ds(first, groups, stride=double), :])
        return found

    def ghosts(n, distance):
        rows = slots(distance)
        table = [rows[k][j : j + 1] for j in range(groups) for k in range(double)]
        found = pick([table], ghost[n, 1], ghost[n, 0])[0]
        return [found[r : r + 1] for r in range(found.shape[0])]

    rows = slots(0)
    temps = []
    for h in range(half):
        index = code[h]
        temp = jnp.zeros(index.shape, F32)
        for k in range(double):
            value = jnp.take_along_axis(rows[k], index & (LANES - 1), axis=1)
            temp = jnp.where(lax.shift_right_logical(index, 7) == k, value, temp)
        temps.append(temp)
    own = [temps[h][j : j + 1] for j in range(groups) for h in range(half)]
    first = pick([own], acted[...])[0]
    second = pick([own + ghosts(0, -1) + ghosts(1, 1)], other[...])[0]
    scale = base[...] - slope[...] * (first + second)
    values = [split(scale * delta[ch]) for ch in range(3)]
    values = [piece.astype(F32) for pair in values for piece in pair]
    high_count = len(own)
    high_place = iota((high_count, LANES), 0)
    for r in range(acted.shape[0]):
        span = slice(r * LANES, (r + 1) * LANES)
        at_row = lax.shift_right_logical(acted[r : r + 1, :], 7) == high_place
        for n, value in enumerate(values):
            force[n * high_count : (n + 1) * high_count, span] = jnp.where(
                at_row, jnp.broadcast_to(value[r : r + 1], (high_count, LANES)), 0.0
            ).astype(BF16)
    total = lax.dot_general(
        force[...], hot[...], (((1,), (1,)), ((), ())), preferred_element_type=F32
    )
    for ch in range(3):
        base_row = 2 * ch * high_count
        summed = (
            total[base_row : base_row + high_count]
            + total[base_row + high_count : base_row + 2 * high_count]
        )
        for r in range(high_count):
            span = slice(r * LANES, (r + 1) * LANES)
            velocity = vel[ch : ch + 1, span] + 0.5 * summed[r : r + 1]
            vel_out[ch : ch + 1, span] = velocity
            pos_out[ch : ch + 1, span] = pos[ch : ch + 1, span] + 0.5 * velocity


def swaps(axis, closed, even, odd):
    count = lax.axis_size(axis)
    results = []
    for first, block in ((0, even), (1, odd)):
        pairs = []
        for i in range(first, count if closed else count - 1, 2):
            pairs += [(i, (i + 1) % count), ((i + 1) % count, i)]
        results.append(lax.ppermute(block, axis, pairs))
    return results


def per_device(
    warming_above_ambient,
    fourier_stability_factor,
    patch_locator,
    photon_gain_wattage,
    on_skin_marker,
    grain_placements,
    grain_motion_parts,
    tether_acted_grain,
    tether_other_grain,
    tether_relaxed_gap,
    snapped_marker,
    exported_copies,
):
    planes, rows, lanes = warming_above_ambient.shape
    temp = warming_above_ambient.reshape(planes * rows, lanes)
    kappa = fourier_stability_factor.reshape(planes * rows, lanes)
    blocks = lax.axis_size("cut")
    groups = lax.axis_size("cross")
    count = patch_locator.shape[0]
    half = count // groups // LANES
    pitch = rows + PAD
    total = planes + 2 * RIM
    flat = jax.ShapeDtypeStruct(((total + 2) * pitch, lanes), F32)
    wide = RIM * rows

    exports = exported_copies.shape[0] // LANES
    carried = jax.ShapeDtypeStruct((2 * wide + 4 * (count // LANES) + exports, LANES), F32)
    devices = blocks * groups
    strips = jax.ShapeDtypeStruct((2 * RIM, planes, lanes), F32)
    whole = pltpu.VMEM(temp.shape, F32)
    sent, even_x, odd_x, even_y, odd_y, code = call(
        functools.partial(parcel_kernel, rows),
        [
            jax.ShapeDtypeStruct((devices * 4 * half, LANES), F32),
            carried,
            carried,
            strips,
            strips,
            jax.ShapeDtypeStruct((half, groups, LANES), I32),
        ],
        [
            temp,
            kappa,
            patch_locator.reshape(-1, LANES),
            photon_gain_wattage.reshape(-1, LANES),
            on_skin_marker.reshape(-1, LANES),
            grain_placements,
            exported_copies.reshape(-1, LANES),
        ],
        [
            pltpu.VMEM((count // LANES, LANES), I32),
            pltpu.VMEM((count // LANES, LANES), F32),
            pltpu.VMEM((count // LANES, LANES), I32),
            pltpu.VMEM(grain_placements.shape, F32),
            pltpu.VMEM((exports, LANES), I32),
            whole,
            whole,
            pltpu.SemaphoreType.DMA((11,)),
        ],
        left=7,
        limit=None,
    )

    def exchange(sent):
        sent = sent.reshape(devices, -1, LANES)
        return lax.all_to_all(sent, BOTH, split_axis=0, concat_axis=0, tiled=True)

    got = exchange(sent).reshape(blocks, groups, 4 * half, LANES)
    even_x, odd_x = swaps("cut", True, even_x, odd_x)

    even_y, odd_y = swaps("cross", False, even_y, odd_y)

    strips = jax.ShapeDtypeStruct(((RIM - 1) * (-(-total // 8) * 8), lanes), F32)
    entries = 2 * count + 4 * count // QUARTERS
    source, even_s, odd_s = call(
        functools.partial(deposit_kernel, planes),
        [flat, strips, strips],
        [got],
        [
            pltpu.VMEM((2 * lanes, entries), BF16),
            pltpu.VMEM((rows, entries), BF16),
            pltpu.VMEM((rows, entries), jnp.int16),
        ],
    )
    corners = jax.ShapeDtypeStruct((strips.shape[0] + 2 * RIM * PAD, lanes), F32)
    even_s, odd_s = call(
        functools.partial(corner_kernel, rows), [corners, corners], [even_s, odd_s, even_x, odd_x]
    )
    sent_strips = even_s
    even_s, odd_s = swaps("cross", False, even_s, odd_s)

    grid = pltpu.VMEM(flat.shape, F32)
    matrix = pltpu.VMEM((2 * lanes, 2 * lanes), BF16)
    ends = jax.ShapeDtypeStruct((2 * ENDS * pitch, lanes), F32)
    opened, kappa, ends = call(
        functools.partial(open_kernel, rows),
        [flat, flat, ends],
        [sent_strips, temp, kappa, even_x, odd_x, even_y, odd_y],
        [grid, grid, grid, matrix, matrix],
        left=1,
    )
    ends_grid = pltpu.VMEM((2 * ENDS * pitch + pitch, lanes), F32)
    temp, looked = call(
        heat_kernel,
        [
            jax.ShapeDtypeStruct((planes, rows, lanes), F32),
            jax.ShapeDtypeStruct((devices * 2 * half, LANES), F32),
        ],
        [got, opened, kappa, ends, source, even_s, odd_s],
        [
            grid, grid, ends_grid, ends_grid, grid, grid, grid, grid, matrix, matrix,
            pltpu.VMEM((2 * lanes, planes * rows), BF16),
            pltpu.VMEM((planes, rows, lanes), F32),
            pltpu.SemaphoreType.DMA,
        ],
        outs_left=1,
    )
    back = exchange(looked).reshape(looked.shape)
    acted = tether_acted_grain.reshape(-1, LANES)
    other = tether_other_grain.reshape(-1, LANES)
    entry = jax.ShapeDtypeStruct(acted.shape, F32)
    base, slope, delta, hot, ghost = call(
        functools.partial(stretch_kernel, 2 * wide, half),
        [
            entry,
            entry,
            jax.ShapeDtypeStruct((3,) + acted.shape, F32),
            jax.ShapeDtypeStruct((LANES, acted.size), BF16),
            jax.ShapeDtypeStruct((2, 2, exports, LANES), I32),
        ],
        [
            looked,
            grain_placements,
            acted,
            other,
            tether_relaxed_gap.reshape(-1, LANES),
            snapped_marker.reshape(-1, LANES),
            even_x,
            odd_x,
        ],
        left=1,
    )
    out = jax.ShapeDtypeStruct(grain_placements.shape, F32)
    positions_new, velocities_new = call(
        functools.partial(bond_kernel, blocks),
        [out, out],
        [
            back, code, grain_placements, grain_motion_parts, acted, other, ghost,
            base, slope, delta, hot,
        ],
        [pltpu.VMEM((6 * (count // LANES), acted.size), BF16)],
    )
    return (temp, positions_new, velocities_new)


def solution(mesh):
    return jax.shard_map(
        per_device,
        mesh=mesh,
        in_specs=(
            P("cut", "cross", None),
            P("cut", "cross", None),
            P(("cut", "cross")),
            P(("cut", "cross")),
            P(("cut", "cross")),
            P(None, ("cut", "cross")),
            P(None, ("cut", "cross")),
            P(("cut", "cross")),
            P(("cut", "cross")),
            P(("cut", "cross")),
            P(("cut", "cross")),
            P(("cut", "cross")),
        ),
        out_specs=(P("cut", "cross", None), P(None, ("cut", "cross")), P(None, ("cut", "cross"))),
        check_vma=False,
    )
```

```python
import functools

import jax
import jax.numpy as jnp
from jax import lax
from jax.experimental import pallas as pl
from jax.experimental.pallas import tpu as pltpu
from jax.sharding import PartitionSpec as P

F32 = jnp.float32
BF16 = jnp.bfloat16
I32 = jnp.int32
LANES = 128
BOTH = ("cut", "cross")
VMEM = pl.BlockSpec(memory_space=pltpu.VMEM)
LIMIT = 32 * 1024 * 1024


def call(kernel, outs, operands, scratch=(), left=0, limit=LIMIT, outs_left=0):
    return pl.pallas_call(
        kernel,
        out_shape=outs,
        in_specs=[pl.BlockSpec(memory_space=pltpu.HBM)] * left + [VMEM] * (len(operands) - left),
        out_specs=[pl.BlockSpec(memory_space=pltpu.HBM)] * outs_left + [VMEM] * (len(outs) - outs_left),
        scratch_shapes=list(scratch),
        compiler_params=pltpu.CompilerParams(vmem_limit_bytes=limit),
    )(*operands)


class Either:
    def __init__(self, flag, yes, no):
        self.flag, self.yes, self.no = flag, yes, no
        self.shape = yes.shape

    def __getitem__(self, index):
        yes, no = self.yes[index], self.no[index]
        return jnp.where(jnp.full(yes.shape, self.flag, I32) > 0, yes, no)

    def part(self, index):
        return Either(self.flag, self.yes.at[index], self.no.at[index])


def is_odd(axis):
    return lax.rem(lax.axis_index(axis), 2)


def low_and_high(axis, even, odd):
    flag = is_odd(axis)
    return Either(flag, even, odd), Either(flag, odd, even)


def split(value):
    high = value.astype(BF16)
    return high, (value - high.astype(F32)).astype(BF16)


def iota(shape, dim):
    return lax.broadcasted_iota(I32, shape, dim)


RIM = 3
PAD = 8
QUARTERS = 4


def groups_of(count, most):
    return max(n for n in range(1, most + 1) if count % n == 0)


def difference_matrices(lanes):
    shape = (2 * lanes, 2 * lanes)
    given = iota(shape, 0) & (lanes - 1)
    wanted = iota(shape, 1)
    lower = wanted >= lanes
    wanted = wanted & (lanes - 1)
    beside = jnp.where(lower, wanted - 1, wanted + 1)
    neighbour = jnp.where(given == beside, 1.0, 0.0)
    same = jnp.where(given == wanted, 1.0, 0.0)
    return (neighbour - same).astype(BF16), (neighbour + same).astype(BF16)


def pieces_of(value):
    high, low = split(value)
    return jnp.concatenate([high, low], axis=1)


def conduct_pass(temp, kappa, cond, along_z, minus, plus, first, blocks, pitch):
    lanes = temp.shape[1]
    size = groups_of(blocks, 135)

    def body(n, unused):
        at = pl.ds(pl.multiple_of((first + n * size) * pitch, 8), size * pitch)
        t = temp[at, :]
        c = kappa[at, :] * (0.5 + 1.0 / (1.0 + t * t))
        cond[at, :] = c
        change = jnp.dot(pieces_of(t), minus[...], preferred_element_type=F32)
        both = jnp.dot(pieces_of(c), plus[...], preferred_element_type=F32)
        along_z[at, :] = change[:, :lanes] * both[:, :lanes] + change[:, lanes:] * both[:, lanes:]
        return unused

    lax.fori_loop(0, blocks // size, body, 0)


def flow_pass(temp, cond, along_z, first, blocks, pitch, most, put):
    size = groups_of(blocks, most)

    def rows_at(ref, base):
        return ref[pl.ds(base, pitch), :]

    def body(n, carried):
        t, c, flux = carried
        for k in range(size):
            block = first + n * size + k
            base = pl.multiple_of(block * pitch, 8)
            t_next = rows_at(temp, base + pitch)
            c_next = rows_at(cond, base + pitch)
            onward = (c + c_next) * (t_next - t)
            net = rows_at(along_z, base) + (onward - flux)
            for shift in (1, -1):
                net = net + (c + rows_at(cond, base + shift)) * (rows_at(temp, base + shift) - t)
            put(block, t + net)
            t, c, flux = t_next, c_next, onward
        return t, c, flux

    base = first * pitch
    t, c = rows_at(temp, base), rows_at(cond, base)
    flux = (c + rows_at(cond, base - pitch)) * (t - rows_at(temp, base - pitch))
    lax.fori_loop(0, blocks // size, body, (t, c, flux))


def rim_mask(pitch, lanes):
    place = iota((pitch, lanes), 0)
    side = lax.axis_index("cross")
    below = jnp.where(side > 0, 1.0, 0.0)
    above = jnp.where(side < lax.axis_size("cross") - 1, 1.0, 0.0)
    return jnp.where(place < PAD - RIM, above, jnp.where(place < PAD, below, 1.0))


def fill(flat, own, x_low, x_high, y_low, y_high, rows, scale):
    pitch = rows + PAD
    planes = own.shape[0] // rows
    flat[...] = jnp.zeros(flat.shape, F32)

    def place(p, part):
        flat[pl.ds(pl.multiple_of(p * pitch + PAD, 8), rows), :] = part * scale

    for n in range(RIM):
        place(n, x_low[n * rows : (n + 1) * rows, :])
        place(RIM + planes + n, x_high[n * rows : (n + 1) * rows, :])

    def body(p, unused):
        place(p + RIM, own[pl.ds(pl.multiple_of(p * rows, 8), rows), :])
        return unused

    lax.fori_loop(0, planes, body, 0, unroll=8)
    for r in range(RIM):
        below = PAD - RIM + r
        flat[pl.ds(RIM * pitch + below, planes, stride=pitch), :] = y_low[r, :, :] * scale
        flat[pl.ds((RIM + 1) * pitch + r, planes, stride=pitch), :] = y_high[r, :, :] * scale


def fill_corners(flat, first, low, high, rows, scale):
    pitch = rows + PAD
    for n in range(2 * RIM):
        block = n if n < RIM else first + n - RIM
        for r in range(RIM):
            below = block * pitch + PAD - RIM + r
            above = (block + 1) * pitch + r
            flat[below : below + 1, :] = low[r, n : n + 1, :] * scale
            flat[above : above + 1, :] = high[r, n : n + 1, :] * scale


def parcel_kernel(
    rows, temp, kappa, cells, watts, marks, pos, export, sent, even, odd, even_y, odd_y, code,
    cell_in, watt_in, mark_in, pos_in, export_in, temp_in, kappa_in, sems,
):
    count = pos.shape[1] // LANES
    exports = export.shape[0]
    wide = (even.shape[0] - 4 * exports) // 2
    height, lanes = temp.shape
    patch = height * lanes
    half, groups, _ = code.shape
    cap = half * LANES
    quarter = cap // QUARTERS
    moves = [(cells, cell_in), (watts, watt_in), (marks, mark_in), (pos, pos_in), (export, export_in)]
    tail = (1 - is_odd("cut")) * (height - wide)
    for n, field in enumerate((temp, kappa)):
        target = pl.ds(n * wide, wide)
        for out, start in ((even, tail), (odd, height - wide - tail)):
            moves.append((field.at[pl.ds(pl.multiple_of(start, 16), wide)], out.at[target]))
    moves += [(temp, temp_in), (kappa, kappa_in)]
    copies = [pltpu.make_async_copy(*move, sems.at[n]) for n, move in enumerate(moves)]
    for copy in copies:
        copy.start()
    for copy in copies[:3]:
        copy.wait()

    def by_group(ref):
        return jnp.concatenate([ref[pl.ds(h, groups, stride=half), :] for h in range(half)], axis=1)

    cell = by_group(cell_in)
    power = by_group(mark_in).astype(F32) * by_group(watt_in) * 0.5
    upper = cell >= patch
    cell = jnp.where(upper, cell - patch, cell)
    share = cell // (patch // QUARTERS)
    kind = jnp.where(upper, share + QUARTERS, share)
    members = [jnp.where(kind == k, 1.0, 0.0) for k in range(2 * QUARTERS)]
    earlier = jnp.where(iota((cap, cap), 0) < iota((cap, cap), 1), 1.0, 0.0).astype(BF16)
    before = jnp.dot(
        jnp.concatenate(members, axis=0).astype(BF16), earlier, preferred_element_type=F32
    )
    rank = jnp.zeros((groups, cap), F32)
    most = jnp.zeros((groups, 1), F32)
    for k, member in enumerate(members):
        ahead = before[k * groups : (k + 1) * groups]
        rank = rank + member * ahead
        most = jnp.maximum(most, ahead[:, cap - 1 :] + member[:, cap - 1 :])
    fits = jnp.broadcast_to(most, (groups, cap)) <= quarter
    region = share ^ is_odd("cross")
    slot = jnp.where(fits, region * quarter + rank.astype(I32), iota((groups, cap), 1))
    mark = jnp.where(upper, slot + cap, slot)
    for h in range(half):
        code[h] = mark[:, h * LANES : (h + 1) * LANES]
    number = cell + 1
    digits = [number & 255, lax.shift_right_logical(number, 8) & 255, lax.shift_right_logical(number, 16)]
    digits = [d.astype(F32) for d in digits]
    top = power.astype(BF16).astype(F32)
    middle = (power - top).astype(BF16).astype(F32)
    digits += [top, middle, power - top - middle]
    stacked = [jnp.where(upper, 0.0, d) for d in digits] + [jnp.where(upper, d, 0.0) for d in digits]
    stacked = jnp.concatenate(stacked, axis=0).astype(BF16)
    place = iota((16, cap), 0).astype(jnp.int16)
    one = jnp.ones((16, cap), BF16)
    of_group = iota((stacked.shape[0], cap), 0) & (groups - 1)
    moved = jnp.zeros(stacked.shape, F32)
    for j in range(groups):
        goes = jnp.broadcast_to(slot[j : j + 1], (16, cap)).astype(jnp.int16)
        swap = jnp.concatenate(
            [
                jnp.where(goes == place + jnp.int16(t * 16), one, jnp.zeros_like(one))
                for t in range(cap // 16)
            ],
            axis=0,
        )
        result = lax.dot_general(
            stacked, swap, (((1,), (1,)), ((), ())), preferred_element_type=F32
        )
        moved = jnp.where(of_group == j, result, moved)
    sign = jnp.where(fits, 1.0, -1.0)
    blocks = sent.shape[0] // (groups * 4 * half)
    for kind in range(2):
        part = [
            moved[(6 * kind + n) * groups : (6 * kind + n + 1) * groups] for n in range(6)
        ]
        numbers = (part[0] + 256.0 * part[1] + 65536.0 * part[2]) * sign
        powers = part[3] + part[4] + part[5]
        for n, value in enumerate((numbers, powers)):
            for h in range(half):
                row = kind * 2 * half + n * half + h
                for block in range(blocks):
                    at = pl.ds(block * groups * 4 * half + row, groups, stride=4 * half)
                    sent[at, :] = value[:, h * LANES : (h + 1) * LANES]
    for copy in copies[3:5]:
        copy.wait()
    index = export_in[...]
    codes = [
        mark[j : j + 1, h * LANES : (h + 1) * LANES].astype(F32)
        for j in range(groups)
        for h in range(half)
    ]
    ghost = pick([rows_of(pos_in, ch) for ch in range(3)] + [codes], index)
    ghost[3] = (index // cap * (2 * cap) + ghost[3].astype(I32)).astype(F32)
    for out in (even, odd):
        for n, value in enumerate(ghost):
            out[2 * wide + n * exports : 2 * wide + (n + 1) * exports, :] = value
    for copy in copies[5:]:
        copy.wait()
    top = (1 - is_odd("cross")) * (rows - RIM)
    for n, own in enumerate((temp_in, kappa_in)):
        for r in range(RIM):
            for out, first in ((even_y, top), (odd_y, rows - RIM - top)):
                out[n * RIM + r] = own[pl.ds(first + r, height // rows, stride=rows), :]


def corner_kernel(rows, even_s, odd_s, even_x, odd_x, even, odd):
    side = RIM * rows
    low, high = low_and_high("cut", even_x, odd_x)
    top = (1 - is_odd("cross")) * (rows - RIM)
    base = even_s.shape[0]
    for out, strips, first in ((even, even_s, top), (odd, odd_s, rows - RIM - top)):
        out[:base, :] = strips[...]
        for n in range(2 * RIM):
            for p in range(RIM):
                at = pl.ds(n // RIM * side + p * rows + first + n % RIM, 1)
                to = base + n * PAD + p
                out[to : to + 1, :] = low[at, :]
                out[to + RIM : to + RIM + 1, :] = high[at, :]
            out[base + n * PAD + 2 * RIM : base + (n + 1) * PAD, :] = jnp.zeros((PAD - 2 * RIM, LANES), F32)


class Rows:
    def __init__(self, ref, base, size):
        self.ref, self.base, self.size = ref, base, size

    def __getitem__(self, index):
        r, at, lanes = index
        first = self.base + r * self.size
        return self.ref[first + (at.start or 0) : first + (self.size if at.stop is None else at.stop), :]


ENDS = 2 * RIM


def open_kernel(
    rows, after, temp, kappa_own, even_x, odd_x, even_y, odd_y,
    opened, kappa, ends, now, cond, along_z, minus, plus,
):
    lanes = temp.shape[1]
    pitch = rows + PAD
    planes = temp.shape[0] // rows
    blocks = planes + 2 * RIM + 1
    side = RIM * rows
    x_low, x_high = low_and_high("cut", even_x, odd_x)
    y_low, y_high = low_and_high("cross", even_y, odd_y)
    minus[...], plus[...] = difference_matrices(lanes)
    for n, (flat, own, scale) in enumerate(((now, temp, 1.0), (kappa, kappa_own, 0.5))):
        beside = [half.part(slice(n * side, (n + 1) * side)) for half in (x_low, x_high)]
        strips = [half.part(slice(n * RIM, (n + 1) * RIM)) for half in (y_low, y_high)]
        fill(flat, own, *beside, *strips, rows, scale)
    size = ENDS * pitch
    ends[:size, :] = now[:size, :]
    ends[size:, :] = now[(blocks - ENDS) * pitch : blocks * pitch, :]
    conduct_pass(now, kappa, cond, along_z, minus, plus, 0, blocks, pitch)
    opened[0:pitch, :] = jnp.zeros((pitch, lanes), F32)
    opened[(blocks - 1) * pitch :, :] = jnp.zeros((opened.shape[0] - (blocks - 1) * pitch, lanes), F32)

    def put(block, value):
        opened[pl.ds(pl.multiple_of(block * pitch, 8), pitch), :] = value

    flow_pass(now, cond, along_z, 1, blocks - 2, pitch, 1000, put)


def heat_kernel(
    got, opened, kappa_in, ends_in, source_own, even_s, odd_s,
    temp_out, looked, source, kappa, ends, ends_kappa, now, then, cond, along_z, minus, plus, pieces,
    result, sem,
):
    lanes = kappa.shape[1]
    planes, rows, _ = result.shape
    pitch = rows + PAD
    total = planes + 2 * RIM
    blocks = total + 1
    wide = RIM - 1
    s_low, s_high = low_and_high("cross", even_s, odd_s)
    height = -(-total // 8) * 8
    minus[...], plus[...] = difference_matrices(lanes)
    source[...] = source_own[...]
    for first, half in ((PAD - wide, s_low), (PAD + rows, s_high)):
        strips = Rows(half, 0, height)
        for r in range(wide):
            source[pl.ds(first + r, total, stride=pitch), :] = strips[r, :total, :]
    mask = rim_mask(pitch, lanes)

    corners = [
        [Rows(half, wide * height + n * RIM * PAD, PAD) for half in (s_low, s_high)] for n in range(2)
    ]
    size = ENDS * pitch
    last_end = blocks - ENDS
    ends[: 2 * size, :] = ends_in[...]
    ends[2 * size :, :] = jnp.zeros((pitch, lanes), F32)
    fill_corners(ends, 2 * ENDS - RIM - 1, *corners[0], rows, 1.0)
    kappa[...] = kappa_in[...]
    fill_corners(kappa, blocks - RIM - 1, *corners[1], rows, 0.5)
    ends_kappa[:size, :] = kappa[:size, :]
    ends_kappa[size : 2 * size, :] = kappa[last_end * pitch : blocks * pitch, :]
    conduct_pass(ends, ends_kappa, cond, along_z, minus, plus, 0, 2 * ENDS, pitch)
    then[0:pitch, :] = jnp.zeros((pitch, lanes), F32)
    then[(blocks - 1) * pitch :, :] = jnp.zeros((then.shape[0] - (blocks - 1) * pitch, lanes), F32)
    for n in range(1, blocks - 1):
        if not (1 <= n < ENDS - 1 or last_end + 1 <= n):
            at = pl.ds(n * pitch, pitch)
            then[at, :] = (opened[at, :] + source[at, :]) * mask
    for first, to in ((1, 1), (ENDS + 1, last_end + 1)):

        def again(block, value, first=first, to=to):
            at = pl.ds((block - first + to) * pitch, pitch)
            then[at, :] = (value + source[at, :]) * mask

        flow_pass(ends, cond, along_z, first, ENDS - 2, pitch, 1000, again)

    now[0:pitch, :] = jnp.zeros((pitch, lanes), F32)
    now[(blocks - 1) * pitch :, :] = jnp.zeros((now.shape[0] - (blocks - 1) * pitch, lanes), F32)
    conduct_pass(then, kappa, cond, along_z, minus, plus, 0, blocks, pitch)

    def middle(block, value):
        at = pl.ds(pl.multiple_of(block * pitch, 8), pitch)
        now[at, :] = (value + source[at, :]) * mask

    flow_pass(then, cond, along_z, 1, blocks - 2, pitch, 1000, middle)
    conduct_pass(now, kappa, cond, along_z, minus, plus, 0, blocks, pitch)

    def last(block, value):
        at = pl.ds(pl.multiple_of(block * pitch, 8), pitch)
        result[block - RIM] = (value + source[at, :])[PAD:]

    flow_pass(now, cond, along_z, RIM, planes, pitch, 1000, last)
    copy = pltpu.make_async_copy(result, temp_out, sem)
    copy.start()
    height = planes * rows
    for first in range(0, planes, lanes // rows):
        turned = result[first : first + lanes // rows].reshape(lanes, lanes).T
        high, low = split(turned)
        pieces[:lanes, first * rows : first * rows + lanes] = high
        pieces[lanes:, first * rows : first * rows + lanes] = low
    lookup(lax.axis_index("cut"), got, height, lanes, rows, looked, pieces)
    copy.wait()


def paired(got, block, kind, row, s):
    at = kind * (got.shape[2] // 2) + row
    first = got[block, s, pl.ds(at, 1), :]
    second = got[block, s + 1, pl.ds(at, 1), :]
    left = iota((1, LANES), 1) < LANES // 2
    return jnp.where(left, first, second), jnp.where(left, second, first)


def cell_of(number):
    return jnp.abs(number).astype(I32) - 1


def unsorted(got):
    half = got.shape[2] // 4
    lowest = jnp.minimum(got[:, :, :half, :], got[:, :, 2 * half : 3 * half, :])
    return jnp.min(lowest) < 0.0


def deposit_kernel(planes, got, source, even, odd, spread, across, plane_of):
    blocks, groups, rows_sent, _ = got.shape
    half = rows_sent // 4
    lanes = source.shape[1]
    rows = across.shape[0]
    pitch = rows + PAD
    here = lax.axis_index("cut")
    place = iota((rows, LANES), 0)
    place16 = place.astype(jnp.int16)
    zero = jnp.zeros((rows, LANES), BF16)
    pairs = groups // 2
    tile = planes // QUARTERS
    region = 2 * pairs * LANES
    inside = QUARTERS * region
    wide = RIM - 1

    def block(distance):
        return lax.rem(here + (blocks + distance), blocks)

    def fill_columns(at, number, power):
        span = pl.ds(pl.multiple_of(at, LANES), LANES)
        cell = cell_of(jnp.broadcast_to(number, (rows, LANES)))
        high, low = split(jnp.broadcast_to(power, (rows, LANES)))
        lane = (cell & (lanes - 1)).astype(jnp.int16)
        for t in range(lanes // rows):
            hit = lane == place16 + jnp.int16(t * rows)
            spread[t * rows : (t + 1) * rows, span] = jnp.where(hit, high, zero)
            spread[lanes + t * rows : lanes + (t + 1) * rows, span] = jnp.where(hit, low, zero)
        row = lax.shift_right_arithmetic(cell, 7)
        across[:, span] = jnp.where((row & (rows - 1)) == place, 1.0, 0.0).astype(BF16)
        plane_of[:, span] = lax.shift_right_arithmetic(row, rows.bit_length() - 1).astype(jnp.int16)

    def sides(pair, quarter_high, quarter_low):
        for n, (distance, kind) in enumerate(((1, 0), (0, 1), (-1, 0), (-2, 1))):
            share = quarter_high if n < 2 else quarter_low
            h, which = share // 2, share % 2
            number = paired(got, block(distance), kind, h, 2 * pair)[which]
            power = paired(got, block(distance), kind, half + h, 2 * pair)[which]
            fill_columns(inside + (n * pairs + pair) * LANES, number, power)

    def fill_pair(pair, unused):
        for part in range(2):
            for h in range(half):
                numbers = paired(got, block(-part), part, h, 2 * pair)
                powers = paired(got, block(-part), part, half + h, 2 * pair)
                for which in range(2):
                    at = (2 * h + which) * region + (part * pairs + pair) * LANES
                    fill_columns(at, numbers[which], powers[which])
        sides(pair, 0, QUARTERS - 1)
        return unused

    lax.fori_loop(0, pairs, fill_pair, 0)
    source[...] = jnp.zeros(source.shape, F32)

    def product(first, base, count, columns, added=False):
        where_y = across[:, columns]
        where_x = plane_of[:, columns] - jnp.asarray(base, I32).astype(jnp.int16)
        nothing = jnp.zeros_like(where_y)
        hot = jnp.concatenate(
            [jnp.where(where_x == jnp.int16(x), where_y, nothing) for x in range(count)], axis=0
        )
        both = lax.dot_general(
            hot, spread[:, columns], (((1,), (1,)), ((), ())), preferred_element_type=F32
        )
        value = both[:, :lanes] + both[:, lanes:]
        for n in range(count):
            at = pl.ds(pl.multiple_of((first + n + RIM) * pitch + PAD, 8), rows)
            part = value[n * rows : (n + 1) * rows]
            source[at, :] = source[at, :] + part if added else part

    for q in range(QUARTERS):
        product(q * tile, q * tile, tile, slice(q * region, (q + 1) * region))

    def outside(added):
        product(planes, 0, wide, slice(inside, inside + region), added)
        product(-wide, planes - wide, wide, slice(inside + region, inside + 2 * region), added)

    outside(False)

    @pl.when(unsorted(got))
    def _():
        def whole(m, unused):
            product(m * tile, m * tile, tile, slice(0, inside))
            return unused

        lax.fori_loop(0, QUARTERS, whole, 0)
        for step in range(1, QUARTERS):

            def others(pair, unused, step=step):
                sides(pair, step, QUARTERS - 1 - step)
                return unused

            lax.fori_loop(0, pairs, others, 0)
            outside(True)

    planes_all = planes + 2 * RIM
    top = (1 - is_odd("cross")) * (rows - wide)
    for r in range(wide):
        for out, first in ((even, top), (odd, rows - wide - top)):
            at = r * (out.shape[0] // wide)
            out[at : at + planes_all, :] = source[pl.ds(PAD + first + r, planes_all, stride=pitch), :]


def lookup(me, got, height, lanes, rows, looked, pieces):
    blocks, groups, rows_sent, _ = got.shape
    half = rows_sent // 4
    pairs = groups // 2
    shift = rows.bit_length() - 1
    place = iota((rows, LANES), 0)
    lane_place = iota((lanes, LANES), 0)
    zero = jnp.zeros((rows, LANES), BF16)

    def search(numbers, base, size):
        hots = []
        for number in numbers:
            row = lax.shift_right_arithmetic(cell_of(jnp.broadcast_to(number, (rows, LANES))), 7)
            plane = lax.shift_right_arithmetic(row, shift).astype(jnp.int16)
            hot_row = jnp.where((row & (rows - 1)) == place, 1.0, 0.0).astype(BF16)
            hots.append(
                jnp.concatenate(
                    [
                        jnp.where(plane == jnp.int16(x), hot_row, zero)
                        for x in range(base // rows, (base + size) // rows)
                    ],
                    axis=0,
                )
            )
        both = jnp.dot(
            pieces[:, base : base + size],
            jnp.concatenate(hots, axis=1),
            preferred_element_type=F32,
        )
        value = both[:lanes] + both[lanes:]
        results = []
        for n, number in enumerate(numbers):
            lane = cell_of(jnp.broadcast_to(number, (lanes, LANES))) & (lanes - 1)
            part = jnp.where(lane == lane_place, value[:, n * LANES : (n + 1) * LANES], 0.0)
            results.append(jnp.sum(part, axis=0, keepdims=True))
        return results

    left = iota((1, LANES), 1) < LANES // 2

    def run(full):
        for h in range(half):
            found = []
            for which in range(2):
                numbers = []
                for part in range(2):
                    block = lax.rem(me + (blocks - part), blocks)
                    for pair in range(pairs):
                        numbers.append(paired(got, block, part, h, 2 * pair)[which])
                size = height // QUARTERS
                found.append(
                    search(numbers, 0, height) if full else search(numbers, (2 * h + which) * size, size)
                )
            for part in range(2):
                for pair in range(pairs):
                    a, b = (f[part * pairs + pair] for f in found)
                    for s, value in ((0, jnp.where(left, a, b)), (1, jnp.where(left, b, a))):
                        row = (2 * pair + s) * 2 * half + part * half + h
                        for block in range(blocks):
                            at = block * groups * 2 * half + row
                            looked[at : at + 1, :] = value

    run(False)

    @pl.when(unsorted(got))
    def _():
        run(True)


def pick(tables, index):
    row = lax.shift_right_logical(index, 7)
    lane = index & (LANES - 1)
    results = [jnp.zeros(index.shape, F32) for _ in tables]
    for r in range(len(tables[0])):
        here = row == r
        for ch, rows in enumerate(tables):
            value = jnp.take_along_axis(jnp.broadcast_to(rows[r], index.shape), lane, axis=1)
            results[ch] = jnp.where(here, value, results[ch])
    return results


def rows_of(ref, ch):
    return [ref[ch : ch + 1, r * LANES : (r + 1) * LANES] for r in range(ref.shape[1] // LANES)]


def stretch_kernel(
    side, after, pos, acted, other, gap, snapped, even_x, odd_x, base, slope, delta, hot, ghost,
):
    exports = ghost.shape[1]
    low_ghost, high_ghost = low_and_high("cut", even_x, odd_x)

    def ghosts(n, ref):
        ghost[n] = ref[side + 3 * exports : side + 4 * exports, :].astype(I32)
        places = ref[side : side + 3 * exports, :]
        return [[places[ch * exports + r : ch * exports + r + 1] for r in range(exports)] for ch in range(3)]

    own = [rows_of(pos, ch) for ch in range(3)]
    low = ghosts(0, low_ghost)
    high = ghosts(1, high_ghost)
    first = pick(own, acted[...])
    second = pick([own[ch] + low[ch] + high[ch] for ch in range(3)], other[...])
    d = [second[ch] - first[ch] for ch in range(3)]
    dist = jnp.sqrt(d[0] * d[0] + d[1] * d[1] + d[2] * d[2])
    weight = (1.0 - snapped[...].astype(F32)) / jnp.maximum(dist, 0.3)
    base[...] = weight * (dist - gap[...])
    slope[...] = weight * (gap[...] * (0.2 * 0.5))
    for ch in range(3):
        delta[ch] = d[ch]
    place = iota((16, LANES), 0).astype(jnp.int16)
    one = jnp.ones((16, LANES), BF16)
    for r in range(acted.shape[0]):
        lane = jnp.broadcast_to(acted[r : r + 1, :] & (LANES - 1), (16, LANES)).astype(jnp.int16)
        for t in range(LANES // 16):
            hot[t * 16 : (t + 1) * 16, r * LANES : (r + 1) * LANES] = jnp.where(
                lane == place + jnp.int16(t * 16), one, jnp.zeros_like(one)
            )


def bond_kernel(
    blocks, back, code, pos, vel, acted, other, ghost, base, slope, delta, hot, pos_out, vel_out, force,
):
    half, groups, _ = code.shape
    here = lax.axis_index("cut")
    double = 2 * half

    def slots(distance):
        found = []
        for kind in range(2):
            block = lax.rem(here + (blocks + distance + kind), blocks)
            for h in range(half):
                first = block * groups * double + kind * half + h
                found.append(back[pl.ds(first, groups, stride=double), :])
        return found

    def ghosts(n, distance):
        rows = slots(distance)
        table = [rows[k][j : j + 1] for j in range(groups) for k in range(double)]
        found = pick([table], ghost[n])[0]
        return [found[r : r + 1] for r in range(found.shape[0])]

    rows = slots(0)
    temps = []
    for h in range(half):
        index = code[h]
        temp = jnp.zeros(index.shape, F32)
        for k in range(double):
            value = jnp.take_along_axis(rows[k], index & (LANES - 1), axis=1)
            temp = jnp.where(lax.shift_right_logical(index, 7) == k, value, temp)
        temps.append(temp)
    own = [temps[h][j : j + 1] for j in range(groups) for h in range(half)]
    first = pick([own], acted[...])[0]
    second = pick([own + ghosts(0, -1) + ghosts(1, 1)], other[...])[0]
    scale = base[...] - slope[...] * (first + second)
    values = [split(scale * delta[ch]) for ch in range(3)]
    values = [piece.astype(F32) for pair in values for piece in pair]
    high_count = len(own)
    high_place = iota((high_count, LANES), 0)
    for r in range(acted.shape[0]):
        span = slice(r * LANES, (r + 1) * LANES)
        at_row = lax.shift_right_logical(acted[r : r + 1, :], 7) == high_place
        for n, value in enumerate(values):
            force[n * high_count : (n + 1) * high_count, span] = jnp.where(
                at_row, jnp.broadcast_to(value[r : r + 1], (high_count, LANES)), 0.0
            ).astype(BF16)
    total = lax.dot_general(
        force[...], hot[...], (((1,), (1,)), ((), ())), preferred_element_type=F32
    )
    for ch in range(3):
        base_row = 2 * ch * high_count
        summed = (
            total[base_row : base_row + high_count]
            + total[base_row + high_count : base_row + 2 * high_count]
        )
        for r in range(high_count):
            span = slice(r * LANES, (r + 1) * LANES)
            velocity = vel[ch : ch + 1, span] + 0.5 * summed[r : r + 1]
            vel_out[ch : ch + 1, span] = velocity
            pos_out[ch : ch + 1, span] = pos[ch : ch + 1, span] + 0.5 * velocity


def swaps(axis, closed, even, odd):
    count = lax.axis_size(axis)
    results = []
    for first, block in ((0, even), (1, odd)):
        pairs = []
        for i in range(first, count if closed else count - 1, 2):
            pairs += [(i, (i + 1) % count), ((i + 1) % count, i)]
        results.append(lax.ppermute(block, axis, pairs))
    return results


def per_device(
    warming_above_ambient,
    fourier_stability_factor,
    patch_locator,
    photon_gain_wattage,
    on_skin_marker,
    grain_placements,
    grain_motion_parts,
    tether_acted_grain,
    tether_other_grain,
    tether_relaxed_gap,
    snapped_marker,
    exported_copies,
):
    planes, rows, lanes = warming_above_ambient.shape
    temp = warming_above_ambient.reshape(planes * rows, lanes)
    kappa = fourier_stability_factor.reshape(planes * rows, lanes)
    blocks = lax.axis_size("cut")
    groups = lax.axis_size("cross")
    count = patch_locator.shape[0]
    half = count // groups // LANES
    pitch = rows + PAD
    total = planes + 2 * RIM
    flat = jax.ShapeDtypeStruct(((total + 2) * pitch, lanes), F32)
    wide = RIM * rows

    exports = exported_copies.shape[0] // LANES
    carried = jax.ShapeDtypeStruct((2 * wide + 4 * exports, LANES), F32)
    devices = blocks * groups
    strips = jax.ShapeDtypeStruct((2 * RIM, planes, lanes), F32)
    whole = pltpu.VMEM(temp.shape, F32)
    sent, even_x, odd_x, even_y, odd_y, code = call(
        functools.partial(parcel_kernel, rows),
        [
            jax.ShapeDtypeStruct((devices * 4 * half, LANES), F32),
            carried,
            carried,
            strips,
            strips,
            jax.ShapeDtypeStruct((half, groups, LANES), I32),
        ],
        [
            temp,
            kappa,
            patch_locator.reshape(-1, LANES),
            photon_gain_wattage.reshape(-1, LANES),
            on_skin_marker.reshape(-1, LANES),
            grain_placements,
            exported_copies.reshape(-1, LANES),
        ],
        [
            pltpu.VMEM((count // LANES, LANES), I32),
            pltpu.VMEM((count // LANES, LANES), F32),
            pltpu.VMEM((count // LANES, LANES), I32),
            pltpu.VMEM(grain_placements.shape, F32),
            pltpu.VMEM((exports, LANES), I32),
            whole,
            whole,
            pltpu.SemaphoreType.DMA((11,)),
        ],
        left=7,
        limit=None,
    )

    def exchange(sent):
        sent = sent.reshape(devices, -1, LANES)
        return lax.all_to_all(sent, BOTH, split_axis=0, concat_axis=0, tiled=True)

    got = exchange(sent).reshape(blocks, groups, 4 * half, LANES)
    even_x, odd_x = swaps("cut", True, even_x, odd_x)

    even_y, odd_y = swaps("cross", False, even_y, odd_y)

    strips = jax.ShapeDtypeStruct(((RIM - 1) * (-(-total // 8) * 8), lanes), F32)
    entries = 2 * count + 4 * count // QUARTERS
    source, even_s, odd_s = call(
        functools.partial(deposit_kernel, planes),
        [flat, strips, strips],
        [got],
        [
            pltpu.VMEM((2 * lanes, entries), BF16),
            pltpu.VMEM((rows, entries), BF16),
            pltpu.VMEM((rows, entries), jnp.int16),
        ],
    )
    corners = jax.ShapeDtypeStruct((strips.shape[0] + 2 * RIM * PAD, lanes), F32)
    even_s, odd_s = call(
        functools.partial(corner_kernel, rows), [corners, corners], [even_s, odd_s, even_x, odd_x]
    )
    sent_strips = even_s
    even_s, odd_s = swaps("cross", False, even_s, odd_s)

    grid = pltpu.VMEM(flat.shape, F32)
    matrix = pltpu.VMEM((2 * lanes, 2 * lanes), BF16)
    ends = jax.ShapeDtypeStruct((2 * ENDS * pitch, lanes), F32)
    opened, kappa, ends = call(
        functools.partial(open_kernel, rows),
        [flat, flat, ends],
        [sent_strips, temp, kappa, even_x, odd_x, even_y, odd_y],
        [grid, grid, grid, matrix, matrix],
        left=1,
    )
    ends_grid = pltpu.VMEM((2 * ENDS * pitch + pitch, lanes), F32)
    temp, looked = call(
        heat_kernel,
        [
            jax.ShapeDtypeStruct((planes, rows, lanes), F32),
            jax.ShapeDtypeStruct((devices * 2 * half, LANES), F32),
        ],
        [got, opened, kappa, ends, source, even_s, odd_s],
        [
            grid, grid, ends_grid, ends_grid, grid, grid, grid, grid, matrix, matrix,
            pltpu.VMEM((2 * lanes, planes * rows), BF16),
            pltpu.VMEM((planes, rows, lanes), F32),
            pltpu.SemaphoreType.DMA,
        ],
        outs_left=1,
    )
    back = exchange(looked).reshape(looked.shape)
    acted = tether_acted_grain.reshape(-1, LANES)
    other = tether_other_grain.reshape(-1, LANES)
    entry = jax.ShapeDtypeStruct(acted.shape, F32)
    base, slope, delta, hot, ghost = call(
        functools.partial(stretch_kernel, 2 * wide),
        [
            entry,
            entry,
            jax.ShapeDtypeStruct((3,) + acted.shape, F32),
            jax.ShapeDtypeStruct((LANES, acted.size), BF16),
            jax.ShapeDtypeStruct((2, exports, LANES), I32),
        ],
        [
            looked,
            grain_placements,
            acted,
            other,
            tether_relaxed_gap.reshape(-1, LANES),
            snapped_marker.reshape(-1, LANES),
            even_x,
            odd_x,
        ],
        left=1,
    )
    out = jax.ShapeDtypeStruct(grain_placements.shape, F32)
    positions_new, velocities_new = call(
        functools.partial(bond_kernel, blocks),
        [out, out],
        [
            back, code, grain_placements, grain_motion_parts, acted, other, ghost,
            base, slope, delta, hot,
        ],
        [pltpu.VMEM((6 * (count // LANES), acted.size), BF16)],
    )
    return (temp, positions_new, velocities_new)


def solution(mesh):
    return jax.shard_map(
        per_device,
        mesh=mesh,
        in_specs=(
            P("cut", "cross", None),
            P("cut", "cross", None),
            P(("cut", "cross")),
            P(("cut", "cross")),
            P(("cut", "cross")),
            P(None, ("cut", "cross")),
            P(None, ("cut", "cross")),
            P(("cut", "cross")),
            P(("cut", "cross")),
            P(("cut", "cross")),
            P(("cut", "cross")),
            P(("cut", "cross")),
        ),
        out_specs=(P("cut", "cross", None), P(None, ("cut", "cross")), P(None, ("cut", "cross"))),
        check_vma=False,
    )
```

```python
import functools

import jax
import jax.numpy as jnp
from jax import lax
from jax.experimental import pallas as pl
from jax.experimental.pallas import tpu as pltpu
from jax.sharding import PartitionSpec as P

F32 = jnp.float32
BF16 = jnp.bfloat16
I32 = jnp.int32
LANES = 128
BOTH = ("cut", "cross")
VMEM = pl.BlockSpec(memory_space=pltpu.VMEM)
LIMIT = 32 * 1024 * 1024


def call(kernel, outs, operands, scratch=(), left=0, limit=LIMIT, outs_left=0):
    return pl.pallas_call(
        kernel,
        out_shape=outs,
        in_specs=[pl.BlockSpec(memory_space=pltpu.HBM)] * left + [VMEM] * (len(operands) - left),
        out_specs=[pl.BlockSpec(memory_space=pltpu.HBM)] * outs_left + [VMEM] * (len(outs) - outs_left),
        scratch_shapes=list(scratch),
        compiler_params=pltpu.CompilerParams(vmem_limit_bytes=limit),
    )(*operands)


class Either:
    def __init__(self, flag, yes, no):
        self.flag, self.yes, self.no = flag, yes, no
        self.shape = yes.shape

    def __getitem__(self, index):
        yes, no = self.yes[index], self.no[index]
        return jnp.where(jnp.full(yes.shape, self.flag, I32) > 0, yes, no)

    def part(self, index):
        return Either(self.flag, self.yes.at[index], self.no.at[index])


def is_odd(axis):
    return lax.rem(lax.axis_index(axis), 2)


def low_and_high(axis, even, odd):
    flag = is_odd(axis)
    return Either(flag, even, odd), Either(flag, odd, even)


def split(value):
    high = value.astype(BF16)
    return high, (value - high.astype(F32)).astype(BF16)


def iota(shape, dim):
    return lax.broadcasted_iota(I32, shape, dim)


RIM = 3
PAD = 8
QUARTERS = 4


def groups_of(count, most):
    return max(n for n in range(1, most + 1) if count % n == 0)


def difference_matrices(lanes):
    shape = (2 * lanes, 2 * lanes)
    given = iota(shape, 0) & (lanes - 1)
    wanted = iota(shape, 1)
    lower = wanted >= lanes
    wanted = wanted & (lanes - 1)
    beside = jnp.where(lower, wanted - 1, wanted + 1)
    neighbour = jnp.where(given == beside, 1.0, 0.0)
    same = jnp.where(given == wanted, 1.0, 0.0)
    return (neighbour - same).astype(BF16), (neighbour + same).astype(BF16)


def pieces_of(value):
    high, low = split(value)
    return jnp.concatenate([high, low], axis=1)


def conduct_pass(temp, kappa, cond, along_z, minus, plus, first, blocks, pitch):
    lanes = temp.shape[1]
    size = groups_of(blocks, 135)

    def body(n, unused):
        at = pl.ds(pl.multiple_of((first + n * size) * pitch, 8), size * pitch)
        t = temp[at, :]
        c = kappa[at, :] * (0.5 + 1.0 / (1.0 + t * t))
        cond[at, :] = c
        change = jnp.dot(pieces_of(t), minus[...], preferred_element_type=F32)
        both = jnp.dot(pieces_of(c), plus[...], preferred_element_type=F32)
        along_z[at, :] = change[:, :lanes] * both[:, :lanes] + change[:, lanes:] * both[:, lanes:]
        return unused

    lax.fori_loop(0, blocks // size, body, 0)


def flow_pass(temp, cond, along_z, first, blocks, pitch, most, put):
    size = groups_of(blocks, most)

    def rows_at(ref, base):
        return ref[pl.ds(base, pitch), :]

    def body(n, carried):
        t, c, flux = carried
        for k in range(size):
            block = first + n * size + k
            base = pl.multiple_of(block * pitch, 8)
            t_next = rows_at(temp, base + pitch)
            c_next = rows_at(cond, base + pitch)
            onward = (c + c_next) * (t_next - t)
            net = rows_at(along_z, base) + (onward - flux)
            for shift in (1, -1):
                net = net + (c + rows_at(cond, base + shift)) * (rows_at(temp, base + shift) - t)
            put(block, t + net)
            t, c, flux = t_next, c_next, onward
        return t, c, flux

    base = first * pitch
    t, c = rows_at(temp, base), rows_at(cond, base)
    flux = (c + rows_at(cond, base - pitch)) * (t - rows_at(temp, base - pitch))
    lax.fori_loop(0, blocks // size, body, (t, c, flux))


def rim_mask(pitch, lanes):
    place = iota((pitch, lanes), 0)
    side = lax.axis_index("cross")
    below = jnp.where(side > 0, 1.0, 0.0)
    above = jnp.where(side < lax.axis_size("cross") - 1, 1.0, 0.0)
    return jnp.where(place < PAD - RIM, above, jnp.where(place < PAD, below, 1.0))


def fill(flat, own, x_low, x_high, y_low, y_high, rows, scale):
    pitch = rows + PAD
    planes = own.shape[0] // rows
    flat[...] = jnp.zeros(flat.shape, F32)

    def place(p, part):
        flat[pl.ds(pl.multiple_of(p * pitch + PAD, 8), rows), :] = part * scale

    for n in range(RIM):
        place(n, x_low[n * rows : (n + 1) * rows, :])
        place(RIM + planes + n, x_high[n * rows : (n + 1) * rows, :])

    def body(p, unused):
        place(p + RIM, own[pl.ds(pl.multiple_of(p * rows, 8), rows), :])
        return unused

    lax.fori_loop(0, planes, body, 0, unroll=8)
    for r in range(RIM):
        below = PAD - RIM + r
        flat[pl.ds(RIM * pitch + below, planes, stride=pitch), :] = y_low[r, :, :] * scale
        flat[pl.ds((RIM + 1) * pitch + r, planes, stride=pitch), :] = y_high[r, :, :] * scale


def fill_corners(flat, first, low, high, rows, scale):
    pitch = rows + PAD
    for n in range(2 * RIM):
        block = n if n < RIM else first + n - RIM
        for r in range(RIM):
            below = block * pitch + PAD - RIM + r
            above = (block + 1) * pitch + r
            flat[below : below + 1, :] = low[r, n : n + 1, :] * scale
            flat[above : above + 1, :] = high[r, n : n + 1, :] * scale


def parcel_kernel(
    rows, temp, kappa, cells, watts, marks, pos, export, sent, even, odd, even_y, odd_y, code,
    cell_in, watt_in, mark_in, pos_in, export_in, temp_in, kappa_in, sems,
):
    count = pos.shape[1] // LANES
    exports = export.shape[0]
    wide = (even.shape[0] - 4 * exports) // 2
    height, lanes = temp.shape
    patch = height * lanes
    half, groups, _ = code.shape
    cap = half * LANES
    quarter = cap // QUARTERS
    moves = [(cells, cell_in), (watts, watt_in), (marks, mark_in), (pos, pos_in), (export, export_in)]
    tail = (1 - is_odd("cut")) * (height - wide)
    for n, field in enumerate((temp, kappa)):
        target = pl.ds(n * wide, wide)
        for out, start in ((even, tail), (odd, height - wide - tail)):
            moves.append((field.at[pl.ds(pl.multiple_of(start, 16), wide)], out.at[target]))
    moves += [(temp, temp_in), (kappa, kappa_in)]
    copies = [pltpu.make_async_copy(*move, sems.at[n]) for n, move in enumerate(moves)]
    for copy in copies:
        copy.start()
    for copy in copies[:3]:
        copy.wait()

    def by_group(ref):
        return jnp.concatenate([ref[pl.ds(h, groups, stride=half), :] for h in range(half)], axis=1)

    cell = by_group(cell_in)
    power = by_group(mark_in).astype(F32) * by_group(watt_in) * 0.5
    upper = cell >= patch
    cell = jnp.where(upper, cell - patch, cell)
    share = cell // (patch // QUARTERS)
    kind = jnp.where(upper, share + QUARTERS, share)
    members = [jnp.where(kind == k, 1.0, 0.0) for k in range(2 * QUARTERS)]
    earlier = jnp.where(iota((cap, cap), 0) < iota((cap, cap), 1), 1.0, 0.0).astype(BF16)
    before = jnp.dot(
        jnp.concatenate(members, axis=0).astype(BF16), earlier, preferred_element_type=F32
    )
    rank = jnp.zeros((groups, cap), F32)
    most = jnp.zeros((groups, 1), F32)
    for k, member in enumerate(members):
        ahead = before[k * groups : (k + 1) * groups]
        rank = rank + member * ahead
        most = jnp.maximum(most, ahead[:, cap - 1 :] + member[:, cap - 1 :])
    fits = jnp.broadcast_to(most, (groups, cap)) <= quarter
    region = share ^ is_odd("cross")
    slot = jnp.where(fits, region * quarter + rank.astype(I32), iota((groups, cap), 1))
    mark = jnp.where(upper, slot + cap, slot)
    for h in range(half):
        code[h] = mark[:, h * LANES : (h + 1) * LANES]
    number = cell + 1
    digits = [number & 255, lax.shift_right_logical(number, 8) & 255, lax.shift_right_logical(number, 16)]
    digits = [d.astype(F32) for d in digits]
    top = power.astype(BF16).astype(F32)
    middle = (power - top).astype(BF16).astype(F32)
    digits += [top, middle, power - top - middle]
    stacked = [jnp.where(upper, 0.0, d) for d in digits] + [jnp.where(upper, d, 0.0) for d in digits]
    stacked = jnp.concatenate(stacked, axis=0).astype(BF16)
    place = iota((16, cap), 0).astype(jnp.int16)
    one = jnp.ones((16, cap), BF16)
    of_group = iota((stacked.shape[0], cap), 0) & (groups - 1)
    moved = jnp.zeros(stacked.shape, F32)
    for j in range(groups):
        goes = jnp.broadcast_to(slot[j : j + 1], (16, cap)).astype(jnp.int16)
        swap = jnp.concatenate(
            [
                jnp.where(goes == place + jnp.int16(t * 16), one, jnp.zeros_like(one))
                for t in range(cap // 16)
            ],
            axis=0,
        )
        result = lax.dot_general(
            stacked, swap, (((1,), (1,)), ((), ())), preferred_element_type=F32
        )
        moved = jnp.where(of_group == j, result, moved)
    sign = jnp.where(fits, 1.0, -1.0)
    blocks = sent.shape[0] // (groups * 4 * half)
    for kind in range(2):
        part = [
            moved[(6 * kind + n) * groups : (6 * kind + n + 1) * groups] for n in range(6)
        ]
        numbers = (part[0] + 256.0 * part[1] + 65536.0 * part[2]) * sign
        powers = part[3] + part[4] + part[5]
        for n, value in enumerate((numbers, powers)):
            for h in range(half):
                row = kind * 2 * half + n * half + h
                for block in range(blocks):
                    at = pl.ds(block * groups * 4 * half + row, groups, stride=4 * half)
                    sent[at, :] = value[:, h * LANES : (h + 1) * LANES]
    for copy in copies[3:5]:
        copy.wait()
    index = export_in[...]
    codes = [
        mark[j : j + 1, h * LANES : (h + 1) * LANES].astype(F32)
        for j in range(groups)
        for h in range(half)
    ]
    ghost = pick([rows_of(pos_in, ch) for ch in range(3)] + [codes], index)
    ghost[3] = (index // cap * (2 * cap) + ghost[3].astype(I32)).astype(F32)
    for out in (even, odd):
        for n, value in enumerate(ghost):
            out[2 * wide + n * exports : 2 * wide + (n + 1) * exports, :] = value
    for copy in copies[5:]:
        copy.wait()
    top = (1 - is_odd("cross")) * (rows - RIM)
    for n, own in enumerate((temp_in, kappa_in)):
        for r in range(RIM):
            for out, first in ((even_y, top), (odd_y, rows - RIM - top)):
                out[n * RIM + r] = own[pl.ds(first + r, height // rows, stride=rows), :]


def corner_kernel(rows, even_s, odd_s, even_x, odd_x, even, odd):
    side = RIM * rows
    low, high = low_and_high("cut", even_x, odd_x)
    top = (1 - is_odd("cross")) * (rows - RIM)
    base = even_s.shape[0]
    for out, strips, first in ((even, even_s, top), (odd, odd_s, rows - RIM - top)):
        out[:base, :] = strips[...]
        for n in range(2 * RIM):
            for p in range(RIM):
                at = pl.ds(n // RIM * side + p * rows + first + n % RIM, 1)
                to = base + n * PAD + p
                out[to : to + 1, :] = low[at, :]
                out[to + RIM : to + RIM + 1, :] = high[at, :]
            out[base + n * PAD + 2 * RIM : base + (n + 1) * PAD, :] = jnp.zeros((PAD - 2 * RIM, LANES), F32)


class Rows:
    def __init__(self, ref, base, size):
        self.ref, self.base, self.size = ref, base, size

    def __getitem__(self, index):
        r, at, lanes = index
        first = self.base + r * self.size
        return self.ref[first + (at.start or 0) : first + (self.size if at.stop is None else at.stop), :]


ENDS = 2 * RIM


def open_kernel(
    rows, after, temp, kappa_own, even_x, odd_x, even_y, odd_y,
    opened, kappa, ends, now, cond, along_z, minus, plus,
):
    lanes = temp.shape[1]
    pitch = rows + PAD
    planes = temp.shape[0] // rows
    blocks = planes + 2 * RIM + 1
    side = RIM * rows
    x_low, x_high = low_and_high("cut", even_x, odd_x)
    y_low, y_high = low_and_high("cross", even_y, odd_y)
    minus[...], plus[...] = difference_matrices(lanes)
    for n, (flat, own, scale) in enumerate(((now, temp, 1.0), (kappa, kappa_own, 0.5))):
        beside = [half.part(slice(n * side, (n + 1) * side)) for half in (x_low, x_high)]
        strips = [half.part(slice(n * RIM, (n + 1) * RIM)) for half in (y_low, y_high)]
        fill(flat, own, *beside, *strips, rows, scale)
    size = ENDS * pitch
    ends[:size, :] = now[:size, :]
    ends[size:, :] = now[(blocks - ENDS) * pitch : blocks * pitch, :]
    conduct_pass(now, kappa, cond, along_z, minus, plus, 0, blocks, pitch)
    opened[0:pitch, :] = jnp.zeros((pitch, lanes), F32)
    opened[(blocks - 1) * pitch :, :] = jnp.zeros((opened.shape[0] - (blocks - 1) * pitch, lanes), F32)

    def put(block, value):
        opened[pl.ds(pl.multiple_of(block * pitch, 8), pitch), :] = value

    flow_pass(now, cond, along_z, 1, blocks - 2, pitch, 1000, put)


def heat_kernel(
    got, opened, kappa_in, ends_in, source_own, even_s, odd_s,
    temp_out, looked, source, kappa, ends, ends_kappa, now, then, cond, along_z, minus, plus, pieces,
    result, sem,
):
    lanes = kappa.shape[1]
    planes, rows, _ = result.shape
    pitch = rows + PAD
    total = planes + 2 * RIM
    blocks = total + 1
    wide = RIM - 1
    s_low, s_high = low_and_high("cross", even_s, odd_s)
    height = -(-total // 8) * 8
    minus[...], plus[...] = difference_matrices(lanes)
    source[...] = source_own[...]
    for first, half in ((PAD - wide, s_low), (PAD + rows, s_high)):
        strips = Rows(half, 0, height)
        for r in range(wide):
            source[pl.ds(first + r, total, stride=pitch), :] = strips[r, :total, :]
    mask = rim_mask(pitch, lanes)

    corners = [
        [Rows(half, wide * height + n * RIM * PAD, PAD) for half in (s_low, s_high)] for n in range(2)
    ]
    size = ENDS * pitch
    last_end = blocks - ENDS
    ends[: 2 * size, :] = ends_in[...]
    ends[2 * size :, :] = jnp.zeros((pitch, lanes), F32)
    fill_corners(ends, 2 * ENDS - RIM - 1, *corners[0], rows, 1.0)
    kappa[...] = kappa_in[...]
    fill_corners(kappa, blocks - RIM - 1, *corners[1], rows, 0.5)
    ends_kappa[:size, :] = kappa[:size, :]
    ends_kappa[size : 2 * size, :] = kappa[last_end * pitch : blocks * pitch, :]
    conduct_pass(ends, ends_kappa, cond, along_z, minus, plus, 0, 2 * ENDS, pitch)
    then[0:pitch, :] = jnp.zeros((pitch, lanes), F32)
    then[(blocks - 1) * pitch :, :] = jnp.zeros((then.shape[0] - (blocks - 1) * pitch, lanes), F32)
    for n in range(1, blocks - 1):
        if not (1 <= n < ENDS - 1 or last_end + 1 <= n):
            at = pl.ds(n * pitch, pitch)
            then[at, :] = (opened[at, :] + source[at, :]) * mask
    for first, to in ((1, 1), (ENDS + 1, last_end + 1)):

        def again(block, value, first=first, to=to):
            at = pl.ds((block - first + to) * pitch, pitch)
            then[at, :] = (value + source[at, :]) * mask

        flow_pass(ends, cond, along_z, first, ENDS - 2, pitch, 1000, again)

    now[0:pitch, :] = jnp.zeros((pitch, lanes), F32)
    now[(blocks - 1) * pitch :, :] = jnp.zeros((now.shape[0] - (blocks - 1) * pitch, lanes), F32)
    conduct_pass(then, kappa, cond, along_z, minus, plus, 0, blocks, pitch)

    def middle(block, value):
        at = pl.ds(pl.multiple_of(block * pitch, 8), pitch)
        now[at, :] = (value + source[at, :]) * mask

    flow_pass(then, cond, along_z, 1, blocks - 2, pitch, 1000, middle)
    conduct_pass(now, kappa, cond, along_z, minus, plus, 0, blocks, pitch)

    def last(block, value):
        at = pl.ds(pl.multiple_of(block * pitch, 8), pitch)
        result[block - RIM] = (value + source[at, :])[PAD:]

    flow_pass(now, cond, along_z, RIM, planes, pitch, 1000, last)
    copy = pltpu.make_async_copy(result, temp_out, sem)
    copy.start()
    height = planes * rows
    for first in range(0, planes, lanes // rows):
        turned = result[first : first + lanes // rows].reshape(lanes, lanes).T
        high, low = split(turned)
        pieces[:lanes, first * rows : first * rows + lanes] = high
        pieces[lanes:, first * rows : first * rows + lanes] = low
    lookup(lax.axis_index("cut"), got, height, lanes, rows, looked, pieces)
    copy.wait()


def paired(got, block, kind, row, s):
    at = kind * (got.shape[2] // 2) + row
    first = got[block, s, pl.ds(at, 1), :]
    second = got[block, s + 1, pl.ds(at, 1), :]
    left = iota((1, LANES), 1) < LANES // 2
    return jnp.where(left, first, second), jnp.where(left, second, first)


def cell_of(number):
    return jnp.abs(number).astype(I32) - 1


def unsorted(got):
    half = got.shape[2] // 4
    lowest = jnp.minimum(got[:, :, :half, :], got[:, :, 2 * half : 3 * half, :])
    return jnp.min(lowest) < 0.0


def deposit_kernel(planes, got, source, even, odd, spread, across, plane_of):
    blocks, groups, rows_sent, _ = got.shape
    half = rows_sent // 4
    lanes = source.shape[1]
    rows = across.shape[0]
    pitch = rows + PAD
    here = lax.axis_index("cut")
    place = iota((rows, LANES), 0)
    place16 = place.astype(jnp.int16)
    zero = jnp.zeros((rows, LANES), BF16)
    pairs = groups // 2
    tile = planes // QUARTERS
    region = 2 * pairs * LANES
    inside = QUARTERS * region
    wide = RIM - 1

    def block(distance):
        return lax.rem(here + (blocks + distance), blocks)

    def fill_columns(at, number, power):
        span = pl.ds(pl.multiple_of(at, LANES), LANES)
        cell = cell_of(jnp.broadcast_to(number, (rows, LANES)))
        high, low = split(jnp.broadcast_to(power, (rows, LANES)))
        lane = (cell & (lanes - 1)).astype(jnp.int16)
        for t in range(lanes // rows):
            hit = lane == place16 + jnp.int16(t * rows)
            spread[t * rows : (t + 1) * rows, span] = jnp.where(hit, high, zero)
            spread[lanes + t * rows : lanes + (t + 1) * rows, span] = jnp.where(hit, low, zero)
        row = lax.shift_right_arithmetic(cell, 7)
        across[:, span] = jnp.where((row & (rows - 1)) == place, 1.0, 0.0).astype(BF16)
        plane_of[:, span] = lax.shift_right_arithmetic(row, rows.bit_length() - 1).astype(jnp.int16)

    def sides(pair, quarter_high, quarter_low):
        for n, (distance, kind) in enumerate(((1, 0), (0, 1), (-1, 0), (-2, 1))):
            share = quarter_high if n < 2 else quarter_low
            h, which = share // 2, share % 2
            number = paired(got, block(distance), kind, h, 2 * pair)[which]
            power = paired(got, block(distance), kind, half + h, 2 * pair)[which]
            fill_columns(inside + (n * pairs + pair) * LANES, number, power)

    def fill_pair(pair, unused):
        for part in range(2):
            for h in range(half):
                numbers = paired(got, block(-part), part, h, 2 * pair)
                powers = paired(got, block(-part), part, half + h, 2 * pair)
                for which in range(2):
                    at = (2 * h + which) * region + (part * pairs + pair) * LANES
                    fill_columns(at, numbers[which], powers[which])
        sides(pair, 0, QUARTERS - 1)
        return unused

    lax.fori_loop(0, pairs, fill_pair, 0, unroll=True)
    blocks_all = source.shape[0] // pitch
    for n in range(blocks_all):
        inner = 1 <= n < planes + 2 * RIM - 1
        end = PAD if inner else pitch
        source[n * pitch : n * pitch + end, :] = jnp.zeros((end, lanes), F32)

    def product(first, base, count, columns, added=False):
        where_y = across[:, columns]
        where_x = plane_of[:, columns] - jnp.asarray(base, I32).astype(jnp.int16)
        nothing = jnp.zeros_like(where_y)
        hot = jnp.concatenate(
            [jnp.where(where_x == jnp.int16(x), where_y, nothing) for x in range(count)], axis=0
        )
        both = lax.dot_general(
            hot, spread[:, columns], (((1,), (1,)), ((), ())), preferred_element_type=F32
        )
        value = both[:, :lanes] + both[:, lanes:]
        for n in range(count):
            at = pl.ds(pl.multiple_of((first + n + RIM) * pitch + PAD, 8), rows)
            part = value[n * rows : (n + 1) * rows]
            source[at, :] = source[at, :] + part if added else part

    for q in range(QUARTERS):
        product(q * tile, q * tile, tile, slice(q * region, (q + 1) * region))

    def outside(added):
        product(planes, 0, wide, slice(inside, inside + region), added)
        product(-wide, planes - wide, wide, slice(inside + region, inside + 2 * region), added)

    outside(False)

    @pl.when(unsorted(got))
    def _():
        def whole(m, unused):
            product(m * tile, m * tile, tile, slice(0, inside))
            return unused

        lax.fori_loop(0, QUARTERS, whole, 0)
        for step in range(1, QUARTERS):

            def others(pair, unused, step=step):
                sides(pair, step, QUARTERS - 1 - step)
                return unused

            lax.fori_loop(0, pairs, others, 0)
            outside(True)

    planes_all = planes + 2 * RIM
    top = (1 - is_odd("cross")) * (rows - wide)
    for r in range(wide):
        for out, first in ((even, top), (odd, rows - wide - top)):
            at = r * (out.shape[0] // wide)
            out[at : at + planes_all, :] = source[pl.ds(PAD + first + r, planes_all, stride=pitch), :]


def lookup(me, got, height, lanes, rows, looked, pieces):
    blocks, groups, rows_sent, _ = got.shape
    half = rows_sent // 4
    pairs = groups // 2
    shift = rows.bit_length() - 1
    place = iota((rows, LANES), 0)
    lane_place = iota((lanes, LANES), 0)
    zero = jnp.zeros((rows, LANES), BF16)

    def search(numbers, base, size):
        hots = []
        for number in numbers:
            row = lax.shift_right_arithmetic(cell_of(jnp.broadcast_to(number, (rows, LANES))), 7)
            plane = lax.shift_right_arithmetic(row, shift).astype(jnp.int16)
            hot_row = jnp.where((row & (rows - 1)) == place, 1.0, 0.0).astype(BF16)
            hots.append(
                jnp.concatenate(
                    [
                        jnp.where(plane == jnp.int16(x), hot_row, zero)
                        for x in range(base // rows, (base + size) // rows)
                    ],
                    axis=0,
                )
            )
        both = jnp.dot(
            pieces[:, base : base + size],
            jnp.concatenate(hots, axis=1),
            preferred_element_type=F32,
        )
        value = both[:lanes] + both[lanes:]
        results = []
        for n, number in enumerate(numbers):
            lane = cell_of(jnp.broadcast_to(number, (lanes, LANES))) & (lanes - 1)
            part = jnp.where(lane == lane_place, value[:, n * LANES : (n + 1) * LANES], 0.0)
            results.append(jnp.sum(part, axis=0, keepdims=True))
        return results

    left = iota((1, LANES), 1) < LANES // 2

    def run(full):
        for h in range(half):
            found = []
            for which in range(2):
                numbers = []
                for part in range(2):
                    block = lax.rem(me + (blocks - part), blocks)
                    for pair in range(pairs):
                        numbers.append(paired(got, block, part, h, 2 * pair)[which])
                size = height // QUARTERS
                found.append(
                    search(numbers, 0, height) if full else search(numbers, (2 * h + which) * size, size)
                )
            for part in range(2):
                for pair in range(pairs):
                    a, b = (f[part * pairs + pair] for f in found)
                    for s, value in ((0, jnp.where(left, a, b)), (1, jnp.where(left, b, a))):
                        row = (2 * pair + s) * 2 * half + part * half + h
                        for block in range(blocks):
                            at = block * groups * 2 * half + row
                            looked[at : at + 1, :] = value

    run(False)

    @pl.when(unsorted(got))
    def _():
        run(True)


def pick(tables, index):
    row = lax.shift_right_logical(index, 7)
    lane = index & (LANES - 1)
    results = [jnp.zeros(index.shape, F32) for _ in tables]
    for r in range(len(tables[0])):
        here = row == r
        for ch, rows in enumerate(tables):
            value = jnp.take_along_axis(jnp.broadcast_to(rows[r], index.shape), lane, axis=1)
            results[ch] = jnp.where(here, value, results[ch])
    return results


def rows_of(ref, ch):
    return [ref[ch : ch + 1, r * LANES : (r + 1) * LANES] for r in range(ref.shape[1] // LANES)]


def stretch_kernel(
    side, after, pos, acted, other, gap, snapped, even_x, odd_x, base, slope, delta, hot, ghost,
):
    exports = ghost.shape[1]
    low_ghost, high_ghost = low_and_high("cut", even_x, odd_x)

    def ghosts(n, ref):
        ghost[n] = ref[side + 3 * exports : side + 4 * exports, :].astype(I32)
        places = ref[side : side + 3 * exports, :]
        return [[places[ch * exports + r : ch * exports + r + 1] for r in range(exports)] for ch in range(3)]

    own = [rows_of(pos, ch) for ch in range(3)]
    low = ghosts(0, low_ghost)
    high = ghosts(1, high_ghost)
    first = pick(own, acted[...])
    second = pick([own[ch] + low[ch] + high[ch] for ch in range(3)], other[...])
    d = [second[ch] - first[ch] for ch in range(3)]
    dist = jnp.sqrt(d[0] * d[0] + d[1] * d[1] + d[2] * d[2])
    weight = (1.0 - snapped[...].astype(F32)) / jnp.maximum(dist, 0.3)
    base[...] = weight * (dist - gap[...])
    slope[...] = weight * (gap[...] * (0.2 * 0.5))
    for ch in range(3):
        delta[ch] = d[ch]
    place = iota((16, LANES), 0).astype(jnp.int16)
    one = jnp.ones((16, LANES), BF16)
    for r in range(acted.shape[0]):
        lane = jnp.broadcast_to(acted[r : r + 1, :] & (LANES - 1), (16, LANES)).astype(jnp.int16)
        for t in range(LANES // 16):
            hot[t * 16 : (t + 1) * 16, r * LANES : (r + 1) * LANES] = jnp.where(
                lane == place + jnp.int16(t * 16), one, jnp.zeros_like(one)
            )


def bond_kernel(
    blocks, back, code, pos, vel, acted, other, ghost, base, slope, delta, hot, pos_out, vel_out, force,
):
    half, groups, _ = code.shape
    here = lax.axis_index("cut")
    double = 2 * half

    def slots(distance):
        found = []
        for kind in range(2):
            block = lax.rem(here + (blocks + distance + kind), blocks)
            for h in range(half):
                first = block * groups * double + kind * half + h
                found.append(back[pl.ds(first, groups, stride=double), :])
        return found

    def ghosts(n, distance):
        rows = slots(distance)
        table = [rows[k][j : j + 1] for j in range(groups) for k in range(double)]
        found = pick([table], ghost[n])[0]
        return [found[r : r + 1] for r in range(found.shape[0])]

    rows = slots(0)
    temps = []
    for h in range(half):
        index = code[h]
        temp = jnp.zeros(index.shape, F32)
        for k in range(double):
            value = jnp.take_along_axis(rows[k], index & (LANES - 1), axis=1)
            temp = jnp.where(lax.shift_right_logical(index, 7) == k, value, temp)
        temps.append(temp)
    own = [temps[h][j : j + 1] for j in range(groups) for h in range(half)]
    first = pick([own], acted[...])[0]
    second = pick([own + ghosts(0, -1) + ghosts(1, 1)], other[...])[0]
    scale = base[...] - slope[...] * (first + second)
    values = [split(scale * delta[ch]) for ch in range(3)]
    values = [piece.astype(F32) for pair in values for piece in pair]
    high_count = len(own)
    high_place = iota((high_count, LANES), 0)
    for r in range(acted.shape[0]):
        span = slice(r * LANES, (r + 1) * LANES)
        at_row = lax.shift_right_logical(acted[r : r + 1, :], 7) == high_place
        for n, value in enumerate(values):
            force[n * high_count : (n + 1) * high_count, span] = jnp.where(
                at_row, jnp.broadcast_to(value[r : r + 1], (high_count, LANES)), 0.0
            ).astype(BF16)
    total = lax.dot_general(
        force[...], hot[...], (((1,), (1,)), ((), ())), preferred_element_type=F32
    )
    for ch in range(3):
        base_row = 2 * ch * high_count
        summed = (
            total[base_row : base_row + high_count]
            + total[base_row + high_count : base_row + 2 * high_count]
        )
        for r in range(high_count):
            span = slice(r * LANES, (r + 1) * LANES)
            velocity = vel[ch : ch + 1, span] + 0.5 * summed[r : r + 1]
            vel_out[ch : ch + 1, span] = velocity
            pos_out[ch : ch + 1, span] = pos[ch : ch + 1, span] + 0.5 * velocity


def swaps(axis, closed, even, odd):
    count = lax.axis_size(axis)
    results = []
    for first, block in ((0, even), (1, odd)):
        pairs = []
        for i in range(first, count if closed else count - 1, 2):
            pairs += [(i, (i + 1) % count), ((i + 1) % count, i)]
        results.append(lax.ppermute(block, axis, pairs))
    return results


def per_device(
    warming_above_ambient,
    fourier_stability_factor,
    patch_locator,
    photon_gain_wattage,
    on_skin_marker,
    grain_placements,
    grain_motion_parts,
    tether_acted_grain,
    tether_other_grain,
    tether_relaxed_gap,
    snapped_marker,
    exported_copies,
):
    planes, rows, lanes = warming_above_ambient.shape
    temp = warming_above_ambient.reshape(planes * rows, lanes)
    kappa = fourier_stability_factor.reshape(planes * rows, lanes)
    blocks = lax.axis_size("cut")
    groups = lax.axis_size("cross")
    count = patch_locator.shape[0]
    half = count // groups // LANES
    pitch = rows + PAD
    total = planes + 2 * RIM
    flat = jax.ShapeDtypeStruct(((total + 2) * pitch, lanes), F32)
    wide = RIM * rows

    exports = exported_copies.shape[0] // LANES
    carried = jax.ShapeDtypeStruct((2 * wide + 4 * exports, LANES), F32)
    devices = blocks * groups
    strips = jax.ShapeDtypeStruct((2 * RIM, planes, lanes), F32)
    whole = pltpu.VMEM(temp.shape, F32)
    sent, even_x, odd_x, even_y, odd_y, code = call(
        functools.partial(parcel_kernel, rows),
        [
            jax.ShapeDtypeStruct((devices * 4 * half, LANES), F32),
            carried,
            carried,
            strips,
            strips,
            jax.ShapeDtypeStruct((half, groups, LANES), I32),
        ],
        [
            temp,
            kappa,
            patch_locator.reshape(-1, LANES),
            photon_gain_wattage.reshape(-1, LANES),
            on_skin_marker.reshape(-1, LANES),
            grain_placements,
            exported_copies.reshape(-1, LANES),
        ],
        [
            pltpu.VMEM((count // LANES, LANES), I32),
            pltpu.VMEM((count // LANES, LANES), F32),
            pltpu.VMEM((count // LANES, LANES), I32),
            pltpu.VMEM(grain_placements.shape, F32),
            pltpu.VMEM((exports, LANES), I32),
            whole,
            whole,
            pltpu.SemaphoreType.DMA((11,)),
        ],
        left=7,
        limit=None,
    )

    def exchange(sent):
        sent = sent.reshape(devices, -1, LANES)
        return lax.all_to_all(sent, BOTH, split_axis=0, concat_axis=0, tiled=True)

    got = exchange(sent).reshape(blocks, groups, 4 * half, LANES)
    even_x, odd_x = swaps("cut", True, even_x, odd_x)

    even_y, odd_y = swaps("cross", False, even_y, odd_y)

    strips = jax.ShapeDtypeStruct(((RIM - 1) * (-(-total // 8) * 8), lanes), F32)
    entries = 2 * count + 4 * count // QUARTERS
    source, even_s, odd_s = call(
        functools.partial(deposit_kernel, planes),
        [flat, strips, strips],
        [got],
        [
            pltpu.VMEM((2 * lanes, entries), BF16),
            pltpu.VMEM((rows, entries), BF16),
            pltpu.VMEM((rows, entries), jnp.int16),
        ],
    )
    corners = jax.ShapeDtypeStruct((strips.shape[0] + 2 * RIM * PAD, lanes), F32)
    even_s, odd_s = call(
        functools.partial(corner_kernel, rows), [corners, corners], [even_s, odd_s, even_x, odd_x]
    )
    sent_strips = even_s
    even_s, odd_s = swaps("cross", False, even_s, odd_s)

    grid = pltpu.VMEM(flat.shape, F32)
    matrix = pltpu.VMEM((2 * lanes, 2 * lanes), BF16)
    ends = jax.ShapeDtypeStruct((2 * ENDS * pitch, lanes), F32)
    opened, kappa, ends = call(
        functools.partial(open_kernel, rows),
        [flat, flat, ends],
        [sent_strips, temp, kappa, even_x, odd_x, even_y, odd_y],
        [grid, grid, grid, matrix, matrix],
        left=1,
    )
    ends_grid = pltpu.VMEM((2 * ENDS * pitch + pitch, lanes), F32)
    temp, looked = call(
        heat_kernel,
        [
            jax.ShapeDtypeStruct((planes, rows, lanes), F32),
            jax.ShapeDtypeStruct((devices * 2 * half, LANES), F32),
        ],
        [got, opened, kappa, ends, source, even_s, odd_s],
        [
            grid, grid, ends_grid, ends_grid, grid, grid, grid, grid, matrix, matrix,
            pltpu.VMEM((2 * lanes, planes * rows), BF16),
            pltpu.VMEM((planes, rows, lanes), F32),
            pltpu.SemaphoreType.DMA,
        ],
        outs_left=1,
    )
    back = exchange(looked).reshape(looked.shape)
    acted = tether_acted_grain.reshape(-1, LANES)
    other = tether_other_grain.reshape(-1, LANES)
    entry = jax.ShapeDtypeStruct(acted.shape, F32)
    base, slope, delta, hot, ghost = call(
        functools.partial(stretch_kernel, 2 * wide),
        [
            entry,
            entry,
            jax.ShapeDtypeStruct((3,) + acted.shape, F32),
            jax.ShapeDtypeStruct((LANES, acted.size), BF16),
            jax.ShapeDtypeStruct((2, exports, LANES), I32),
        ],
        [
            looked,
            grain_placements,
            acted,
            other,
            tether_relaxed_gap.reshape(-1, LANES),
            snapped_marker.reshape(-1, LANES),
            even_x,
            odd_x,
        ],
        left=1,
    )
    out = jax.ShapeDtypeStruct(grain_placements.shape, F32)
    positions_new, velocities_new = call(
        functools.partial(bond_kernel, blocks),
        [out, out],
        [
            back, code, grain_placements, grain_motion_parts, acted, other, ghost,
            base, slope, delta, hot,
        ],
        [pltpu.VMEM((6 * (count // LANES), acted.size), BF16)],
    )
    return (temp, positions_new, velocities_new)


def solution(mesh):
    return jax.shard_map(
        per_device,
        mesh=mesh,
        in_specs=(
            P("cut", "cross", None),
            P("cut", "cross", None),
            P(("cut", "cross")),
            P(("cut", "cross")),
            P(("cut", "cross")),
            P(None, ("cut", "cross")),
            P(None, ("cut", "cross")),
            P(("cut", "cross")),
            P(("cut", "cross")),
            P(("cut", "cross")),
            P(("cut", "cross")),
            P(("cut", "cross")),
        ),
        out_specs=(P("cut", "cross", None), P(None, ("cut", "cross")), P(None, ("cut", "cross"))),
        check_vma=False,
    )
```

```python
import functools

import jax
import jax.numpy as jnp
from jax import lax
from jax.experimental import pallas as pl
from jax.experimental.pallas import tpu as pltpu
from jax.sharding import PartitionSpec as P

F32 = jnp.float32
BF16 = jnp.bfloat16
I32 = jnp.int32
LANES = 128
BOTH = ("cut", "cross")
VMEM = pl.BlockSpec(memory_space=pltpu.VMEM)
LIMIT = 32 * 1024 * 1024


def call(kernel, outs, operands, scratch=(), left=0, limit=LIMIT, outs_left=0):
    return pl.pallas_call(
        kernel,
        out_shape=outs,
        in_specs=[pl.BlockSpec(memory_space=pltpu.HBM)] * left + [VMEM] * (len(operands) - left),
        out_specs=[pl.BlockSpec(memory_space=pltpu.HBM)] * outs_left + [VMEM] * (len(outs) - outs_left),
        scratch_shapes=list(scratch),
        compiler_params=pltpu.CompilerParams(vmem_limit_bytes=limit),
    )(*operands)


class Either:
    def __init__(self, flag, yes, no):
        self.flag, self.yes, self.no = flag, yes, no
        self.shape = yes.shape

    def __getitem__(self, index):
        yes, no = self.yes[index], self.no[index]
        return jnp.where(jnp.full(yes.shape, self.flag, I32) > 0, yes, no)

    def part(self, index):
        return Either(self.flag, self.yes.at[index], self.no.at[index])


def is_odd(axis):
    return lax.rem(lax.axis_index(axis), 2)


def low_and_high(axis, even, odd):
    flag = is_odd(axis)
    return Either(flag, even, odd), Either(flag, odd, even)


def split(value):
    high = value.astype(BF16)
    return high, (value - high.astype(F32)).astype(BF16)


def iota(shape, dim):
    return lax.broadcasted_iota(I32, shape, dim)


RIM = 3
PAD = 8
QUARTERS = 4


def groups_of(count, most):
    return max(n for n in range(1, most + 1) if count % n == 0)


def difference_matrices(lanes):
    shape = (2 * lanes, 2 * lanes)
    given = iota(shape, 0) & (lanes - 1)
    wanted = iota(shape, 1)
    lower = wanted >= lanes
    wanted = wanted & (lanes - 1)
    beside = jnp.where(lower, wanted - 1, wanted + 1)
    neighbour = jnp.where(given == beside, 1.0, 0.0)
    same = jnp.where(given == wanted, 1.0, 0.0)
    return (neighbour - same).astype(BF16), (neighbour + same).astype(BF16)


def pieces_of(value):
    high, low = split(value)
    return jnp.concatenate([high, low], axis=1)


def conduct_pass(temp, kappa, cond, along_z, minus, plus, first, blocks, pitch):
    lanes = temp.shape[1]
    size = groups_of(blocks, 135)

    def body(n, unused):
        at = pl.ds(pl.multiple_of((first + n * size) * pitch, 8), size * pitch)
        t = temp[at, :]
        c = kappa[at, :] * (0.5 + 1.0 / (1.0 + t * t))
        cond[at, :] = c
        change = jnp.dot(pieces_of(t), minus[...], preferred_element_type=F32)
        both = jnp.dot(pieces_of(c), plus[...], preferred_element_type=F32)
        along_z[at, :] = change[:, :lanes] * both[:, :lanes] + change[:, lanes:] * both[:, lanes:]
        return unused

    lax.fori_loop(0, blocks // size, body, 0)


def flow_pass(temp, cond, along_z, first, blocks, pitch, most, put):
    size = groups_of(blocks, most)

    def rows_at(ref, base):
        return ref[pl.ds(base, pitch), :]

    def body(n, carried):
        t, c, flux = carried
        for k in range(size):
            block = first + n * size + k
            base = pl.multiple_of(block * pitch, 8)
            t_next = rows_at(temp, base + pitch)
            c_next = rows_at(cond, base + pitch)
            onward = (c + c_next) * (t_next - t)
            net = rows_at(along_z, base) + (onward - flux)
            for shift in (1, -1):
                net = net + (c + rows_at(cond, base + shift)) * (rows_at(temp, base + shift) - t)
            put(block, t + net)
            t, c, flux = t_next, c_next, onward
        return t, c, flux

    base = first * pitch
    t, c = rows_at(temp, base), rows_at(cond, base)
    flux = (c + rows_at(cond, base - pitch)) * (t - rows_at(temp, base - pitch))
    lax.fori_loop(0, blocks // size, body, (t, c, flux))


def rim_mask(pitch, lanes):
    place = iota((pitch, lanes), 0)
    side = lax.axis_index("cross")
    below = jnp.where(side > 0, 1.0, 0.0)
    above = jnp.where(side < lax.axis_size("cross") - 1, 1.0, 0.0)
    return jnp.where(place < PAD - RIM, above, jnp.where(place < PAD, below, 1.0))


def fill(flat, own, x_low, x_high, y_low, y_high, rows, scale):
    pitch = rows + PAD
    planes = own.shape[0] // rows
    flat[...] = jnp.zeros(flat.shape, F32)

    def place(p, part):
        flat[pl.ds(pl.multiple_of(p * pitch + PAD, 8), rows), :] = part * scale

    for n in range(RIM):
        place(n, x_low[n * rows : (n + 1) * rows, :])
        place(RIM + planes + n, x_high[n * rows : (n + 1) * rows, :])

    def body(p, unused):
        place(p + RIM, own[pl.ds(pl.multiple_of(p * rows, 8), rows), :])
        return unused

    lax.fori_loop(0, planes, body, 0, unroll=8)
    for r in range(RIM):
        below = PAD - RIM + r
        flat[pl.ds(RIM * pitch + below, planes, stride=pitch), :] = y_low[r, :, :] * scale
        flat[pl.ds((RIM + 1) * pitch + r, planes, stride=pitch), :] = y_high[r, :, :] * scale


def fill_corners(flat, first, low, high, rows, scale):
    pitch = rows + PAD
    for n in range(2 * RIM):
        block = n if n < RIM else first + n - RIM
        for r in range(RIM):
            below = block * pitch + PAD - RIM + r
            above = (block + 1) * pitch + r
            flat[below : below + 1, :] = low[r, n : n + 1, :] * scale
            flat[above : above + 1, :] = high[r, n : n + 1, :] * scale


def parcel_kernel(
    rows, temp, kappa, cells, watts, marks, pos, export, sent, even, odd, even_y, odd_y, code,
    cell_in, watt_in, mark_in, pos_in, export_in, temp_in, kappa_in, sems,
):
    count = pos.shape[1] // LANES
    exports = export.shape[0]
    wide = (even.shape[0] - 4 * exports) // 2
    height, lanes = temp.shape
    patch = height * lanes
    half, groups, _ = code.shape
    cap = half * LANES
    quarter = cap // QUARTERS
    moves = [(cells, cell_in), (watts, watt_in), (marks, mark_in), (pos, pos_in), (export, export_in)]
    tail = (1 - is_odd("cut")) * (height - wide)
    for n, field in enumerate((temp, kappa)):
        target = pl.ds(n * wide, wide)
        for out, start in ((even, tail), (odd, height - wide - tail)):
            moves.append((field.at[pl.ds(pl.multiple_of(start, 16), wide)], out.at[target]))
    moves += [(temp, temp_in), (kappa, kappa_in)]
    copies = [pltpu.make_async_copy(*move, sems.at[n]) for n, move in enumerate(moves)]
    for copy in copies:
        copy.start()
    for copy in copies[:3]:
        copy.wait()

    def by_group(ref):
        return jnp.concatenate([ref[pl.ds(h, groups, stride=half), :] for h in range(half)], axis=1)

    cell = by_group(cell_in)
    power = by_group(mark_in).astype(F32) * by_group(watt_in) * 0.5
    upper = cell >= patch
    cell = jnp.where(upper, cell - patch, cell)
    share = cell // (patch // QUARTERS)
    kind = jnp.where(upper, share + QUARTERS, share)
    members = [jnp.where(kind == k, 1.0, 0.0) for k in range(2 * QUARTERS)]
    earlier = jnp.where(iota((cap, cap), 0) < iota((cap, cap), 1), 1.0, 0.0).astype(BF16)
    before = jnp.dot(
        jnp.concatenate(members, axis=0).astype(BF16), earlier, preferred_element_type=F32
    )
    rank = jnp.zeros((groups, cap), F32)
    most = jnp.zeros((groups, 1), F32)
    for k, member in enumerate(members):
        ahead = before[k * groups : (k + 1) * groups]
        rank = rank + member * ahead
        most = jnp.maximum(most, ahead[:, cap - 1 :] + member[:, cap - 1 :])
    fits = jnp.broadcast_to(most, (groups, cap)) <= quarter
    region = share ^ is_odd("cross")
    slot = jnp.where(fits, region * quarter + rank.astype(I32), iota((groups, cap), 1))
    mark = jnp.where(upper, slot + cap, slot)
    for h in range(half):
        code[h] = mark[:, h * LANES : (h + 1) * LANES]
    number = cell + 1
    digits = [number & 255, lax.shift_right_logical(number, 8) & 255, lax.shift_right_logical(number, 16)]
    digits = [d.astype(F32) for d in digits]
    top = power.astype(BF16).astype(F32)
    middle = (power - top).astype(BF16).astype(F32)
    digits += [top, middle, power - top - middle]
    stacked = [jnp.where(upper, 0.0, d) for d in digits] + [jnp.where(upper, d, 0.0) for d in digits]
    stacked = jnp.concatenate(stacked, axis=0).astype(BF16)
    place = iota((16, cap), 0).astype(jnp.int16)
    one = jnp.ones((16, cap), BF16)
    of_group = iota((stacked.shape[0], cap), 0) & (groups - 1)
    moved = jnp.zeros(stacked.shape, F32)
    for j in range(groups):
        goes = jnp.broadcast_to(slot[j : j + 1], (16, cap)).astype(jnp.int16)
        swap = jnp.concatenate(
            [
                jnp.where(goes == place + jnp.int16(t * 16), one, jnp.zeros_like(one))
                for t in range(cap // 16)
            ],
            axis=0,
        )
        result = lax.dot_general(
            stacked, swap, (((1,), (1,)), ((), ())), preferred_element_type=F32
        )
        moved = jnp.where(of_group == j, result, moved)
    sign = jnp.where(fits, 1.0, -1.0)
    blocks = sent.shape[0] // (groups * 4 * half)
    for kind in range(2):
        part = [
            moved[(6 * kind + n) * groups : (6 * kind + n + 1) * groups] for n in range(6)
        ]
        numbers = (part[0] + 256.0 * part[1] + 65536.0 * part[2]) * sign
        powers = part[3] + part[4] + part[5]
        for n, value in enumerate((numbers, powers)):
            for h in range(half):
                row = kind * 2 * half + n * half + h
                for block in range(blocks):
                    at = pl.ds(block * groups * 4 * half + row, groups, stride=4 * half)
                    sent[at, :] = value[:, h * LANES : (h + 1) * LANES]
    for copy in copies[3:5]:
        copy.wait()
    index = export_in[...]
    codes = [
        mark[j : j + 1, h * LANES : (h + 1) * LANES].astype(F32)
        for j in range(groups)
        for h in range(half)
    ]
    ghost = pick([rows_of(pos_in, ch) for ch in range(3)] + [codes], index)
    ghost[3] = (index // cap * (2 * cap) + ghost[3].astype(I32)).astype(F32)
    for out in (even, odd):
        for n, value in enumerate(ghost):
            out[2 * wide + n * exports : 2 * wide + (n + 1) * exports, :] = value
    for copy in copies[5:]:
        copy.wait()
    top = (1 - is_odd("cross")) * (rows - RIM)
    for n, own in enumerate((temp_in, kappa_in)):
        for r in range(RIM):
            for out, first in ((even_y, top), (odd_y, rows - RIM - top)):
                out[n * RIM + r] = own[pl.ds(first + r, height // rows, stride=rows), :]


def corner_kernel(rows, even_s, odd_s, even_x, odd_x, even, odd):
    side = RIM * rows
    low, high = low_and_high("cut", even_x, odd_x)
    top = (1 - is_odd("cross")) * (rows - RIM)
    base = even_s.shape[0]
    for out, strips, first in ((even, even_s, top), (odd, odd_s, rows - RIM - top)):
        out[:base, :] = strips[...]
        for n in range(2 * RIM):
            for p in range(RIM):
                at = pl.ds(n // RIM * side + p * rows + first + n % RIM, 1)
                to = base + n * PAD + p
                out[to : to + 1, :] = low[at, :]
                out[to + RIM : to + RIM + 1, :] = high[at, :]
            out[base + n * PAD + 2 * RIM : base + (n + 1) * PAD, :] = jnp.zeros((PAD - 2 * RIM, LANES), F32)


class Rows:
    def __init__(self, ref, base, size):
        self.ref, self.base, self.size = ref, base, size

    def __getitem__(self, index):
        r, at, lanes = index
        first = self.base + r * self.size
        return self.ref[first + (at.start or 0) : first + (self.size if at.stop is None else at.stop), :]


ENDS = 2 * RIM


def open_kernel(
    rows, after, temp, kappa_own, even_x, odd_x, even_y, odd_y,
    opened, kappa, ends, now, cond, along_z, minus, plus,
):
    lanes = temp.shape[1]
    pitch = rows + PAD
    planes = temp.shape[0] // rows
    blocks = planes + 2 * RIM + 1
    side = RIM * rows
    x_low, x_high = low_and_high("cut", even_x, odd_x)
    y_low, y_high = low_and_high("cross", even_y, odd_y)
    minus[...], plus[...] = difference_matrices(lanes)
    for n, (flat, own, scale) in enumerate(((now, temp, 1.0), (kappa, kappa_own, 0.5))):
        beside = [half.part(slice(n * side, (n + 1) * side)) for half in (x_low, x_high)]
        strips = [half.part(slice(n * RIM, (n + 1) * RIM)) for half in (y_low, y_high)]
        fill(flat, own, *beside, *strips, rows, scale)
    size = ENDS * pitch
    ends[:size, :] = now[:size, :]
    ends[size:, :] = now[(blocks - ENDS) * pitch : blocks * pitch, :]
    conduct_pass(now, kappa, cond, along_z, minus, plus, 0, blocks, pitch)
    opened[0:pitch, :] = jnp.zeros((pitch, lanes), F32)
    opened[(blocks - 1) * pitch :, :] = jnp.zeros((opened.shape[0] - (blocks - 1) * pitch, lanes), F32)

    def put(block, value):
        opened[pl.ds(pl.multiple_of(block * pitch, 8), pitch), :] = value

    flow_pass(now, cond, along_z, 1, blocks - 2, pitch, 1000, put)


def heat_kernel(
    got, opened, kappa_in, ends_in, source_own, even_s, odd_s,
    temp_out, looked, source, kappa, ends, ends_kappa, now, then, cond, along_z, minus, plus, pieces,
    result, sem,
):
    lanes = kappa.shape[1]
    planes, rows, _ = result.shape
    pitch = rows + PAD
    total = planes + 2 * RIM
    blocks = total + 1
    wide = RIM - 1
    s_low, s_high = low_and_high("cross", even_s, odd_s)
    height = -(-total // 8) * 8
    minus[...], plus[...] = difference_matrices(lanes)
    source[...] = source_own[...]
    for first, half in ((PAD - wide, s_low), (PAD + rows, s_high)):
        strips = Rows(half, 0, height)
        for r in range(wide):
            source[pl.ds(first + r, total, stride=pitch), :] = strips[r, :total, :]
    mask = rim_mask(pitch, lanes)

    corners = [
        [Rows(half, wide * height + n * RIM * PAD, PAD) for half in (s_low, s_high)] for n in range(2)
    ]
    size = ENDS * pitch
    last_end = blocks - ENDS
    ends[: 2 * size, :] = ends_in[...]
    ends[2 * size :, :] = jnp.zeros((pitch, lanes), F32)
    fill_corners(ends, 2 * ENDS - RIM - 1, *corners[0], rows, 1.0)
    kappa[...] = kappa_in[...]
    fill_corners(kappa, blocks - RIM - 1, *corners[1], rows, 0.5)
    ends_kappa[:size, :] = kappa[:size, :]
    ends_kappa[size : 2 * size, :] = kappa[last_end * pitch : blocks * pitch, :]
    conduct_pass(ends, ends_kappa, cond, along_z, minus, plus, 0, 2 * ENDS, pitch)
    then[0:pitch, :] = jnp.zeros((pitch, lanes), F32)
    then[(blocks - 1) * pitch :, :] = jnp.zeros((then.shape[0] - (blocks - 1) * pitch, lanes), F32)
    for n in range(1, blocks - 1):
        if not (1 <= n < ENDS - 1 or last_end + 1 <= n):
            at = pl.ds(n * pitch, pitch)
            then[at, :] = (opened[at, :] + source[at, :]) * mask
    for first, to in ((1, 1), (ENDS + 1, last_end + 1)):

        def again(block, value, first=first, to=to):
            at = pl.ds((block - first + to) * pitch, pitch)
            then[at, :] = (value + source[at, :]) * mask

        flow_pass(ends, cond, along_z, first, ENDS - 2, pitch, 1000, again)

    now[0:pitch, :] = jnp.zeros((pitch, lanes), F32)
    now[(blocks - 1) * pitch :, :] = jnp.zeros((now.shape[0] - (blocks - 1) * pitch, lanes), F32)
    conduct_pass(then, kappa, cond, along_z, minus, plus, 0, blocks, pitch)

    def middle(block, value):
        at = pl.ds(pl.multiple_of(block * pitch, 8), pitch)
        now[at, :] = (value + source[at, :]) * mask

    flow_pass(then, cond, along_z, 1, blocks - 2, pitch, 1000, middle)
    conduct_pass(now, kappa, cond, along_z, minus, plus, 0, blocks, pitch)

    def last(block, value):
        at = pl.ds(pl.multiple_of(block * pitch, 8), pitch)
        result[block - RIM] = (value + source[at, :])[PAD:]

    flow_pass(now, cond, along_z, RIM, planes, pitch, 1000, last)
    copy = pltpu.make_async_copy(result, temp_out, sem)
    copy.start()
    height = planes * rows
    for first in range(0, planes, lanes // rows):
        turned = result[first : first + lanes // rows].reshape(lanes, lanes).T
        high, low = split(turned)
        pieces[:lanes, first * rows : first * rows + lanes] = high
        pieces[lanes:, first * rows : first * rows + lanes] = low
    lookup(lax.axis_index("cut"), got, height, lanes, rows, looked, pieces)
    copy.wait()


def paired(got, block, kind, row, s):
    at = kind * (got.shape[2] // 2) + row
    first = got[block, s, pl.ds(at, 1), :]
    second = got[block, s + 1, pl.ds(at, 1), :]
    left = iota((1, LANES), 1) < LANES // 2
    return jnp.where(left, first, second), jnp.where(left, second, first)


def cell_of(number):
    return jnp.abs(number).astype(I32) - 1


def unsorted(got):
    half = got.shape[2] // 4
    lowest = jnp.minimum(got[:, :, :half, :], got[:, :, 2 * half : 3 * half, :])
    return jnp.min(lowest) < 0.0


def deposit_kernel(planes, got, source, even, odd, spread, across, plane_of):
    blocks, groups, rows_sent, _ = got.shape
    half = rows_sent // 4
    lanes = source.shape[1]
    rows = across.shape[0]
    pitch = rows + PAD
    here = lax.axis_index("cut")
    place = iota((rows, LANES), 0)
    place16 = place.astype(jnp.int16)
    zero = jnp.zeros((rows, LANES), BF16)
    pairs = groups // 2
    tile = planes // QUARTERS
    region = 2 * pairs * LANES
    inside = QUARTERS * region
    wide = RIM - 1

    def block(distance):
        return lax.rem(here + (blocks + distance), blocks)

    def fill_columns(at, number, power):
        span = pl.ds(pl.multiple_of(at, LANES), LANES)
        cell = cell_of(jnp.broadcast_to(number, (rows, LANES)))
        high, low = split(jnp.broadcast_to(power, (rows, LANES)))
        lane = (cell & (lanes - 1)).astype(jnp.int16)
        for t in range(lanes // rows):
            hit = lane == place16 + jnp.int16(t * rows)
            spread[t * rows : (t + 1) * rows, span] = jnp.where(hit, high, zero)
            spread[lanes + t * rows : lanes + (t + 1) * rows, span] = jnp.where(hit, low, zero)
        row = lax.shift_right_arithmetic(cell, 7)
        across[:, span] = jnp.where((row & (rows - 1)) == place, 1.0, 0.0).astype(BF16)
        plane_of[:, span] = lax.shift_right_arithmetic(row, rows.bit_length() - 1).astype(jnp.int16)

    def sides(pair, quarter_high, quarter_low):
        for n, (distance, kind) in enumerate(((1, 0), (0, 1), (-1, 0), (-2, 1))):
            share = quarter_high if n < 2 else quarter_low
            h, which = share // 2, share % 2
            number = paired(got, block(distance), kind, h, 2 * pair)[which]
            power = paired(got, block(distance), kind, half + h, 2 * pair)[which]
            fill_columns(inside + (n * pairs + pair) * LANES, number, power)

    def fill_pair(pair, unused):
        for part in range(2):
            for h in range(half):
                numbers = paired(got, block(-part), part, h, 2 * pair)
                powers = paired(got, block(-part), part, half + h, 2 * pair)
                for which in range(2):
                    at = (2 * h + which) * region + (part * pairs + pair) * LANES
                    fill_columns(at, numbers[which], powers[which])
        sides(pair, 0, QUARTERS - 1)
        return unused

    lax.fori_loop(0, pairs, fill_pair, 0, unroll=True)
    blocks_all = source.shape[0] // pitch
    for n in range(blocks_all):
        inner = 1 <= n < planes + 2 * RIM - 1
        end = PAD if inner else pitch
        source[n * pitch : n * pitch + end, :] = jnp.zeros((end, lanes), F32)

    def product(first, base, count, columns, added=False):
        where_y = across[:, columns]
        where_x = plane_of[:, columns] - jnp.asarray(base, I32).astype(jnp.int16)
        nothing = jnp.zeros_like(where_y)
        hot = jnp.concatenate(
            [jnp.where(where_x == jnp.int16(x), where_y, nothing) for x in range(count)], axis=0
        )
        both = lax.dot_general(
            hot, spread[:, columns], (((1,), (1,)), ((), ())), preferred_element_type=F32
        )
        value = both[:, :lanes] + both[:, lanes:]
        for n in range(count):
            at = pl.ds(pl.multiple_of((first + n + RIM) * pitch + PAD, 8), rows)
            part = value[n * rows : (n + 1) * rows]
            source[at, :] = source[at, :] + part if added else part

    for q in range(QUARTERS):
        product(q * tile, q * tile, tile, slice(q * region, (q + 1) * region))

    def outside(added):
        product(planes, 0, wide, slice(inside, inside + region), added)
        product(-wide, planes - wide, wide, slice(inside + region, inside + 2 * region), added)

    outside(False)

    @pl.when(unsorted(got))
    def _():
        def whole(m, unused):
            product(m * tile, m * tile, tile, slice(0, inside))
            return unused

        lax.fori_loop(0, QUARTERS, whole, 0)
        for step in range(1, QUARTERS):

            def others(pair, unused, step=step):
                sides(pair, step, QUARTERS - 1 - step)
                return unused

            lax.fori_loop(0, pairs, others, 0)
            outside(True)

    planes_all = planes + 2 * RIM
    top = (1 - is_odd("cross")) * (rows - wide)
    for r in range(wide):
        for out, first in ((even, top), (odd, rows - wide - top)):
            at = r * (out.shape[0] // wide)
            out[at : at + planes_all, :] = source[pl.ds(PAD + first + r, planes_all, stride=pitch), :]


def lookup(me, got, height, lanes, rows, looked, pieces):
    blocks, groups, rows_sent, _ = got.shape
    half = rows_sent // 4
    pairs = groups // 2
    shift = rows.bit_length() - 1
    place = iota((rows, LANES), 0)
    lane_place = iota((lanes, LANES), 0)
    zero = jnp.zeros((rows, LANES), BF16)

    def search(numbers, base, size):
        hots = []
        for number in numbers:
            row = lax.shift_right_arithmetic(cell_of(jnp.broadcast_to(number, (rows, LANES))), 7)
            plane = lax.shift_right_arithmetic(row, shift).astype(jnp.int16)
            hot_row = jnp.where((row & (rows - 1)) == place, 1.0, 0.0).astype(BF16)
            hots.append(
                jnp.concatenate(
                    [
                        jnp.where(plane == jnp.int16(x), hot_row, zero)
                        for x in range(base // rows, (base + size) // rows)
                    ],
                    axis=0,
                )
            )
        both = jnp.dot(
            pieces[:, base : base + size],
            jnp.concatenate(hots, axis=1),
            preferred_element_type=F32,
        )
        value = both[:lanes] + both[lanes:]
        results = []
        for n, number in enumerate(numbers):
            lane = cell_of(jnp.broadcast_to(number, (lanes, LANES))) & (lanes - 1)
            part = jnp.where(lane == lane_place, value[:, n * LANES : (n + 1) * LANES], 0.0)
            results.append(jnp.sum(part, axis=0, keepdims=True))
        return results

    left = iota((1, LANES), 1) < LANES // 2

    def run(full):
        for h in range(half):
            found = []
            for which in range(2):
                numbers = []
                for part in range(2):
                    block = lax.rem(me + (blocks - part), blocks)
                    for pair in range(pairs):
                        numbers.append(paired(got, block, part, h, 2 * pair)[which])
                size = height // QUARTERS
                found.append(
                    search(numbers, 0, height) if full else search(numbers, (2 * h + which) * size, size)
                )
            for part in range(2):
                for pair in range(pairs):
                    a, b = (f[part * pairs + pair] for f in found)
                    for s, value in ((0, jnp.where(left, a, b)), (1, jnp.where(left, b, a))):
                        row = (2 * pair + s) * 2 * half + part * half + h
                        for block in range(blocks):
                            at = block * groups * 2 * half + row
                            looked[at : at + 1, :] = value

    run(False)

    @pl.when(unsorted(got))
    def _():
        run(True)


def pick(tables, index):
    row = lax.shift_right_logical(index, 7)
    lane = index & (LANES - 1)
    results = [jnp.zeros(index.shape, F32) for _ in tables]
    for r in range(len(tables[0])):
        here = row == r
        for ch, rows in enumerate(tables):
            value = jnp.take_along_axis(jnp.broadcast_to(rows[r], index.shape), lane, axis=1)
            results[ch] = jnp.where(here, value, results[ch])
    return results


def rows_of(ref, ch):
    return [ref[ch : ch + 1, r * LANES : (r + 1) * LANES] for r in range(ref.shape[1] // LANES)]


def stretch_kernel(
    side, after, pos, acted, other, gap, snapped, even_x, odd_x, base, slope, delta, hot, ghost,
):
    exports = ghost.shape[1]
    low_ghost, high_ghost = low_and_high("cut", even_x, odd_x)

    def ghosts(n, ref):
        ghost[n] = ref[side + 3 * exports : side + 4 * exports, :].astype(I32)
        places = ref[side : side + 3 * exports, :]
        return [[places[ch * exports + r : ch * exports + r + 1] for r in range(exports)] for ch in range(3)]

    own = [rows_of(pos, ch) for ch in range(3)]
    low = ghosts(0, low_ghost)
    high = ghosts(1, high_ghost)
    first = pick(own, acted[...])
    second = pick([own[ch] + low[ch] + high[ch] for ch in range(3)], other[...])
    d = [second[ch] - first[ch] for ch in range(3)]
    dist = jnp.sqrt(d[0] * d[0] + d[1] * d[1] + d[2] * d[2])
    weight = (1.0 - snapped[...].astype(F32)) / jnp.maximum(dist, 0.3)
    base[...] = weight * (dist - gap[...])
    slope[...] = weight * (gap[...] * (0.2 * 0.5))
    for ch in range(3):
        delta[ch] = d[ch]
    place = iota((16, LANES), 0).astype(jnp.int16)
    one = jnp.ones((16, LANES), BF16)
    for r in range(acted.shape[0]):
        lane = jnp.broadcast_to(acted[r : r + 1, :] & (LANES - 1), (16, LANES)).astype(jnp.int16)
        for t in range(LANES // 16):
            hot[t * 16 : (t + 1) * 16, r * LANES : (r + 1) * LANES] = jnp.where(
                lane == place + jnp.int16(t * 16), one, jnp.zeros_like(one)
            )


def bond_kernel(
    blocks, back, code, pos, vel, acted, other, ghost, base, slope, delta, hot, pos_out, vel_out, force,
):
    half, groups, _ = code.shape
    here = lax.axis_index("cut")
    double = 2 * half

    def slots(distance):
        found = []
        for kind in range(2):
            block = lax.rem(here + (blocks + distance + kind), blocks)
            for h in range(half):
                first = block * groups * double + kind * half + h
                found.append(back[pl.ds(first, groups, stride=double), :])
        return found

    def ghosts(n, distance):
        rows = slots(distance)
        table = [rows[k][j : j + 1] for j in range(groups) for k in range(double)]
        found = pick([table], ghost[n])[0]
        return [found[r : r + 1] for r in range(found.shape[0])]

    rows = slots(0)
    temps = []
    for h in range(half):
        index = code[h]
        temp = jnp.zeros(index.shape, F32)
        for k in range(double):
            value = jnp.take_along_axis(rows[k], index & (LANES - 1), axis=1)
            temp = jnp.where(lax.shift_right_logical(index, 7) == k, value, temp)
        temps.append(temp)
    own = [temps[h][j : j + 1] for j in range(groups) for h in range(half)]
    first = pick([own], acted[...])[0]
    second = pick([own + ghosts(0, -1) + ghosts(1, 1)], other[...])[0]
    scale = base[...] - slope[...] * (first + second)
    values = [split(scale * delta[ch]) for ch in range(3)]
    values = [piece.astype(F32) for pair in values for piece in pair]
    high_count = len(own)
    high_place = iota((high_count, LANES), 0)
    for r in range(acted.shape[0]):
        span = slice(r * LANES, (r + 1) * LANES)
        at_row = lax.shift_right_logical(acted[r : r + 1, :], 7) == high_place
        for n, value in enumerate(values):
            force[n * high_count : (n + 1) * high_count, span] = jnp.where(
                at_row, jnp.broadcast_to(value[r : r + 1], (high_count, LANES)), 0.0
            ).astype(BF16)
    total = lax.dot_general(
        force[...], hot[...], (((1,), (1,)), ((), ())), preferred_element_type=F32
    )
    for ch in range(3):
        base_row = 2 * ch * high_count
        summed = (
            total[base_row : base_row + high_count]
            + total[base_row + high_count : base_row + 2 * high_count]
        )
        for r in range(high_count):
            span = slice(r * LANES, (r + 1) * LANES)
            velocity = vel[ch : ch + 1, span] + 0.5 * summed[r : r + 1]
            vel_out[ch : ch + 1, span] = velocity
            pos_out[ch : ch + 1, span] = pos[ch : ch + 1, span] + 0.5 * velocity


def swaps(axis, closed, even, odd):
    count = lax.axis_size(axis)
    results = []
    for first, block in ((0, even), (1, odd)):
        pairs = []
        for i in range(first, count if closed else count - 1, 2):
            pairs += [(i, (i + 1) % count), ((i + 1) % count, i)]
        results.append(lax.ppermute(block, axis, pairs))
    return results


def per_device(
    warming_above_ambient,
    fourier_stability_factor,
    patch_locator,
    photon_gain_wattage,
    on_skin_marker,
    grain_placements,
    grain_motion_parts,
    tether_acted_grain,
    tether_other_grain,
    tether_relaxed_gap,
    snapped_marker,
    exported_copies,
):
    planes, rows, lanes = warming_above_ambient.shape
    temp = warming_above_ambient.reshape(planes * rows, lanes)
    kappa = fourier_stability_factor.reshape(planes * rows, lanes)
    blocks = lax.axis_size("cut")
    groups = lax.axis_size("cross")
    count = patch_locator.shape[0]
    half = count // groups // LANES
    pitch = rows + PAD
    total = planes + 2 * RIM
    flat = jax.ShapeDtypeStruct(((total + 2) * pitch, lanes), F32)
    wide = RIM * rows

    exports = exported_copies.shape[0] // LANES
    carried = jax.ShapeDtypeStruct((2 * wide + 4 * exports, LANES), F32)
    devices = blocks * groups
    strips = jax.ShapeDtypeStruct((2 * RIM, planes, lanes), F32)
    whole = pltpu.VMEM(temp.shape, F32)
    sent, even_x, odd_x, even_y, odd_y, code = call(
        functools.partial(parcel_kernel, rows),
        [
            jax.ShapeDtypeStruct((devices * 4 * half, LANES), F32),
            carried,
            carried,
            strips,
            strips,
            jax.ShapeDtypeStruct((half, groups, LANES), I32),
        ],
        [
            temp,
            kappa,
            patch_locator.reshape(-1, LANES),
            photon_gain_wattage.reshape(-1, LANES),
            on_skin_marker.reshape(-1, LANES),
            grain_placements,
            exported_copies.reshape(-1, LANES),
        ],
        [
            pltpu.VMEM((count // LANES, LANES), I32),
            pltpu.VMEM((count // LANES, LANES), F32),
            pltpu.VMEM((count // LANES, LANES), I32),
            pltpu.VMEM(grain_placements.shape, F32),
            pltpu.VMEM((exports, LANES), I32),
            whole,
            whole,
            pltpu.SemaphoreType.DMA((11,)),
        ],
        left=7,
        limit=None,
    )

    def exchange(sent):
        sent = sent.reshape(devices, -1, LANES)
        return lax.all_to_all(sent, BOTH, split_axis=0, concat_axis=0, tiled=True)

    even_y, odd_y = swaps("cross", False, even_y, odd_y)
    got = exchange(sent).reshape(blocks, groups, 4 * half, LANES)
    even_x, odd_x = swaps("cut", True, even_x, odd_x)


    strips = jax.ShapeDtypeStruct(((RIM - 1) * (-(-total // 8) * 8), lanes), F32)
    entries = 2 * count + 4 * count // QUARTERS
    source, even_s, odd_s = call(
        functools.partial(deposit_kernel, planes),
        [flat, strips, strips],
        [got],
        [
            pltpu.VMEM((2 * lanes, entries), BF16),
            pltpu.VMEM((rows, entries), BF16),
            pltpu.VMEM((rows, entries), jnp.int16),
        ],
    )
    corners = jax.ShapeDtypeStruct((strips.shape[0] + 2 * RIM * PAD, lanes), F32)
    even_s, odd_s = call(
        functools.partial(corner_kernel, rows), [corners, corners], [even_s, odd_s, even_x, odd_x]
    )
    sent_strips = even_s
    even_s, odd_s = swaps("cross", False, even_s, odd_s)

    grid = pltpu.VMEM(flat.shape, F32)
    matrix = pltpu.VMEM((2 * lanes, 2 * lanes), BF16)
    ends = jax.ShapeDtypeStruct((2 * ENDS * pitch, lanes), F32)
    opened, kappa, ends = call(
        functools.partial(open_kernel, rows),
        [flat, flat, ends],
        [sent_strips, temp, kappa, even_x, odd_x, even_y, odd_y],
        [grid, grid, grid, matrix, matrix],
        left=1,
    )
    ends_grid = pltpu.VMEM((2 * ENDS * pitch + pitch, lanes), F32)
    temp, looked = call(
        heat_kernel,
        [
            jax.ShapeDtypeStruct((planes, rows, lanes), F32),
            jax.ShapeDtypeStruct((devices * 2 * half, LANES), F32),
        ],
        [got, opened, kappa, ends, source, even_s, odd_s],
        [
            grid, grid, ends_grid, ends_grid, grid, grid, grid, grid, matrix, matrix,
            pltpu.VMEM((2 * lanes, planes * rows), BF16),
            pltpu.VMEM((planes, rows, lanes), F32),
            pltpu.SemaphoreType.DMA,
        ],
        outs_left=1,
    )
    back = exchange(looked).reshape(looked.shape)
    acted = tether_acted_grain.reshape(-1, LANES)
    other = tether_other_grain.reshape(-1, LANES)
    entry = jax.ShapeDtypeStruct(acted.shape, F32)
    base, slope, delta, hot, ghost = call(
        functools.partial(stretch_kernel, 2 * wide),
        [
            entry,
            entry,
            jax.ShapeDtypeStruct((3,) + acted.shape, F32),
            jax.ShapeDtypeStruct((LANES, acted.size), BF16),
            jax.ShapeDtypeStruct((2, exports, LANES), I32),
        ],
        [
            looked,
            grain_placements,
            acted,
            other,
            tether_relaxed_gap.reshape(-1, LANES),
            snapped_marker.reshape(-1, LANES),
            even_x,
            odd_x,
        ],
        left=1,
    )
    out = jax.ShapeDtypeStruct(grain_placements.shape, F32)
    positions_new, velocities_new = call(
        functools.partial(bond_kernel, blocks),
        [out, out],
        [
            back, code, grain_placements, grain_motion_parts, acted, other, ghost,
            base, slope, delta, hot,
        ],
        [pltpu.VMEM((6 * (count // LANES), acted.size), BF16)],
    )
    return (temp, positions_new, velocities_new)


def solution(mesh):
    return jax.shard_map(
        per_device,
        mesh=mesh,
        in_specs=(
            P("cut", "cross", None),
            P("cut", "cross", None),
            P(("cut", "cross")),
            P(("cut", "cross")),
            P(("cut", "cross")),
            P(None, ("cut", "cross")),
            P(None, ("cut", "cross")),
            P(("cut", "cross")),
            P(("cut", "cross")),
            P(("cut", "cross")),
            P(("cut", "cross")),
            P(("cut", "cross")),
        ),
        out_specs=(P("cut", "cross", None), P(None, ("cut", "cross")), P(None, ("cut", "cross"))),
        check_vma=False,
    )
```
